32 devices in a mesh: parts: 2 (over x), tile: 16 (over z, y, core).
Axes of the slice: x: 2, y: 2, z: 4, core: 2. Of those that a mesh axis runs over, the one named last changes fastest.
Arguments:
- probe_wave: float32 [2, 128, 128], replicated, may hold values from -6 to 6
- object_slices: float32 [8, 2, 2048, 1024], P('parts', None, 'tile'), parts along dimension 0, may hold values from -4 to 4
- intensities: float32 [256, 128, 128], P(('parts', 'tile')), parts along dimension 0, may hold values from 0 to 2
- row_offset: int32 [256], P(('parts', 'tile')), parts along dimension 0, may hold values from 0 to 127
- col_offset: int32 [256], P(('parts', 'tile')), parts along dimension 0, may hold values from 0 to 896
- counts: int32 [32], P(('parts', 'tile')), parts along dimension 0, may hold values from 1 to 8, 64 in all
Outputs:
- object_grad: float32 [8, 2, 2048, 1024], P('parts', None, 'tile'), parts along dimension 0
- misfit_total: float32 [2], P('parts'), parts along dimension 0
The draws below stay inside these ranges and needn't reach their ends.
There are 2 independent parts, one for each index of `parts`. The reference program is written for one: setup_inputs(seed, part) draws one part's arguments, and reference() takes and returns one part's arrays. A program takes and returns all parts, laid end to end along the dimension named above; an argument that names none is the same for every part. Nothing has to cross between parts.
Inputs may be any that keep to these rules, and one draw needn't show every extreme that they name: `counts`: every strip holds at least one position; some strip holds exactly 8.
All inputs are finite; a program needn't handle non-finite values. No bound on the sum of `counts` on one device may be relied on, other than what follows from the above.
Results may differ from the reference program's by a relative error of at most 0.0003.
Values sent between devices are 32-bit elements; how exact they have to be, the bound alone decides.
No kernel may reach another device: no remote copies, remote signals or barrier semaphores. Data moves between devices by JAX's collectives and lax.ppermute only.
A program may use at most 128 MiB of HBM per device.

```python
import math
import jax
import jax.numpy as jnp
import numpy as np
from jax import lax

W = 128
SLICES = 4
TILE_ROWS = 128
NX = 1024
MEAN = 4
CAP = 8
SLOTS = 128
NY = 2048
N_TILE = 16


def plant(entries, rng, smallest, high):
    place = [jax.random.randint(jax.random.fold_in(rng, axis), (), 0, length) for axis, length in enumerate(entries.shape)]
    main_axis = entries.shape.index(max(entries.shape))
    beside = place[:main_axis] + [(place[main_axis] + 1) % entries.shape[main_axis]] + place[main_axis + 1:]
    return entries.at[tuple(place)].set(smallest).at[tuple(beside)].set(high)


def shard_levels(own_key, extent, split, least, largest):
    gain = 1.0
    for axis_at, parts in split:
        heights = jax.random.uniform(jax.random.fold_in(jax.random.fold_in(own_key, 6), axis_at), (parts,), jnp.float32, least / len(split), largest / len(split))
        gain = gain * jnp.repeat(jnp.exp(heights), extent[axis_at] // parts).reshape((-1,) + (1,) * (len(extent) - 1 - axis_at))
    return gain


def length_profile(count, total, most, lean):
    weights = [(1 << 20) // math.isqrt(grade ** lean) + 1 for grade in range(2, count + 1)]
    surplus, given = total - most - (count - 1), [1] * (count - 1)
    while surplus > 0:
        movable = [i for i in range(count - 1) if given[i] < most]
        whole, remaining = sum([weights[i] for i in movable]), surplus
        for i in movable:
            addition = min(most - given[i], max(1, remaining * weights[i] // whole), surplus)
            given[i] = given[i] + addition
            surplus = surplus - addition
    return np.array([most] + given)


def uneven_parts(stream_key, amount, total, most, lean):
    if amount == 2:
        one = jax.random.randint(stream_key, (), max(1, total - most), min(most, total - 1) + 1)
        return jnp.stack([one, total - one])
    tallies = jnp.asarray(length_profile(amount, total, most, lean), jnp.int32)
    couples = (amount - 1) // 2
    source_of, sink = tallies[1:1 + 2 * couples:2], tallies[2:2 + 2 * couples:2]
    slack = jnp.minimum(source_of - 1, most - sink)
    shifted = jax.random.randint(jax.random.fold_in(stream_key, 1), (couples,), 0, 1 << 20) % (slack + 1)
    tallies = tallies.at[1:1 + 2 * couples:2].set(source_of - shifted).at[2:2 + 2 * couples:2].set(sink + shifted)
    return tallies[jax.random.permutation(jax.random.fold_in(stream_key, 2), amount)]


def centred(stream_key, shape, scale, limit, shards=(), held_as=jnp.bfloat16):
    entries = scale * jax.random.normal(stream_key, shape, jnp.float32)
    if shards:
        entries = entries * shard_levels(stream_key, shape, shards, -0.22, 0.18)
    return jnp.clip(entries, -limit, limit).astype(held_as)


def setup_inputs(seed: int = 0, part: int = 0) -> dict:
    arg_keys = jax.random.split(jax.random.key(seed), 7)
    own_keys = jax.random.split(jax.random.fold_in(arg_keys[6], part), 7)
    probe_wave = centred(arg_keys[0], (2, W, W), 1.0, 6.0, (), jnp.float32)
    object_slices = centred(own_keys[1], (SLICES, 2, NY, NX), 0.7071, 4.0, ((2, 16),), jnp.float32)
    intensities = jnp.clip(2.0 * jax.random.uniform(own_keys[2], (SLOTS, W, W), jnp.float32) ** shard_levels(own_keys[2], (SLOTS, W, W), ((0, 16),), -0.2, 0.2), 0.0, 2.0)
    row_offset = plant(jax.random.randint(own_keys[3], (SLOTS,), 0, TILE_ROWS), jax.random.fold_in(own_keys[3], 1), 0, TILE_ROWS - 1).astype(jnp.int32)
    col_offset = plant(jax.random.randint(own_keys[4], (SLOTS,), 0, NX - W + 1), jax.random.fold_in(own_keys[4], 1), 0, NX - W).astype(jnp.int32)
    counts = uneven_parts(own_keys[5], N_TILE, MEAN * N_TILE, CAP, 2).astype(jnp.int32)
    return {"probe_wave": probe_wave, "object_slices": object_slices, "intensities": intensities, "row_offset": row_offset, "col_offset": col_offset, "counts": counts}


def kernel_field(width):
    indices = jnp.arange(width)
    freqs = jnp.where(indices < width // 2, indices, indices - width).astype(jnp.float32)
    phase = -0.0015 * (freqs[:, None] ** 2 + freqs[None, :] ** 2)
    return jnp.cos(phase) + 1j * jnp.sin(phase)

def slot_misfit(window, probe_wave, measured, propagator):
    wave = probe_wave[0] + 1j * probe_wave[1]
    for layer in range(SLICES):
        exit_wave = wave * (window[layer, 0] + 1j * window[layer, 1])
        if layer + 1 < SLICES:
            wave = jnp.fft.ifft2(jnp.fft.fft2(exit_wave) * propagator)
    far = jnp.fft.fft2(exit_wave) / W
    misfit = jnp.real(far) ** 2 + jnp.imag(far) ** 2 - measured
    return 0.25 * jnp.sum(misfit * misfit)

def reference(probe_wave, object_slices, intensities, row_offset, col_offset, counts):
    propagator = kernel_field(W)
    slot_ids = jnp.arange(SLOTS)
    strips = slot_ids // CAP
    live = (slot_ids % CAP < counts[strips]).astype(object_slices.dtype)
    ramp = jnp.arange(W)

    def step(carry, inputs):
        total, loss = carry
        row_at, col_at, measured, strip_at, weight = inputs
        rows = (strip_at * TILE_ROWS + row_at + ramp) % NY
        cols = col_at + ramp
        window = object_slices[:, :, rows][:, :, :, cols]
        value, pullback = jax.vjp(lambda piece: slot_misfit(piece, probe_wave, measured, propagator), window)
        grad_window, = pullback(weight.astype(value.dtype))
        total = total.at[:, :, rows[:, None], cols[None, :]].add(grad_window)
        return ((total, loss + weight * value), None)
    start = (jnp.zeros_like(object_slices), jnp.zeros((), object_slices.dtype))
    (total, loss), _ = lax.scan(step, start, (row_offset, col_offset, intensities, strips, live))
    return (total, loss.reshape(1))
```

```python
import functools

import jax
import jax.numpy as jnp
import ml_dtypes
import numpy as np
from jax import lax
from jax.experimental import pallas as pl
from jax.experimental.pallas import tpu as pltpu
from jax.sharding import PartitionSpec as P

BATCH = 2


def make_tables(width):
    indices = np.arange(width)
    dft = np.exp(-2j * np.pi * (np.outer(indices, indices) % width) / width) / np.sqrt(width)
    freqs = np.where(indices < width // 2, indices, indices - width).astype(np.float64)
    along = np.conj(dft) @ (np.exp(-0.0015j * freqs**2)[:, None] * dft)
    out = []
    for matrix in (along, dft):
        left = np.block([[matrix.real, -matrix.imag], [matrix.imag, matrix.real]])
        forms = []
        for form in (left, left.T):
            form = form.astype(np.float32)
            high = form.astype(ml_dtypes.bfloat16)
            low = (form - high.astype(np.float32)).astype(ml_dtypes.bfloat16)
            forms.append(np.stack([high, low]))
        out.append(np.stack(forms))
    return np.stack(out)


def split(x):
    high = x.astype(jnp.bfloat16)
    return high, (x - high.astype(jnp.float32)).astype(jnp.bfloat16)


def dot(a, b):
    return jnp.dot(a, b, preferred_element_type=jnp.float32)


def two_sided(tables, which, conj, re, im):
    batch, width = len(re), re[0].shape[0]
    left_form, right_form = (1, 0) if conj else (0, 1)
    rows = jnp.concatenate([jnp.concatenate([a, b], axis=1) for a, b in zip(re, im)], axis=0)
    high, low = split(rows)
    m_high, m_low = tables[which, right_form, 0], tables[which, right_form, 1]
    out = dot(high, m_high) + (dot(high, m_low) + dot(low, m_high))
    re = [out[b * width : (b + 1) * width, :width] for b in range(batch)]
    im = [out[b * width : (b + 1) * width, width:] for b in range(batch)]
    cols = jnp.concatenate([jnp.concatenate(re, axis=1), jnp.concatenate(im, axis=1)], axis=0)
    high, low = split(cols)
    m_high, m_low = tables[which, left_form, 0], tables[which, left_form, 1]
    out = dot(m_high, high) + (dot(m_low, high) + dot(m_high, low))
    re = [out[:width, b * width : (b + 1) * width] for b in range(batch)]
    im = [out[width:, b * width : (b + 1) * width] for b in range(batch)]
    return re, im


def field_grads(tables, wave_ref, window_ref, measured, scales, batch, slices):
    for layer in range(slices):
        re, im = [], []
        for b in range(batch):
            w_re, w_im = wave_ref[b, layer, 0], wave_ref[b, layer, 1]
            t_re, t_im = window_ref[b, layer, 0], window_ref[b, layer, 1]
            re.append(w_re * t_re - w_im * t_im)
            im.append(w_re * t_im + w_im * t_re)
        if layer + 1 < slices:
            re, im = two_sided(tables, 0, False, re, im)
            for b in range(batch):
                wave_ref[b, layer + 1, 0] = re[b]
                wave_ref[b, layer + 1, 1] = im[b]
    re, im = two_sided(tables, 1, False, re, im)
    loss = 0.0
    back_re, back_im = [], []
    for b in range(batch):
        misfit = re[b] * re[b] + im[b] * im[b] - measured[b]
        loss = loss + scales[b] * (0.25 * jnp.sum(misfit * misfit))
        back_re.append(misfit * re[b])
        back_im.append(misfit * im[b])
    re, im = two_sided(tables, 1, True, back_re, back_im)
    for layer in reversed(range(slices)):
        upper_re, upper_im = [], []
        for b in range(batch):
            w_re, w_im = wave_ref[b, layer, 0], wave_ref[b, layer, 1]
            t_re, t_im = window_ref[b, layer, 0], window_ref[b, layer, 1]
            window_ref[b, layer, 0] = re[b] * w_re + im[b] * w_im
            window_ref[b, layer, 1] = im[b] * w_re - re[b] * w_im
            upper_re.append(re[b] * t_re + im[b] * t_im)
            upper_im.append(im[b] * t_re - re[b] * t_im)
        if layer > 0:
            re, im = two_sided(tables, 0, True, upper_re, upper_im)
    return loss


def kernel(count_ref, row_ref, col_ref, probe_ref, own_ref, next_ref, seen_ref, tables_ref,
           grad_ref, grad_next_ref, loss_ref, wave_ref, window_ref):
    slices, _, width, columns = own_ref.shape
    cap = row_ref.shape[0]
    count = count_ref[0]
    grad_ref[...] = jnp.zeros_like(grad_ref)
    grad_next_ref[...] = jnp.zeros_like(grad_next_ref)
    last_tile = columns // width - 1

    def step(group, loss):
        places, scales = [], []
        row_iota = lax.broadcasted_iota(jnp.int32, (width, width), 0)
        lane_iota = lax.broadcasted_iota(jnp.int32, (width, width), 1)
        for b in range(BATCH):
            slot = jnp.minimum(group * BATCH + b, cap - 1)
            scales.append((group * BATCH + b < count).astype(jnp.float32))
            row, col = row_ref[slot], col_ref[slot]
            tile = col // width
            shift = col - tile * width
            here = pl.ds(pl.multiple_of(tile * width, width), width)
            there = pl.ds(pl.multiple_of(jnp.minimum(tile + 1, last_tile) * width, width), width)
            lower, first = row_iota >= row, lane_iota >= shift
            places.append((slot, here, there, lower, first))
            for l in range(slices):
                for p in range(2):
                    window_ref[b, l, p] = jnp.where(
                        lower,
                        jnp.where(first, own_ref[l, p, :, here], own_ref[l, p, :, there]),
                        jnp.where(first, next_ref[l, p, :, here], next_ref[l, p, :, there]),
                    )
            for p in range(2):
                wave_ref[b, 0, p] = pltpu.roll(pltpu.roll(probe_ref[p], row, 0), shift, 1)
        measured = [seen_ref[place[0]] for place in places]
        loss = loss + field_grads(tables_ref, wave_ref, window_ref, measured, scales, BATCH, slices)
        for b in range(BATCH):
            slot, here, there, lower, first = places[b]
            live = scales[b] > 0

            @pl.when(live)
            def _():
                for l in range(slices):
                    for p in range(2):
                        g = window_ref[b, l, p]
                        own, nxt = jnp.where(lower, g, 0.0), jnp.where(lower, 0.0, g)
                        grad_ref[l, p, :, here] += jnp.where(first, own, 0.0)
                        grad_ref[l, p, :, there] += jnp.where(first, 0.0, own)
                        grad_next_ref[l, p, :, here] += jnp.where(first, nxt, 0.0)
                        grad_next_ref[l, p, :, there] += jnp.where(first, 0.0, nxt)

        return loss

    loss_ref[0] = lax.fori_loop(0, (count + BATCH - 1) // BATCH, step, jnp.float32(0.0))


def shifted(x, axis, by):
    peers = lax.axis_size(axis)
    return lax.ppermute(x, axis, [(i, (i + by) % peers) for i in range(peers)])


def local(probe_wave, object_slices, intensities, row_offset, col_offset, counts):
    width = probe_wave.shape[-1]
    slices = object_slices.shape[0]
    tables = jnp.asarray(make_tables(width))
    following = shifted(object_slices, "tile", -1)
    smem = pl.BlockSpec(memory_space=pltpu.SMEM)
    vmem = pl.BlockSpec(memory_space=pltpu.VMEM)
    strip = jax.ShapeDtypeStruct(object_slices.shape, jnp.float32)
    grad, carried, loss = pl.pallas_call(
        kernel,
        out_shape=(strip, strip, jax.ShapeDtypeStruct((1,), jnp.float32)),
        in_specs=[smem] * 3 + [vmem] * 5,
        out_specs=(vmem, vmem, smem),
        scratch_shapes=[
            pltpu.VMEM((BATCH, slices, 2, width, width), jnp.float32),
            pltpu.VMEM((BATCH, slices, 2, width, width), jnp.float32),
        ],
        compiler_params=pltpu.CompilerParams(vmem_limit_bytes=48 << 20),
    )(counts, row_offset, col_offset, probe_wave, object_slices, following, intensities, tables)
    carried = shifted(carried, "tile", 1)
    misfit_total = lax.psum(loss, "tile").reshape(1)
    return (grad + carried, misfit_total)


def solution(mesh):
    placed = (
        P(),
        P("parts", None, "tile", None),
        P(("parts", "tile"), None, None),
        P(("parts", "tile")),
        P(("parts", "tile")),
        P(("parts", "tile")),
    )
    return jax.shard_map(
        local,
        mesh=mesh,
        in_specs=placed,
        out_specs=(P("parts", None, "tile", None), P("parts")),
        check_vma=False,
    )
```

```python
import functools

import jax
import jax.numpy as jnp
import ml_dtypes
import numpy as np
from jax import lax
from jax.experimental import pallas as pl
from jax.experimental.pallas import tpu as pltpu
from jax.sharding import PartitionSpec as P

BATCH = 2
UNIT = 8
ROW, COL, AT_PUSH, AT_BACK, AT_PULL, PUSHED, KEPT, TOTALS = range(8)


def make_tables(width):
    indices = np.arange(width)
    dft = np.exp(-2j * np.pi * (np.outer(indices, indices) % width) / width) / np.sqrt(width)
    freqs = np.where(indices < width // 2, indices, indices - width).astype(np.float64)
    along = np.conj(dft) @ (np.exp(-0.0015j * freqs**2)[:, None] * dft)
    out = []
    for matrix in (along, dft):
        left = np.block([[matrix.real, -matrix.imag], [matrix.imag, matrix.real]])
        forms = []
        for form in (left, left.T):
            form = form.astype(np.float32)
            high = form.astype(ml_dtypes.bfloat16)
            low = (form - high.astype(np.float32)).astype(ml_dtypes.bfloat16)
            forms.append(np.stack([high, low]))
        out.append(np.stack(forms))
    return np.stack(out)


def split(x):
    high = x.astype(jnp.bfloat16)
    return high, (x - high.astype(jnp.float32)).astype(jnp.bfloat16)


def dot(a, b):
    return jnp.dot(a, b, preferred_element_type=jnp.float32)


def two_sided(tables, which, conj, re, im):
    batch, width = len(re), re[0].shape[0]
    left_form, right_form = (1, 0) if conj else (0, 1)
    rows = jnp.concatenate([jnp.concatenate([a, b], axis=1) for a, b in zip(re, im)], axis=0)
    high, low = split(rows)
    m_high, m_low = tables[which, right_form, 0], tables[which, right_form, 1]
    out = dot(high, m_high) + (dot(high, m_low) + dot(low, m_high))
    re = [out[b * width : (b + 1) * width, :width] for b in range(batch)]
    im = [out[b * width : (b + 1) * width, width:] for b in range(batch)]
    cols = jnp.concatenate([jnp.concatenate(re, axis=1), jnp.concatenate(im, axis=1)], axis=0)
    high, low = split(cols)
    m_high, m_low = tables[which, left_form, 0], tables[which, left_form, 1]
    out = dot(m_high, high) + (dot(m_low, high) + dot(m_high, low))
    re = [out[:width, b * width : (b + 1) * width] for b in range(batch)]
    im = [out[width:, b * width : (b + 1) * width] for b in range(batch)]
    return re, im


def field_grads(tables, wave_ref, window_ref, measured, scales):
    batch, slices = wave_ref.shape[:2]
    for layer in range(slices):
        re, im = [], []
        for b in range(batch):
            w_re, w_im = wave_ref[b, layer, 0], wave_ref[b, layer, 1]
            t_re, t_im = window_ref[b, layer, 0], window_ref[b, layer, 1]
            re.append(w_re * t_re - w_im * t_im)
            im.append(w_re * t_im + w_im * t_re)
        if layer + 1 < slices:
            re, im = two_sided(tables, 0, False, re, im)
            for b in range(batch):
                wave_ref[b, layer + 1, 0] = re[b]
                wave_ref[b, layer + 1, 1] = im[b]
    re, im = two_sided(tables, 1, False, re, im)
    loss = 0.0
    back_re, back_im = [], []
    for b in range(batch):
        misfit = re[b] * re[b] + im[b] * im[b] - measured[b]
        loss = loss + scales[b] * (0.25 * jnp.sum(misfit * misfit))
        back_re.append(misfit * re[b])
        back_im.append(misfit * im[b])
    re, im = two_sided(tables, 1, True, back_re, back_im)
    for layer in reversed(range(slices)):
        upper_re, upper_im = [], []
        for b in range(batch):
            w_re, w_im = wave_ref[b, layer, 0], wave_ref[b, layer, 1]
            t_re, t_im = window_ref[b, layer, 0], window_ref[b, layer, 1]
            window_ref[b, layer, 0] = re[b] * w_re + im[b] * w_im
            window_ref[b, layer, 1] = im[b] * w_re - re[b] * w_im
            upper_re.append(re[b] * t_re + im[b] * t_im)
            upper_im.append(im[b] * t_re - re[b] * t_im)
        if layer > 0:
            re, im = two_sided(tables, 0, True, upper_re, upper_im)
    return loss


def place(plan_ref, slot, width, columns):
    row, col = plan_ref[ROW, slot], plan_ref[COL, slot]
    tile = col // width
    here = pl.ds(pl.multiple_of(tile * width, width), width)
    after = jnp.minimum(tile + 1, columns // width - 1)
    there = pl.ds(pl.multiple_of(after * width, width), width)
    return row, col - tile * width, here, there


def sizes(cap, width):
    whole = cap * width // UNIT
    return whole * 5 // 16, whole // 4, whole * 5 // 16


def make_plan(count_ref, row_ref, col_ref, plan_ref, width, room):
    cap = row_ref.shape[0]
    units = width // UNIT
    seen_units = width // (UNIT * UNIT)
    shape = (UNIT, 128)
    choice = lax.broadcasted_iota(jnp.int32, shape, 0) * 128 + lax.broadcasted_iota(jnp.int32, shape, 1)
    zero = jnp.zeros(shape, jnp.int32)
    push, back, pull, kept, bad = zero, zero, zero, zero, (choice >= (1 << cap)).astype(jnp.int32)
    count = count_ref[0]
    for s in range(cap):
        row = row_ref[s]
        crosses = jnp.logical_and(s < count, row > 0).astype(jnp.int32)
        taken = (choice >> s) & 1
        ahead = units - row // UNIT
        push += taken * (ahead + seen_units)
        back += taken * ahead
        pull += (1 - taken) * (crosses * ((row + UNIT - 1) // UNIT))
        kept += 1 - taken
        bad += taken * (1 - crosses)
    bad += (push > room[0]).astype(jnp.int32) + (back > room[1]).astype(jnp.int32) + (pull > room[2]).astype(jnp.int32)
    score = (kept + 16 * (bad > 0).astype(jnp.int32)) * (1 << cap) + choice
    best = jnp.min(score.astype(jnp.float32)).astype(jnp.int32)
    at_push = at_back = at_pull = n_pushed = n_kept = jnp.int32(0)
    for s in range(cap):
        plan_ref[PUSHED, s] = 0
        plan_ref[KEPT, s] = 0
        plan_ref[TOTALS, s] = 0
    for s in range(cap):
        row = row_ref[s]
        taken = (best >> s) & 1
        kept = jnp.where(s < count, 1 - taken, 0)
        plan_ref[ROW, s] = row
        plan_ref[COL, s] = col_ref[s]
        plan_ref[AT_PUSH, s] = at_push
        plan_ref[AT_BACK, s] = at_back
        plan_ref[AT_PULL, s] = at_pull

        @pl.when(taken > 0)
        def _():
            plan_ref[PUSHED, n_pushed] = s

        @pl.when(kept > 0)
        def _():
            plan_ref[KEPT, n_kept] = s

        ahead = units - row // UNIT
        at_push += taken * (ahead + seen_units)
        at_back += taken * ahead
        at_pull += kept * ((row + UNIT - 1) // UNIT)
        n_pushed += taken
        n_kept += kept
    plan_ref[TOTALS, 0] = n_pushed
    plan_ref[TOTALS, 1] = n_kept


def pack(plan_ref, slot, own_ref, buffer_ref, start, first_unit, last_unit):
    slices, planes, width, columns = own_ref.shape
    _, shift, here, there = place(plan_ref, slot, width, columns)
    first = lax.broadcasted_iota(jnp.int32, (UNIT, width), 1) >= shift

    def step(u, carry):
        rows = pl.ds(pl.multiple_of(u * UNIT, UNIT), UNIT)
        for l in range(slices):
            for p in range(planes):
                buffer_ref[start + u - first_unit, l * planes + p] = jnp.where(
                    first, own_ref[l, p, rows, here], own_ref[l, p, rows, there]
                )
        return carry

    lax.fori_loop(first_unit, last_unit, step, 0)


def push_kernel(count_ref, row_ref, col_ref, own_hbm, seen_hbm, plan_ref, out_hbm, own_ref, buffer_ref, sem, seen_sem, *, room):
    width = own_ref.shape[2]
    units, seen_units = width // UNIT, seen_hbm.shape[1]
    load = pltpu.make_async_copy(own_hbm, own_ref, sem)
    load.start()
    make_plan(count_ref, row_ref, col_ref, plan_ref, width, room)
    load.wait()

    def step(i, carry):
        slot = plan_ref[PUSHED, i]
        start, low = plan_ref[AT_PUSH, slot], plan_ref[ROW, slot] // UNIT
        seen = pltpu.make_async_copy(
            seen_hbm.at[slot], buffer_ref.at[pl.ds(start + units - low, seen_units)], seen_sem
        )
        seen.start()
        pack(plan_ref, slot, own_ref, buffer_ref, start, low, units)
        seen.wait()
        return carry

    lax.fori_loop(0, plan_ref[TOTALS, 0], step, 0)
    store = pltpu.make_async_copy(buffer_ref, out_hbm, sem)
    store.start()
    store.wait()


def pull_kernel(plan_ref, own_hbm, out_hbm, own_ref, buffer_ref, sem):
    load = pltpu.make_async_copy(own_hbm, own_ref, sem)
    load.start()
    load.wait()

    def step(i, carry):
        slot = plan_ref[KEPT, i]
        pack(plan_ref, slot, own_ref, buffer_ref, plan_ref[AT_PULL, slot], 0, (plan_ref[ROW, slot] + UNIT - 1) // UNIT)
        return carry

    lax.fori_loop(0, plan_ref[TOTALS, 1], step, 0)
    store = pltpu.make_async_copy(buffer_ref, out_hbm, sem)
    store.start()
    store.wait()


def grad_kernel(plan_ref, loss_in_ref, probe_hbm, own_hbm, came_hbm, seen_hbm, tables_hbm, grad_in_hbm,
                grad_hbm, back_hbm, loss_ref,
                probe_ref, own_ref, came_ref, seen_ref, tables_ref, grad_ref, back_ref, wave_ref, window_ref, sems,
                *, pushed):
    slices, planes, width, columns = own_ref.shape
    units = width // UNIT
    seen_units = width // (UNIT * UNIT)
    came = pl.ds(units, came_hbm.shape[0])
    loads = [
        pltpu.make_async_copy(probe_hbm, probe_ref, sems.at[0]),
        pltpu.make_async_copy(own_hbm, own_ref, sems.at[1]),
        pltpu.make_async_copy(came_hbm, came_ref.at[came], sems.at[2]),
        pltpu.make_async_copy(tables_hbm, tables_ref, sems.at[3]),
    ]
    if not pushed:
        loads.append(pltpu.make_async_copy(seen_hbm, seen_ref, sems.at[4]))
        loads.append(pltpu.make_async_copy(grad_in_hbm, grad_ref, sems.at[5]))
    for load in loads:
        load.start()
    if pushed:
        grad_ref[...] = jnp.zeros_like(grad_ref)
    for load in loads:
        load.wait()
    row_iota = lax.broadcasted_iota(jnp.int32, (width, width), 0)
    lane_iota = lax.broadcasted_iota(jnp.int32, (width, width), 1)
    count = plan_ref[TOTALS, 0 if pushed else 1]

    def step(group, loss):
        slots, scales, measured = [], [], []
        for b in range(BATCH):
            live = group * BATCH + b < count
            slot = plan_ref[PUSHED if pushed else KEPT, jnp.where(live, group * BATCH + b, group * BATCH)]
            slots.append(slot)
            scales.append(live.astype(jnp.float32))
            row, shift, here, there = place(plan_ref, slot, width, columns)
            mine = row_iota < row if pushed else row_iota >= row
            first = lane_iota >= shift
            low = row // UNIT
            if pushed:
                start = units + plan_ref[AT_PUSH, slot] - low
                seen = came_ref[pl.ds(start + units, seen_units)]
                measured.append(seen.reshape(width, width))
            else:
                start = units + plan_ref[AT_PULL, slot]
                measured.append(seen_ref[slot])
            for l in range(slices):
                for p in range(planes):
                    theirs = came_ref[pl.ds(start, units), l * planes + p].reshape(width, width)
                    ours = jnp.where(first, own_ref[l, p, :, here], own_ref[l, p, :, there])
                    window_ref[b, l, p] = jnp.where(mine, ours, theirs)
            for p in range(planes):
                wave_ref[b, 0, p] = pltpu.roll(pltpu.roll(probe_ref[p], row, 0), shift, 1)
        loss = loss + field_grads(tables_ref, wave_ref, window_ref, measured, scales)
        for b in range(BATCH):
            row, shift, here, there = place(plan_ref, slots[b], width, columns)
            mine = row_iota < row if pushed else row_iota >= row
            first = lane_iota >= shift
            if pushed:
                start, begin, end = plan_ref[AT_BACK, slots[b]], row // UNIT, units
            else:
                start, begin, end = plan_ref[AT_PULL, slots[b]], 0, (row + UNIT - 1) // UNIT

            @pl.when(scales[b] > 0)
            def _(b=b, mine=mine, first=first, here=here, there=there, start=start, begin=begin, end=end):
                for l in range(slices):
                    for p in range(planes):
                        ours = jnp.where(mine, window_ref[b, l, p], 0.0)
                        grad_ref[l, p, :, here] += jnp.where(first, ours, 0.0)
                        grad_ref[l, p, :, there] += jnp.where(first, 0.0, ours)

                def unit(u, carry):
                    rows = pl.ds(pl.multiple_of(u * UNIT, UNIT), UNIT)
                    for l in range(slices):
                        for p in range(planes):
                            back_ref[start + u - begin, l * planes + p] = window_ref[b, l, p, rows, :]
                    return carry

                lax.fori_loop(begin, end, unit, 0)

        return loss

    loss_ref[0] = lax.fori_loop(0, (count + BATCH - 1) // BATCH, step, loss_in_ref[0])
    stores = [
        pltpu.make_async_copy(grad_ref, grad_hbm, sems.at[0]),
        pltpu.make_async_copy(back_ref, back_hbm, sems.at[1]),
    ]
    for store in stores:
        store.start()
    for store in stores:
        store.wait()


def add_kernel(plan_ref, before_ref, grad_in_hbm, pushed_hbm, pulled_hbm, grad_hbm,
               grad_ref, pushed_ref, pulled_ref, sems):
    slices, planes, width, columns = grad_ref.shape
    units = width // UNIT
    loads = [pltpu.make_async_copy(grad_in_hbm.at[l], grad_ref.at[l], sems.at[l]) for l in range(slices)]
    stores = [pltpu.make_async_copy(grad_ref.at[l], grad_hbm.at[l], sems.at[slices + l]) for l in range(slices)]
    others = [
        pltpu.make_async_copy(pushed_hbm, pushed_ref, sems.at[2 * slices]),
        pltpu.make_async_copy(pulled_hbm, pulled_ref, sems.at[2 * slices + 1]),
    ]
    for load in others + loads:
        load.start()
    for load in others:
        load.wait()
    lane_iota = lax.broadcasted_iota(jnp.int32, (UNIT, width), 1)
    row_iota = lax.broadcasted_iota(jnp.int32, (UNIT, width), 0)

    def add(plan, slot, l, came, start, begin, end, below):
        row, shift, here, there = place(plan, slot, width, columns)
        first = lane_iota >= shift

        def unit(u, carry):
            rows = pl.ds(pl.multiple_of(u * UNIT, UNIT), UNIT)
            at = u * UNIT + row_iota
            mine = at < row if below else at >= row
            for p in range(planes):
                piece = jnp.where(mine, came[start + u - begin, l * planes + p], 0.0)
                grad_ref[l, p, rows, here] += jnp.where(first, piece, 0.0)
                grad_ref[l, p, rows, there] += jnp.where(first, 0.0, piece)
            return carry

        lax.fori_loop(begin, end, unit, 0)

    for l in range(slices):
        loads[l].wait()

        def returned(i, carry, l=l):
            slot = plan_ref[PUSHED, i]
            add(plan_ref, slot, l, pushed_ref, plan_ref[AT_BACK, slot], plan_ref[ROW, slot] // UNIT, units, False)
            return carry

        def given(i, carry, l=l):
            slot = before_ref[KEPT, i]
            end = (before_ref[ROW, slot] + UNIT - 1) // UNIT
            add(before_ref, slot, l, pulled_ref, before_ref[AT_PULL, slot], 0, end, True)
            return carry

        lax.fori_loop(0, plan_ref[TOTALS, 0], returned, 0)
        lax.fori_loop(0, before_ref[TOTALS, 1], given, 0)
        stores[l].start()
    for store in stores:
        store.wait()


def shifted(x, axis, by):
    peers = lax.axis_size(axis)
    return lax.ppermute(x, axis, [(i, (i + by) % peers) for i in range(peers)])


def total_of(x, axis):
    peers = lax.axis_size(axis)
    step = 1
    while step < peers:
        def other(by):
            return lax.ppermute(x, axis, [(i, i ^ by) for i in range(peers)])

        if step * 4 <= peers:
            x = (x + other(step)) + (other(2 * step) + other(3 * step))
            step *= 4
        else:
            x = x + other(step)
            step *= 2
    return x


def local(probe_wave, object_slices, intensities, row_offset, col_offset, counts):
    width = probe_wave.shape[-1]
    slices, planes = object_slices.shape[:2]
    cap = row_offset.shape[0]
    units = width // UNIT
    seen_units = width // (UNIT * UNIT)
    tables = jnp.asarray(make_tables(width))
    seen = intensities.reshape(cap, seen_units, UNIT, UNIT, width)
    room = sizes(cap, width)
    smem = pl.BlockSpec(memory_space=pltpu.SMEM)
    hbm = pl.BlockSpec(memory_space=pl.ANY)
    f32 = jnp.float32

    def packed(n):
        return (n, slices * planes, UNIT, width)

    def shape(dims, dtype=f32):
        return jax.ShapeDtypeStruct(dims, dtype)

    params = pltpu.CompilerParams(vmem_limit_bytes=48 << 20)
    strip = object_slices.shape
    plan, push = pl.pallas_call(
        functools.partial(push_kernel, room=room),
        out_shape=(shape((8, cap), jnp.int32), shape(packed(room[0]))),
        in_specs=[smem] * 3 + [hbm] * 2,
        out_specs=(smem, hbm),
        scratch_shapes=[
            pltpu.VMEM(strip, f32),
            pltpu.VMEM(packed(room[0]), f32),
            pltpu.SemaphoreType.DMA,
            pltpu.SemaphoreType.DMA,
        ],
        compiler_params=params,
        name="pack_pushed",
    )(counts, row_offset, col_offset, object_slices, seen)
    pushed = shifted(push, "tile", 1)
    before = shifted(plan, "tile", 1)
    pull = pl.pallas_call(
        pull_kernel,
        out_shape=shape(packed(room[2])),
        in_specs=[smem, hbm],
        out_specs=hbm,
        scratch_shapes=[
            pltpu.VMEM(strip, f32),
            pltpu.VMEM(packed(room[2]), f32),
            pltpu.SemaphoreType.DMA,
        ],
        compiler_params=params,
        name="pack_pulled",
    )(before, object_slices)
    pulled = shifted(pull, "tile", -1)

    def grads(plan, loss, came, grad, back, is_pushed):
        return pl.pallas_call(
            functools.partial(grad_kernel, pushed=is_pushed),
            out_shape=(shape(strip), shape(packed(back)), shape((1,))),
            in_specs=[smem, smem] + [hbm] * 6,
            out_specs=(hbm, hbm, smem),
            scratch_shapes=[
                pltpu.VMEM(probe_wave.shape, f32),
                pltpu.VMEM(strip, f32),
                pltpu.VMEM(packed(came.shape[0] + 2 * units), f32),
                pltpu.VMEM(intensities.shape, f32),
                pltpu.VMEM(tables.shape, tables.dtype),
                pltpu.VMEM(strip, f32),
                pltpu.VMEM(packed(back), f32),
                pltpu.VMEM((BATCH, slices, planes, width, width), f32),
                pltpu.VMEM((BATCH, slices, planes, width, width), f32),
                pltpu.SemaphoreType.DMA((6,)),
            ],
            compiler_params=params,
            name="grads_pushed" if is_pushed else "grads_kept",
        )(plan, loss, probe_wave, object_slices, came, intensities, tables, grad)

    grad, back, loss = grads(before, jnp.zeros((1,), f32), pushed, object_slices, room[1], True)
    returned = shifted(back, "tile", -1)
    grad, back, loss = grads(plan, loss, pulled, grad, room[2], False)
    given = shifted(back, "tile", 1)
    misfit_total = total_of(loss, "tile")
    grad = pl.pallas_call(
        add_kernel,
        out_shape=shape(strip),
        in_specs=[smem, smem] + [hbm] * 3,
        out_specs=hbm,
        scratch_shapes=[
            pltpu.VMEM(strip, f32),
            pltpu.VMEM(packed(room[1]), f32),
            pltpu.VMEM(packed(room[2]), f32),
            pltpu.SemaphoreType.DMA((2 * slices + 2,)),
        ],
        compiler_params=params,
        name="add_returned",
    )(plan, before, grad, returned, given)
    return (grad, misfit_total)


def solution(mesh):
    placed = (
        P(),
        P("parts", None, "tile", None),
        P(("parts", "tile"), None, None),
        P(("parts", "tile")),
        P(("parts", "tile")),
        P(("parts", "tile")),
    )
    return jax.shard_map(
        local,
        mesh=mesh,
        in_specs=placed,
        out_specs=(P("parts", None, "tile", None), P("parts")),
        check_vma=False,
    )
```

```python
import functools

import jax
import jax.numpy as jnp
import ml_dtypes
import numpy as np
from jax import lax
from jax.experimental import pallas as pl
from jax.experimental.pallas import tpu as pltpu
from jax.sharding import PartitionSpec as P

BATCH = 4
UNIT = 8
ROW, COL, AT_PUSH, AT_BACK, AT_PULL, PUSHED, KEPT, TOTALS = range(8)


def make_tables(width):
    indices = np.arange(width)
    dft = np.exp(-2j * np.pi * (np.outer(indices, indices) % width) / width) / np.sqrt(width)
    freqs = np.where(indices < width // 2, indices, indices - width).astype(np.float64)
    along = np.conj(dft) @ (np.exp(-0.0015j * freqs**2)[:, None] * dft)
    out = []
    for matrix in (along, dft):
        left = np.block([[matrix.real, -matrix.imag], [matrix.imag, matrix.real]])
        forms = []
        for form in (left, left.T):
            form = form.astype(np.float32)
            high = form.astype(ml_dtypes.bfloat16)
            low = (form - high.astype(np.float32)).astype(ml_dtypes.bfloat16)
            forms.append(np.stack([high, low]))
        out.append(np.stack(forms))
    return np.stack(out)


def split(x):
    high = x.astype(jnp.bfloat16)
    return high, (x - high.astype(jnp.float32)).astype(jnp.bfloat16)


def dot(a, b):
    return jnp.dot(a, b, preferred_element_type=jnp.float32)


def one_sided(tables, which, form, re, im):
    width = re.shape[0]
    high, low = split(jnp.concatenate([re, im], axis=1))
    m_high, m_low = tables[which, form, 0], tables[which, form, 1]
    out = dot(high, m_high) + (dot(high, m_low) + dot(low, m_high))
    return out[:, :width], out[:, width:]


def two_sided(tables, which, conj, re, im):
    form = 0 if conj else 1
    half = [one_sided(tables, which, form, a, b) for a, b in zip(re, im)]
    full = [one_sided(tables, which, form, a.T, b.T) for a, b in half]
    return [a.T for a, _ in full], [b.T for _, b in full]


def field_grads(tables, wave_ref, window_ref, measured, scales):
    batch, slices = wave_ref.shape[:2]
    for layer in range(slices):
        re, im = [], []
        for b in range(batch):
            w_re, w_im = wave_ref[b, layer, 0], wave_ref[b, layer, 1]
            t_re, t_im = window_ref[b, layer, 0], window_ref[b, layer, 1]
            re.append(w_re * t_re - w_im * t_im)
            im.append(w_re * t_im + w_im * t_re)
        if layer + 1 < slices:
            re, im = two_sided(tables, 0, False, re, im)
            for b in range(batch):
                wave_ref[b, layer + 1, 0] = re[b]
                wave_ref[b, layer + 1, 1] = im[b]
    re, im = two_sided(tables, 1, False, re, im)
    loss = 0.0
    back_re, back_im = [], []
    for b in range(batch):
        misfit = re[b] * re[b] + im[b] * im[b] - measured[b]
        loss = loss + scales[b] * (0.25 * jnp.sum(misfit * misfit))
        back_re.append(misfit * re[b])
        back_im.append(misfit * im[b])
    re, im = two_sided(tables, 1, True, back_re, back_im)
    for layer in reversed(range(slices)):
        upper_re, upper_im = [], []
        for b in range(batch):
            w_re, w_im = wave_ref[b, layer, 0], wave_ref[b, layer, 1]
            t_re, t_im = window_ref[b, layer, 0], window_ref[b, layer, 1]
            window_ref[b, layer, 0] = re[b] * w_re + im[b] * w_im
            window_ref[b, layer, 1] = im[b] * w_re - re[b] * w_im
            upper_re.append(re[b] * t_re + im[b] * t_im)
            upper_im.append(im[b] * t_re - re[b] * t_im)
        if layer > 0:
            re, im = two_sided(tables, 0, True, upper_re, upper_im)
    return loss


def place(plan_ref, slot, width, columns):
    row, col = plan_ref[ROW, slot], plan_ref[COL, slot]
    tile = col // width
    here = pl.ds(pl.multiple_of(tile * width, width), width)
    after = jnp.minimum(tile + 1, columns // width - 1)
    there = pl.ds(pl.multiple_of(after * width, width), width)
    return row, col - tile * width, here, there


def sizes(cap, width):
    whole = cap * width // UNIT
    return whole * 5 // 16, whole // 4, whole * 5 // 16


def make_plan(count_ref, row_ref, col_ref, plan_ref, width, room):
    cap = row_ref.shape[0]
    units = width // UNIT
    seen_units = width // (UNIT * UNIT)
    shape = (UNIT, 128)
    choice = lax.broadcasted_iota(jnp.int32, shape, 0) * 128 + lax.broadcasted_iota(jnp.int32, shape, 1)
    zero = jnp.zeros(shape, jnp.int32)
    push, back, pull, kept, bad = zero, zero, zero, zero, (choice >= (1 << cap)).astype(jnp.int32)
    count = count_ref[0]
    for s in range(cap):
        row = row_ref[s]
        crosses = jnp.logical_and(s < count, row > 0).astype(jnp.int32)
        taken = (choice >> s) & 1
        ahead = units - row // UNIT
        push += taken * (ahead + seen_units)
        back += taken * ahead
        pull += (1 - taken) * (crosses * ((row + UNIT - 1) // UNIT))
        kept += 1 - taken
        bad += taken * (1 - crosses)
    bad += (push > room[0]).astype(jnp.int32) + (back > room[1]).astype(jnp.int32) + (pull > room[2]).astype(jnp.int32)
    score = (kept + 16 * (bad > 0).astype(jnp.int32)) * (1 << cap) + choice
    best = jnp.min(score.astype(jnp.float32)).astype(jnp.int32)
    at_push = at_back = at_pull = n_pushed = n_kept = jnp.int32(0)
    for s in range(cap):
        plan_ref[PUSHED, s] = 0
        plan_ref[KEPT, s] = 0
        plan_ref[TOTALS, s] = 0
    for s in range(cap):
        row = row_ref[s]
        taken = (best >> s) & 1
        kept = jnp.where(s < count, 1 - taken, 0)
        plan_ref[ROW, s] = row
        plan_ref[COL, s] = col_ref[s]
        plan_ref[AT_PUSH, s] = at_push
        plan_ref[AT_BACK, s] = at_back
        plan_ref[AT_PULL, s] = at_pull

        @pl.when(taken > 0)
        def _():
            plan_ref[PUSHED, n_pushed] = s

        @pl.when(kept > 0)
        def _():
            plan_ref[KEPT, n_kept] = s

        ahead = units - row // UNIT
        at_push += taken * (ahead + seen_units)
        at_back += taken * ahead
        at_pull += kept * ((row + UNIT - 1) // UNIT)
        n_pushed += taken
        n_kept += kept
    plan_ref[TOTALS, 0] = n_pushed
    plan_ref[TOTALS, 1] = n_kept


def pack(plan_ref, slot, own_ref, buffer_ref, start, first_unit, last_unit):
    slices, planes, width, columns = own_ref.shape
    _, shift, here, there = place(plan_ref, slot, width, columns)
    first = lax.broadcasted_iota(jnp.int32, (UNIT, width), 1) >= shift

    def step(u, carry):
        rows = pl.ds(pl.multiple_of(u * UNIT, UNIT), UNIT)
        for l in range(slices):
            for p in range(planes):
                buffer_ref[start + u - first_unit, l * planes + p] = jnp.where(
                    first, own_ref[l, p, rows, here], own_ref[l, p, rows, there]
                )
        return carry

    lax.fori_loop(first_unit, last_unit, step, 0)


def push_kernel(count_hbm, row_hbm, col_hbm, own_hbm, seen_hbm, plan_ref, push_ref, own_ref,
                count_ref, row_ref, col_ref, sems, seen_sem, *, room):
    width = own_ref.shape[2]
    units, seen_units = width // UNIT, seen_hbm.shape[1]
    small = [
        pltpu.make_async_copy(count_hbm, count_ref, sems.at[1]),
        pltpu.make_async_copy(row_hbm, row_ref, sems.at[2]),
        pltpu.make_async_copy(col_hbm, col_ref, sems.at[3]),
    ]
    load = pltpu.make_async_copy(own_hbm, own_ref, sems.at[0])
    for copy in small + [load]:
        copy.start()
    for copy in small:
        copy.wait()
    make_plan(count_ref, row_ref, col_ref, plan_ref, width, room)

    def seen(i):
        slot = plan_ref[PUSHED, i]
        start = plan_ref[AT_PUSH, slot] + units - plan_ref[ROW, slot] // UNIT
        return pltpu.make_async_copy(seen_hbm.at[slot], push_ref.at[pl.ds(start, seen_units)], seen_sem.at[i])

    def begin(i, carry):
        seen(i).start()
        return carry

    def step(i, carry):
        slot = plan_ref[PUSHED, i]
        pack(plan_ref, slot, own_ref, push_ref, plan_ref[AT_PUSH, slot], plan_ref[ROW, slot] // UNIT, units)
        return carry

    def end(i, carry):
        seen(i).wait()
        return carry

    lax.fori_loop(0, plan_ref[TOTALS, 0], begin, 0)
    load.wait()
    lax.fori_loop(0, plan_ref[TOTALS, 0], step, 0)
    lax.fori_loop(0, plan_ref[TOTALS, 0], end, 0)


def pull_kernel(plan_ref, own_ref, pull_ref):
    def step(i, carry):
        slot = plan_ref[KEPT, i]
        pack(plan_ref, slot, own_ref, pull_ref, plan_ref[AT_PULL, slot], 0, (plan_ref[ROW, slot] + UNIT - 1) // UNIT)
        return carry

    lax.fori_loop(0, plan_ref[TOTALS, 1], step, 0)


def grad_kernel(plan_ref, probe_ref, own_ref, came_ref, tables_ref, *refs, pushed):
    if pushed:
        grad_ref, back_ref, loss_ref, wave_ref, window_ref = refs
    else:
        loss_in_ref, seen_ref, _, grad_ref, back_ref, loss_ref, wave_ref, window_ref = refs
    slices, planes, width, columns = own_ref.shape
    units = width // UNIT
    seen_units = width // (UNIT * UNIT)
    last = came_ref.shape[0] - 1
    if pushed:
        grad_ref[...] = jnp.zeros_like(grad_ref)
    row_iota = lax.broadcasted_iota(jnp.int32, (width, width), 0)
    lane_iota = lax.broadcasted_iota(jnp.int32, (width, width), 1)
    count = plan_ref[TOTALS, 0 if pushed else 1]

    def step(group, loss):
        slots, scales, measured = [], [], []
        for b in range(BATCH):
            live = group * BATCH + b < count
            slot = plan_ref[PUSHED if pushed else KEPT, jnp.where(live, group * BATCH + b, group * BATCH)]
            slots.append(slot)
            scales.append(live.astype(jnp.float32))
            row, shift, here, there = place(plan_ref, slot, width, columns)
            mine = row_iota < row if pushed else row_iota >= row
            first = lane_iota >= shift
            if pushed:
                start = plan_ref[AT_PUSH, slot] - row // UNIT
                seen = came_ref[pl.ds(jnp.minimum(start + units, last + 1 - seen_units), seen_units)]
                measured.append(seen.reshape(width, width))
            else:
                start = plan_ref[AT_PULL, slot]
                measured.append(seen_ref[slot])
            at = [jnp.clip(start + u, 0, last) for u in range(units)]
            for l in range(slices):
                for p in range(planes):
                    theirs = jnp.concatenate([came_ref[i, l * planes + p] for i in at], axis=0)
                    ours = jnp.where(first, own_ref[l, p, :, here], own_ref[l, p, :, there])
                    window_ref[b, l, p] = jnp.where(mine, ours, theirs)
            for p in range(planes):
                wave_ref[b, 0, p] = pltpu.roll(pltpu.roll(probe_ref[p], row, 0), shift, 1)
        loss = loss + field_grads(tables_ref, wave_ref, window_ref, measured, scales)
        for b in range(BATCH):
            row, shift, here, there = place(plan_ref, slots[b], width, columns)
            mine = row_iota < row if pushed else row_iota >= row
            first = lane_iota >= shift
            if pushed:
                start, begin, end = plan_ref[AT_BACK, slots[b]], row // UNIT, units
            else:
                start, begin, end = plan_ref[AT_PULL, slots[b]], 0, (row + UNIT - 1) // UNIT

            @pl.when(scales[b] > 0)
            def _(b=b, mine=mine, first=first, here=here, there=there, start=start, begin=begin, end=end):
                for l in range(slices):
                    for p in range(planes):
                        ours = jnp.where(mine, window_ref[b, l, p], 0.0)
                        grad_ref[l, p, :, here] += jnp.where(first, ours, 0.0)
                        grad_ref[l, p, :, there] += jnp.where(first, 0.0, ours)

                def unit(u, carry):
                    rows = pl.ds(pl.multiple_of(u * UNIT, UNIT), UNIT)
                    for l in range(slices):
                        for p in range(planes):
                            back_ref[start + u - begin, l * planes + p] = window_ref[b, l, p, rows, :]
                    return carry

                lax.fori_loop(begin, end, unit, 0)

        return loss

    before = jnp.float32(0.0) if pushed else loss_in_ref[0]
    loss_ref[0] = lax.fori_loop(0, (count + BATCH - 1) // BATCH, step, before)


def add_kernel(plan_ref, before_ref, grad_in_ref, pushed_ref, pulled_ref, grad_hbm, grad_ref, sems):
    slices, planes, width, columns = grad_ref.shape
    units = width // UNIT
    lane_iota = lax.broadcasted_iota(jnp.int32, (UNIT, width), 1)
    row_iota = lax.broadcasted_iota(jnp.int32, (UNIT, width), 0)

    def add(plan, slot, l, came, start, begin, end, below):
        row, shift, here, there = place(plan, slot, width, columns)
        first = lane_iota >= shift

        def unit(u, carry):
            rows = pl.ds(pl.multiple_of(u * UNIT, UNIT), UNIT)
            at = u * UNIT + row_iota
            mine = at < row if below else at >= row
            for p in range(planes):
                piece = jnp.where(mine, came[start + u - begin, l * planes + p], 0.0)
                grad_ref[l, p, rows, here] += jnp.where(first, piece, 0.0)
                grad_ref[l, p, rows, there] += jnp.where(first, 0.0, piece)
            return carry

        lax.fori_loop(begin, end, unit, 0)

    stores = [pltpu.make_async_copy(grad_ref.at[l], grad_hbm.at[l], sems.at[l]) for l in range(slices)]
    for l in range(slices):
        grad_ref[l] = grad_in_ref[l]

        def returned(i, carry, l=l):
            slot = plan_ref[PUSHED, i]
            add(plan_ref, slot, l, pushed_ref, plan_ref[AT_BACK, slot], plan_ref[ROW, slot] // UNIT, units, False)
            return carry

        def given(i, carry, l=l):
            slot = before_ref[KEPT, i]
            end = (before_ref[ROW, slot] + UNIT - 1) // UNIT
            add(before_ref, slot, l, pulled_ref, before_ref[AT_PULL, slot], 0, end, True)
            return carry

        lax.fori_loop(0, plan_ref[TOTALS, 0], returned, 0)
        lax.fori_loop(0, before_ref[TOTALS, 1], given, 0)
        stores[l].start()
    for store in stores:
        store.wait()


def shifted(x, axis, by):
    peers = lax.axis_size(axis)
    return lax.ppermute(x, axis, [(i, (i + by) % peers) for i in range(peers)])


def total_of(x, axis):
    peers = lax.axis_size(axis)
    step = 1
    while step < peers:
        def other(by):
            return lax.ppermute(x, axis, [(i, i ^ by) for i in range(peers)])

        if step * 4 <= peers:
            x = (x + other(step)) + (other(2 * step) + other(3 * step))
            step *= 4
        else:
            x = x + other(step)
            step *= 2
    return x


def local(probe_wave, object_slices, intensities, row_offset, col_offset, counts):
    width = probe_wave.shape[-1]
    slices, planes = object_slices.shape[:2]
    cap = row_offset.shape[0]
    units = width // UNIT
    seen_units = width // (UNIT * UNIT)
    tables = jnp.asarray(make_tables(width))
    seen = intensities.reshape(cap, seen_units, UNIT, UNIT, width)
    room = sizes(cap, width)
    smem = pl.BlockSpec(memory_space=pltpu.SMEM)
    vmem = pl.BlockSpec(memory_space=pltpu.VMEM)
    hbm = pl.BlockSpec(memory_space=pl.ANY)
    f32 = jnp.float32

    def packed(n):
        return (n, slices * planes, UNIT, width)

    def shape(dims, dtype=f32):
        return jax.ShapeDtypeStruct(dims, dtype)

    def params(mib):
        return pltpu.CompilerParams(vmem_limit_bytes=mib << 20)

    def cost(us):
        return pl.CostEstimate(flops=int(us * 1e9), bytes_accessed=int(us * 1e6), transcendentals=0)

    strip = object_slices.shape
    plan, push, own = pl.pallas_call(
        functools.partial(push_kernel, room=room),
        out_shape=(shape((8, cap), jnp.int32), shape(packed(room[0])), shape(strip)),
        in_specs=[hbm] * 5,
        out_specs=(smem, vmem, vmem),
        scratch_shapes=[
            pltpu.SMEM(counts.shape, jnp.int32),
            pltpu.SMEM(row_offset.shape, jnp.int32),
            pltpu.SMEM(col_offset.shape, jnp.int32),
            pltpu.SemaphoreType.DMA((4,)),
            pltpu.SemaphoreType.DMA((cap,)),
        ],
        compiler_params=params(16),
        cost_estimate=cost(4),
        name="pack_pushed",
    )(counts, row_offset, col_offset, object_slices, seen)
    pushed = shifted(push, "tile", 1)
    before = shifted(plan, "tile", 1)
    pull = pl.pallas_call(
        pull_kernel,
        out_shape=shape(packed(room[2])),
        in_specs=[smem, vmem],
        out_specs=vmem,
        compiler_params=params(16),
        cost_estimate=cost(1),
        name="pack_pulled",
    )(before, own)
    pulled = shifted(pull, "tile", -1)

    def grads(plan, came, back, *kept):
        return pl.pallas_call(
            functools.partial(grad_kernel, pushed=not kept),
            out_shape=(shape(strip), shape(packed(back)), shape((1,))),
            in_specs=[smem] + [vmem] * 4 + ([smem, vmem, vmem] if kept else []),
            out_specs=(vmem, vmem, smem),
            scratch_shapes=[
                pltpu.VMEM((BATCH, slices, planes, width, width), f32),
                pltpu.VMEM((BATCH, slices, planes, width, width), f32),
            ],
            input_output_aliases={7: 0} if kept else {},
            compiler_params=params(24),
            cost_estimate=cost(10),
            name="grads_kept" if kept else "grads_pushed",
        )(plan, probe_wave, own, came, tables, *kept)

    grad, back, loss = grads(before, pushed, room[1])
    returned = shifted(back, "tile", -1)
    grad, back, loss = grads(plan, pulled, room[2], loss, intensities, grad)
    given = shifted(back, "tile", 1)
    misfit_total = total_of(loss, "tile")
    grad = pl.pallas_call(
        add_kernel,
        out_shape=shape(strip),
        in_specs=[smem, smem] + [vmem] * 3,
        out_specs=hbm,
        scratch_shapes=[pltpu.VMEM(strip, f32), pltpu.SemaphoreType.DMA((slices,))],
        compiler_params=params(16),
        cost_estimate=cost(4),
        name="add_returned",
    )(plan, before, grad, returned, given)
    return (grad, misfit_total)


def solution(mesh):
    placed = (
        P(),
        P("parts", None, "tile", None),
        P(("parts", "tile"), None, None),
        P(("parts", "tile")),
        P(("parts", "tile")),
        P(("parts", "tile")),
    )
    return jax.shard_map(
        local,
        mesh=mesh,
        in_specs=placed,
        out_specs=(P("parts", None, "tile", None), P("parts")),
        check_vma=False,
    )
```

```python
import functools

import jax
import jax.numpy as jnp
import ml_dtypes
import numpy as np
from jax import lax
from jax.experimental import pallas as pl
from jax.experimental.pallas import tpu as pltpu
from jax.sharding import PartitionSpec as P

BATCH = 4
UNIT = 8
ROW, COL, AT_PUSH, AT_BACK, AT_PULL, PUSHED, KEPT, TOTALS = range(8)


def make_tables(width):
    indices = np.arange(width)
    dft = np.exp(-2j * np.pi * (np.outer(indices, indices) % width) / width) / np.sqrt(width)
    freqs = np.where(indices < width // 2, indices, indices - width).astype(np.float64)
    along = np.conj(dft) @ (np.exp(-0.0015j * freqs**2)[:, None] * dft)
    out = []
    for matrix in (along, dft):
        left = np.block([[matrix.real, -matrix.imag], [matrix.imag, matrix.real]])
        forms = []
        for form in (left, left.T):
            form = form.astype(np.float32)
            high = form.astype(ml_dtypes.bfloat16)
            low = (form - high.astype(np.float32)).astype(ml_dtypes.bfloat16)
            forms.append(np.stack([high, low]))
        out.append(np.stack(forms))
    return np.stack(out)


def split(x):
    high = x.astype(jnp.bfloat16)
    return high, (x - high.astype(jnp.float32)).astype(jnp.bfloat16)


def dot(a, b):
    return jnp.dot(a, b, preferred_element_type=jnp.float32)


def one_sided(tables, which, form, re, im):
    width = re.shape[0]
    high, low = split(jnp.concatenate([re, im], axis=1))
    m_high, m_low = tables[which, form, 0], tables[which, form, 1]
    out = dot(high, m_high) + (dot(high, m_low) + dot(low, m_high))
    return out[:, :width], out[:, width:]


def two_sided(tables, which, conj, re, im):
    form = 0 if conj else 1
    half = [one_sided(tables, which, form, a, b) for a, b in zip(re, im)]
    full = [one_sided(tables, which, form, a.T, b.T) for a, b in half]
    return [a.T for a, _ in full], [b.T for _, b in full]


def field_grads(tables, wave_ref, window_ref, measured, scales):
    batch, slices = wave_ref.shape[:2]
    for layer in range(slices):
        re, im = [], []
        for b in range(batch):
            w_re, w_im = wave_ref[b, layer, 0], wave_ref[b, layer, 1]
            t_re, t_im = window_ref[b, layer, 0], window_ref[b, layer, 1]
            re.append(w_re * t_re - w_im * t_im)
            im.append(w_re * t_im + w_im * t_re)
        if layer + 1 < slices:
            re, im = two_sided(tables, 0, False, re, im)
            for b in range(batch):
                wave_ref[b, layer + 1, 0] = re[b]
                wave_ref[b, layer + 1, 1] = im[b]
    re, im = two_sided(tables, 1, False, re, im)
    loss = 0.0
    back_re, back_im = [], []
    for b in range(batch):
        misfit = re[b] * re[b] + im[b] * im[b] - measured[b]
        loss = loss + scales[b] * (0.25 * jnp.sum(misfit * misfit))
        back_re.append(misfit * re[b])
        back_im.append(misfit * im[b])
    re, im = two_sided(tables, 1, True, back_re, back_im)
    for layer in reversed(range(slices)):
        upper_re, upper_im = [], []
        for b in range(batch):
            w_re, w_im = wave_ref[b, layer, 0], wave_ref[b, layer, 1]
            t_re, t_im = window_ref[b, layer, 0], window_ref[b, layer, 1]
            window_ref[b, layer, 0] = re[b] * w_re + im[b] * w_im
            window_ref[b, layer, 1] = im[b] * w_re - re[b] * w_im
            upper_re.append(re[b] * t_re + im[b] * t_im)
            upper_im.append(im[b] * t_re - re[b] * t_im)
        if layer > 0:
            re, im = two_sided(tables, 0, True, upper_re, upper_im)
    return loss


def place(plan_ref, slot, width, columns):
    row, col = plan_ref[ROW, slot], plan_ref[COL, slot]
    tile = col // width
    here = pl.ds(pl.multiple_of(tile * width, width), width)
    after = jnp.minimum(tile + 1, columns // width - 1)
    there = pl.ds(pl.multiple_of(after * width, width), width)
    return row, col - tile * width, here, there


def sizes(cap, width):
    whole = cap * width // UNIT
    return whole * 5 // 16, whole // 4, whole * 5 // 16


def make_plan(meta_ref, plan_ref, width, room):
    cap = plan_ref.shape[1]
    units = width // UNIT
    seen_units = width // (UNIT * UNIT)
    shape = (UNIT, 128)
    choice = lax.broadcasted_iota(jnp.int32, shape, 0) * 128 + lax.broadcasted_iota(jnp.int32, shape, 1)
    zero = jnp.zeros(shape, jnp.int32)
    push, back, pull, kept, bad = zero, zero, zero, zero, (choice >= (1 << cap)).astype(jnp.int32)
    count = meta_ref[0]
    for s in range(cap):
        row = meta_ref[1 + s]
        crosses = jnp.logical_and(s < count, row > 0).astype(jnp.int32)
        taken = (choice >> s) & 1
        ahead = units - row // UNIT
        push += taken * (ahead + seen_units)
        back += taken * ahead
        pull += (1 - taken) * (crosses * ((row + UNIT - 1) // UNIT))
        kept += 1 - taken
        bad += taken * (1 - crosses)
    bad += (push > room[0]).astype(jnp.int32) + (back > room[1]).astype(jnp.int32) + (pull > room[2]).astype(jnp.int32)
    score = (kept + 16 * (bad > 0).astype(jnp.int32)) * (1 << cap) + choice
    best = jnp.min(score.astype(jnp.float32)).astype(jnp.int32)
    at_push = at_back = at_pull = n_pushed = n_kept = jnp.int32(0)
    for s in range(cap):
        plan_ref[PUSHED, s] = 0
        plan_ref[KEPT, s] = 0
        plan_ref[TOTALS, s] = 0
    for s in range(cap):
        row = meta_ref[1 + s]
        taken = (best >> s) & 1
        kept = jnp.where(s < count, 1 - taken, 0)
        plan_ref[ROW, s] = row
        plan_ref[COL, s] = meta_ref[1 + cap + s]
        plan_ref[AT_PUSH, s] = at_push
        plan_ref[AT_BACK, s] = at_back
        plan_ref[AT_PULL, s] = at_pull

        @pl.when(taken > 0)
        def _():
            plan_ref[PUSHED, n_pushed] = s

        @pl.when(kept > 0)
        def _():
            plan_ref[KEPT, n_kept] = s

        ahead = units - row // UNIT
        at_push += taken * (ahead + seen_units)
        at_back += taken * ahead
        at_pull += kept * ((row + UNIT - 1) // UNIT)
        n_pushed += taken
        n_kept += kept
    plan_ref[TOTALS, 0] = n_pushed
    plan_ref[TOTALS, 1] = n_kept


def pack(plan_ref, slot, own_ref, buffer_ref, start, first_unit, last_unit):
    slices, planes, width, columns = own_ref.shape
    _, shift, here, there = place(plan_ref, slot, width, columns)
    first = lax.broadcasted_iota(jnp.int32, (UNIT, width), 1) >= shift

    def step(u, carry):
        rows = pl.ds(pl.multiple_of(u * UNIT, UNIT), UNIT)
        for l in range(slices):
            for p in range(planes):
                buffer_ref[start + u - first_unit, l * planes + p] = jnp.where(
                    first, own_ref[l, p, rows, here], own_ref[l, p, rows, there]
                )
        return carry

    lax.fori_loop(first_unit, last_unit, step, 0)


def push_kernel(meta_ref, own_hbm, seen_hbm, plan_ref, push_ref, own_ref, sem, sems, *, room):
    width = own_ref.shape[2]
    units, seen_units = width // UNIT, seen_hbm.shape[1]
    load = pltpu.make_async_copy(own_hbm, own_ref, sem)
    load.start()
    make_plan(meta_ref, plan_ref, width, room)

    def seen(i):
        slot = plan_ref[PUSHED, i]
        start = plan_ref[AT_PUSH, slot] + units - plan_ref[ROW, slot] // UNIT
        return pltpu.make_async_copy(seen_hbm.at[slot], push_ref.at[pl.ds(start, seen_units)], sems.at[i])

    def begin(i, carry):
        seen(i).start()
        return carry

    def step(i, carry):
        slot = plan_ref[PUSHED, i]
        pack(plan_ref, slot, own_ref, push_ref, plan_ref[AT_PUSH, slot], plan_ref[ROW, slot] // UNIT, units)
        return carry

    def end(i, carry):
        seen(i).wait()
        return carry

    lax.fori_loop(0, plan_ref[TOTALS, 0], begin, 0)
    load.wait()
    lax.fori_loop(0, plan_ref[TOTALS, 0], step, 0)
    lax.fori_loop(0, plan_ref[TOTALS, 0], end, 0)


def pull_kernel(meta_ref, own_ref, push_in_ref, plan_ref, pull_ref, push_ref, *, room):
    make_plan(meta_ref, plan_ref, own_ref.shape[2], room)

    def step(i, carry):
        slot = plan_ref[KEPT, i]
        end = (plan_ref[ROW, slot] + UNIT - 1) // UNIT
        pack(plan_ref, slot, own_ref, pull_ref, plan_ref[AT_PULL, slot], 0, end)
        return carry

    lax.fori_loop(0, plan_ref[TOTALS, 1], step, 0)


def grad_kernel(plan_ref, probe_ref, own_ref, came_ref, tables_ref, *refs, pushed):
    if pushed:
        grad_ref, back_ref, loss_ref, wave_ref, window_ref = refs
    else:
        loss_in_ref, seen_ref, _, grad_ref, back_ref, loss_ref, wave_ref, window_ref = refs
    slices, planes, width, columns = own_ref.shape
    units = width // UNIT
    seen_units = width // (UNIT * UNIT)
    last = came_ref.shape[0] - 1
    if pushed:
        grad_ref[...] = jnp.zeros_like(grad_ref)
    row_iota = lax.broadcasted_iota(jnp.int32, (width, width), 0)
    lane_iota = lax.broadcasted_iota(jnp.int32, (width, width), 1)
    count = plan_ref[TOTALS, 0 if pushed else 1]

    def step(group, loss):
        slots, scales, measured = [], [], []
        for b in range(BATCH):
            live = group * BATCH + b < count
            slot = plan_ref[PUSHED if pushed else KEPT, jnp.where(live, group * BATCH + b, group * BATCH)]
            slots.append(slot)
            scales.append(live.astype(jnp.float32))
            row, shift, here, there = place(plan_ref, slot, width, columns)
            mine = row_iota < row if pushed else row_iota >= row
            first = lane_iota >= shift
            if pushed:
                start = plan_ref[AT_PUSH, slot] - row // UNIT
                seen = came_ref[pl.ds(jnp.minimum(start + units, last + 1 - seen_units), seen_units)]
                measured.append(seen.reshape(width, width))
            else:
                start = plan_ref[AT_PULL, slot]
                measured.append(seen_ref[slot])
            at = [jnp.clip(start + u, 0, last) for u in range(units)]
            for l in range(slices):
                for p in range(planes):
                    theirs = jnp.concatenate([came_ref[i, l * planes + p] for i in at], axis=0)
                    ours = jnp.where(first, own_ref[l, p, :, here], own_ref[l, p, :, there])
                    window_ref[b, l, p] = jnp.where(mine, ours, theirs)
            for p in range(planes):
                wave_ref[b, 0, p] = pltpu.roll(pltpu.roll(probe_ref[p], row, 0), shift, 1)
        loss = loss + field_grads(tables_ref, wave_ref, window_ref, measured, scales)
        for b in range(BATCH):
            row, shift, here, there = place(plan_ref, slots[b], width, columns)
            mine = row_iota < row if pushed else row_iota >= row
            first = lane_iota >= shift
            if pushed:
                start, begin, end = plan_ref[AT_BACK, slots[b]], row // UNIT, units
            else:
                start, begin, end = plan_ref[AT_PULL, slots[b]], 0, (row + UNIT - 1) // UNIT

            @pl.when(scales[b] > 0)
            def _(b=b, mine=mine, first=first, here=here, there=there, start=start, begin=begin, end=end):
                for l in range(slices):
                    for p in range(planes):
                        ours = jnp.where(mine, window_ref[b, l, p], 0.0)
                        grad_ref[l, p, :, here] += jnp.where(first, ours, 0.0)
                        grad_ref[l, p, :, there] += jnp.where(first, 0.0, ours)

                def unit(u, carry):
                    rows = pl.ds(pl.multiple_of(u * UNIT, UNIT), UNIT)
                    for l in range(slices):
                        for p in range(planes):
                            back_ref[start + u - begin, l * planes + p] = window_ref[b, l, p, rows, :]
                    return carry

                lax.fori_loop(begin, end, unit, 0)

        return loss

    before = jnp.float32(0.0) if pushed else loss_in_ref[0]
    loss_ref[0] = lax.fori_loop(0, (count + BATCH - 1) // BATCH, step, before)


def after_kernel(x_ref, *refs):
    pass


def add(plan, slot, grad_ref, layers, came, start, begin, end, below):
    planes, width, columns = grad_ref.shape[1:]
    row, shift, here, there = place(plan, slot, width, columns)
    first = lax.broadcasted_iota(jnp.int32, (UNIT, width), 1) >= shift
    row_iota = lax.broadcasted_iota(jnp.int32, (UNIT, width), 0)

    def unit(u, carry):
        rows = pl.ds(pl.multiple_of(u * UNIT, UNIT), UNIT)
        at = u * UNIT + row_iota
        mine = at < row if below else at >= row
        for l in layers:
            for p in range(planes):
                piece = jnp.where(mine, came[start + u - begin, l * planes + p], 0.0)
                grad_ref[l, p, rows, here] += jnp.where(first, piece, 0.0)
                grad_ref[l, p, rows, there] += jnp.where(first, 0.0, piece)
        return carry

    lax.fori_loop(begin, end, unit, 0)


def add_returned_kernel(plan_ref, returned_ref, grad_in_ref, grad_ref):
    slices, _, width, _ = grad_ref.shape

    def step(i, carry):
        slot = plan_ref[PUSHED, i]
        at, low = plan_ref[AT_BACK, slot], plan_ref[ROW, slot] // UNIT
        add(plan_ref, slot, grad_ref, range(slices), returned_ref, at, low, width // UNIT, False)
        return carry

    lax.fori_loop(0, plan_ref[TOTALS, 0], step, 0)


def add_given_kernel(before_ref, given_ref, grad_ref, grad_hbm, sems):
    slices = grad_ref.shape[0]
    stores = [pltpu.make_async_copy(grad_ref.at[l], grad_hbm.at[l], sems.at[l]) for l in range(slices)]
    for l in range(slices):

        def step(i, carry, l=l):
            slot = before_ref[KEPT, i]
            end = (before_ref[ROW, slot] + UNIT - 1) // UNIT
            add(before_ref, slot, grad_ref, [l], given_ref, before_ref[AT_PULL, slot], 0, end, True)
            return carry

        lax.fori_loop(0, before_ref[TOTALS, 1], step, 0)
        stores[l].start()
    for store in stores:
        store.wait()


def shifted(x, axis, by):
    peers = lax.axis_size(axis)
    return lax.ppermute(x, axis, [(i, (i + by) % peers) for i in range(peers)])


def total_stages(peers):
    stages, step = [], 1
    while step < peers:
        radix = 4 if step * 4 <= peers else 2
        stages.append((step, radix))
        step *= radix
    return stages


def partial_total(x, axis, stage):
    peers = lax.axis_size(axis)
    step, radix = stage

    def other(by):
        return lax.ppermute(x, axis, [(i, i ^ by) for i in range(peers)])

    if radix == 2:
        return x + other(step)
    return (x + other(step)) + (other(2 * step) + other(3 * step))


def local(probe_wave, object_slices, intensities, row_offset, col_offset, counts):
    width = probe_wave.shape[-1]
    slices, planes = object_slices.shape[:2]
    cap = row_offset.shape[0]
    units = width // UNIT
    seen_units = width // (UNIT * UNIT)
    tables = jnp.asarray(make_tables(width))
    seen = intensities.reshape(cap, seen_units, UNIT, UNIT, width)
    room = sizes(cap, width)
    smem = pl.BlockSpec(memory_space=pltpu.SMEM)
    vmem = pl.BlockSpec(memory_space=pltpu.VMEM)
    hbm = pl.BlockSpec(memory_space=pl.ANY)
    f32 = jnp.float32

    def packed(n):
        return (n, slices * planes, UNIT, width)

    def shape(dims, dtype=f32):
        return jax.ShapeDtypeStruct(dims, dtype)

    def params(mib):
        return pltpu.CompilerParams(vmem_limit_bytes=int(mib * 2**20))

    def cost(us):
        return pl.CostEstimate(flops=int(us * 1e9), bytes_accessed=int(us * 1e6), transcendentals=0)

    strip = object_slices.shape
    meta = jnp.concatenate([counts, row_offset, col_offset])
    meta_before = shifted(meta, "tile", 1)
    plan_shape = shape((8, cap), jnp.int32)
    plan, push, own = pl.pallas_call(
        functools.partial(push_kernel, room=room),
        out_shape=(plan_shape, shape(packed(room[0])), shape(strip)),
        in_specs=[smem, hbm, hbm],
        out_specs=(smem, vmem, vmem),
        scratch_shapes=[pltpu.SemaphoreType.DMA, pltpu.SemaphoreType.DMA((cap,))],
        compiler_params=params(48),
        cost_estimate=cost(8),
        name="pack_pushed",
    )(meta, object_slices, seen)
    before, pull, push = pl.pallas_call(
        functools.partial(pull_kernel, room=room),
        out_shape=(plan_shape, shape(packed(room[2])), shape(push.shape)),
        in_specs=[smem, vmem, hbm],
        out_specs=(smem, vmem, hbm),
        input_output_aliases={2: 2},
        compiler_params=params(16),
        cost_estimate=cost(2),
        name="pack_pulled",
    )(meta_before, own, push)
    pushed = shifted(push, "tile", 1)
    pulled = shifted(pull, "tile", -1)

    def grads(plan, came, back, *kept):
        return pl.pallas_call(
            functools.partial(grad_kernel, pushed=not kept),
            out_shape=(shape(strip), shape(packed(back)), shape((1,))),
            in_specs=[smem] + [vmem] * 4 + ([smem, vmem, vmem] if kept else []),
            out_specs=(vmem, vmem, smem),
            scratch_shapes=[
                pltpu.VMEM((BATCH, slices, planes, width, width), f32),
                pltpu.VMEM((BATCH, slices, planes, width, width), f32),
            ],
            input_output_aliases={7: 0} if kept else {},
            compiler_params=params(24),
            cost_estimate=cost(10),
            name="grads_kept" if kept else "grads_pushed",
        )(plan, probe_wave, own, came, tables, *kept)

    grad, back, loss = grads(before, pushed, room[1])
    returned = shifted(back, "tile", -1)
    grad, back, loss = grads(plan, pulled, room[2], loss, intensities, grad)
    stages = total_stages(lax.axis_size("tile"))
    loss = partial_total(loss, "tile", stages[0])
    back = pl.pallas_call(
        after_kernel,
        out_shape=shape(back.shape),
        in_specs=[hbm, hbm, hbm],
        out_specs=hbm,
        input_output_aliases={0: 0},
        compiler_params=params(4),
        name="after_returned",
    )(back, returned, loss)
    given = shifted(back, "tile", 1)
    for stage in stages[1:]:
        loss = partial_total(loss, "tile", stage)
    misfit_total = loss.reshape(1)
    grad = pl.pallas_call(
        add_returned_kernel,
        out_shape=shape(strip),
        in_specs=[smem, vmem, vmem],
        out_specs=vmem,
        input_output_aliases={2: 0},
        compiler_params=params(4),
        cost_estimate=cost(1),
        name="add_returned",
    )(plan, returned, grad)
    grad = pl.pallas_call(
        add_given_kernel,
        out_shape=shape(strip),
        in_specs=[smem, vmem, vmem],
        out_specs=hbm,
        scratch_shapes=[pltpu.SemaphoreType.DMA((slices,))],
        compiler_params=params(4),
        cost_estimate=cost(4),
        name="add_given",
    )(before, given, grad)
    return (grad, misfit_total)


def solution(mesh):
    placed = (
        P(),
        P("parts", None, "tile", None),
        P(("parts", "tile"), None, None),
        P(("parts", "tile")),
        P(("parts", "tile")),
        P(("parts", "tile")),
    )
    return jax.shard_map(
        local,
        mesh=mesh,
        in_specs=placed,
        out_specs=(P("parts", None, "tile", None), P("parts")),
        check_vma=False,
    )
```

```python
import functools

import jax
import jax.numpy as jnp
import ml_dtypes
import numpy as np
from jax import lax
from jax.experimental import pallas as pl
from jax.experimental.pallas import tpu as pltpu
from jax.sharding import PartitionSpec as P

BATCH = 4
UNIT = 8
ROW, COL, AT_PUSH, AT_BACK, AT_PULL, PUSHED, KEPT, TOTALS = range(8)


def make_tables(width):
    indices = np.arange(width)
    dft = np.exp(-2j * np.pi * (np.outer(indices, indices) % width) / width) / np.sqrt(width)
    freqs = np.where(indices < width // 2, indices, indices - width).astype(np.float64)
    along = np.conj(dft) @ (np.exp(-0.0015j * freqs**2)[:, None] * dft)
    out = []
    for matrix in (along, dft):
        left = np.block([[matrix.real, -matrix.imag], [matrix.imag, matrix.real]])
        forms = []
        for form in (left, left.T):
            form = form.astype(np.float32)
            high = form.astype(ml_dtypes.bfloat16)
            low = (form - high.astype(np.float32)).astype(ml_dtypes.bfloat16)
            forms.append(np.stack([high, low]))
        out.append(np.stack(forms))
    return np.stack(out)


def split(x):
    high = x.astype(jnp.bfloat16)
    return high, (x - high.astype(jnp.float32)).astype(jnp.bfloat16)


def dot(a, b):
    return jnp.dot(a, b, preferred_element_type=jnp.float32)


def one_sided(tables, which, form, re, im):
    width = re.shape[0]
    high, low = split(jnp.concatenate([re, im], axis=1))
    m_high, m_low = tables[which, form, 0], tables[which, form, 1]
    out = dot(high, m_high) + (dot(high, m_low) + dot(low, m_high))
    return out[:, :width], out[:, width:]


def two_sided(tables, which, conj, re, im):
    form = 0 if conj else 1
    half = [one_sided(tables, which, form, a, b) for a, b in zip(re, im)]
    full = [one_sided(tables, which, form, a.T, b.T) for a, b in half]
    return [a.T for a, _ in full], [b.T for _, b in full]


def field_grads(tables, wave_ref, window_ref, measured, scales):
    batch, slices = wave_ref.shape[:2]
    for layer in range(slices):
        re, im = [], []
        for b in range(batch):
            w_re, w_im = wave_ref[b, layer, 0], wave_ref[b, layer, 1]
            t_re, t_im = window_ref[b, layer, 0], window_ref[b, layer, 1]
            re.append(w_re * t_re - w_im * t_im)
            im.append(w_re * t_im + w_im * t_re)
        if layer + 1 < slices:
            re, im = two_sided(tables, 0, False, re, im)
            for b in range(batch):
                wave_ref[b, layer + 1, 0] = re[b]
                wave_ref[b, layer + 1, 1] = im[b]
    re, im = two_sided(tables, 1, False, re, im)
    loss = 0.0
    back_re, back_im = [], []
    for b in range(batch):
        misfit = re[b] * re[b] + im[b] * im[b] - measured[b]
        loss = loss + scales[b] * (0.25 * jnp.sum(misfit * misfit))
        back_re.append(misfit * re[b])
        back_im.append(misfit * im[b])
    re, im = two_sided(tables, 1, True, back_re, back_im)
    for layer in reversed(range(slices)):
        upper_re, upper_im = [], []
        for b in range(batch):
            w_re, w_im = wave_ref[b, layer, 0], wave_ref[b, layer, 1]
            t_re, t_im = window_ref[b, layer, 0], window_ref[b, layer, 1]
            window_ref[b, layer, 0] = re[b] * w_re + im[b] * w_im
            window_ref[b, layer, 1] = im[b] * w_re - re[b] * w_im
            upper_re.append(re[b] * t_re + im[b] * t_im)
            upper_im.append(im[b] * t_re - re[b] * t_im)
        if layer > 0:
            re, im = two_sided(tables, 0, True, upper_re, upper_im)
    return loss


def place(plan_ref, slot, width, columns):
    row, col = plan_ref[ROW, slot], plan_ref[COL, slot]
    tile = col // width
    here = pl.ds(pl.multiple_of(tile * width, width), width)
    after = jnp.minimum(tile + 1, columns // width - 1)
    there = pl.ds(pl.multiple_of(after * width, width), width)
    return row, col - tile * width, here, there


def sizes(cap, width):
    whole = cap * width // UNIT
    return whole * 5 // 16, whole // 4, whole * 5 // 16


def make_plan(meta_ref, plan_ref, width, room):
    cap = plan_ref.shape[1]
    units = width // UNIT
    seen_units = width // (UNIT * UNIT)
    shape = (UNIT, 128)
    choice = lax.broadcasted_iota(jnp.int32, shape, 0) * 128 + lax.broadcasted_iota(jnp.int32, shape, 1)
    zero = jnp.zeros(shape, jnp.int32)
    push, back, pull, kept, bad = zero, zero, zero, zero, (choice >= (1 << cap)).astype(jnp.int32)
    count = meta_ref[0]
    for s in range(cap):
        row = meta_ref[1 + s]
        crosses = jnp.logical_and(s < count, row > 0).astype(jnp.int32)
        taken = (choice >> s) & 1
        ahead = units - row // UNIT
        push += taken * (ahead + seen_units)
        back += taken * ahead
        pull += (1 - taken) * (crosses * ((row + UNIT - 1) // UNIT))
        kept += 1 - taken
        bad += taken * (1 - crosses)
    bad += (push > room[0]).astype(jnp.int32) + (back > room[1]).astype(jnp.int32) + (pull > room[2]).astype(jnp.int32)
    score = (kept + 16 * (bad > 0).astype(jnp.int32)) * (1 << cap) + choice
    best = jnp.min(score.astype(jnp.float32)).astype(jnp.int32)
    at_push = at_back = at_pull = n_pushed = n_kept = jnp.int32(0)
    for s in range(cap):
        plan_ref[PUSHED, s] = 0
        plan_ref[KEPT, s] = 0
        plan_ref[TOTALS, s] = 0
    for s in range(cap):
        row = meta_ref[1 + s]
        taken = (best >> s) & 1
        kept = jnp.where(s < count, 1 - taken, 0)
        plan_ref[ROW, s] = row
        plan_ref[COL, s] = meta_ref[1 + cap + s]
        plan_ref[AT_PUSH, s] = at_push
        plan_ref[AT_BACK, s] = at_back
        plan_ref[AT_PULL, s] = at_pull

        @pl.when(taken > 0)
        def _():
            plan_ref[PUSHED, n_pushed] = s

        @pl.when(kept > 0)
        def _():
            plan_ref[KEPT, n_kept] = s

        ahead = units - row // UNIT
        at_push += taken * (ahead + seen_units)
        at_back += taken * ahead
        at_pull += kept * ((row + UNIT - 1) // UNIT)
        n_pushed += taken
        n_kept += kept
    plan_ref[TOTALS, 0] = n_pushed
    plan_ref[TOTALS, 1] = n_kept


def pack(plan_ref, slot, own_ref, buffer_ref, start, first_unit, last_unit):
    slices, planes, width, columns = own_ref.shape
    _, shift, here, there = place(plan_ref, slot, width, columns)
    first = lax.broadcasted_iota(jnp.int32, (UNIT, width), 1) >= shift

    def step(u, carry):
        rows = pl.ds(pl.multiple_of(u * UNIT, UNIT), UNIT)
        for l in range(slices):
            for p in range(planes):
                buffer_ref[start + u - first_unit, l * planes + p] = jnp.where(
                    first, own_ref[l, p, rows, here], own_ref[l, p, rows, there]
                )
        return carry

    lax.fori_loop(first_unit, last_unit, step, 0)


def push_kernel(meta_ref, own_hbm, seen_hbm, plan_ref, push_ref, own_ref, sem, sems, *, room):
    width = own_ref.shape[2]
    units, seen_units = width // UNIT, seen_hbm.shape[1]
    load = pltpu.make_async_copy(own_hbm, own_ref, sem)
    load.start()
    make_plan(meta_ref, plan_ref, width, room)

    def seen(i):
        slot = plan_ref[PUSHED, i]
        start = plan_ref[AT_PUSH, slot] + units - plan_ref[ROW, slot] // UNIT
        return pltpu.make_async_copy(seen_hbm.at[slot], push_ref.at[pl.ds(start, seen_units)], sems.at[i])

    def begin(i, carry):
        seen(i).start()
        return carry

    def step(i, carry):
        slot = plan_ref[PUSHED, i]
        pack(plan_ref, slot, own_ref, push_ref, plan_ref[AT_PUSH, slot], plan_ref[ROW, slot] // UNIT, units)
        return carry

    def end(i, carry):
        seen(i).wait()
        return carry

    lax.fori_loop(0, plan_ref[TOTALS, 0], begin, 0)
    shape = (UNIT, width)
    index = lax.broadcasted_iota(jnp.int32, shape, 0) * width + lax.broadcasted_iota(jnp.int32, shape, 1)
    told = jnp.zeros(shape, jnp.float32)
    for r in range(plan_ref.shape[0]):
        for s in range(plan_ref.shape[1]):
            told = jnp.where(index == r * width + s, plan_ref[r, s].astype(jnp.float32), told)
    push_ref[room[0], 0] = told
    load.wait()
    lax.fori_loop(0, plan_ref[TOTALS, 0], step, 0)
    lax.fori_loop(0, plan_ref[TOTALS, 0], end, 0)


def pull_kernel(told_ref, own_ref, plan_ref, pull_ref, whole_ref, numbers_ref, sem):
    whole_ref[...] = told_ref[told_ref.shape[0] - 1, 0].astype(jnp.int32)
    copy = pltpu.make_async_copy(whole_ref, numbers_ref, sem)
    copy.start()
    copy.wait()
    for r in range(plan_ref.shape[0]):
        for s in range(plan_ref.shape[1]):
            plan_ref[r, s] = numbers_ref[r, s]

    def step(i, carry):
        slot = plan_ref[KEPT, i]
        end = (plan_ref[ROW, slot] + UNIT - 1) // UNIT
        pack(plan_ref, slot, own_ref, pull_ref, plan_ref[AT_PULL, slot], 0, end)
        return carry

    lax.fori_loop(0, plan_ref[TOTALS, 1], step, 0)


def grad_kernel(plan_ref, probe_ref, own_ref, came_ref, tables_ref, *refs, pushed):
    if pushed:
        grad_ref, back_ref, loss_ref, wave_ref, window_ref = refs
    else:
        loss_in_ref, seen_ref, _, grad_ref, back_ref, loss_ref, wave_ref, window_ref = refs
    slices, planes, width, columns = own_ref.shape
    units = width // UNIT
    seen_units = width // (UNIT * UNIT)
    last = came_ref.shape[0] - 1
    if pushed:
        grad_ref[...] = jnp.zeros_like(grad_ref)
    row_iota = lax.broadcasted_iota(jnp.int32, (width, width), 0)
    lane_iota = lax.broadcasted_iota(jnp.int32, (width, width), 1)
    count = plan_ref[TOTALS, 0 if pushed else 1]

    def step(group, loss):
        slots, scales, measured = [], [], []
        for b in range(BATCH):
            live = group * BATCH + b < count
            slot = plan_ref[PUSHED if pushed else KEPT, jnp.where(live, group * BATCH + b, group * BATCH)]
            slots.append(slot)
            scales.append(live.astype(jnp.float32))
            row, shift, here, there = place(plan_ref, slot, width, columns)
            mine = row_iota < row if pushed else row_iota >= row
            first = lane_iota >= shift
            if pushed:
                start = plan_ref[AT_PUSH, slot] - row // UNIT
                seen = came_ref[pl.ds(jnp.minimum(start + units, last + 1 - seen_units), seen_units)]
                measured.append(seen.reshape(width, width))
            else:
                start = plan_ref[AT_PULL, slot]
                measured.append(seen_ref[slot])
            at = [jnp.clip(start + u, 0, last) for u in range(units)]
            for l in range(slices):
                for p in range(planes):
                    theirs = jnp.concatenate([came_ref[i, l * planes + p] for i in at], axis=0)
                    ours = jnp.where(first, own_ref[l, p, :, here], own_ref[l, p, :, there])
                    window_ref[b, l, p] = jnp.where(mine, ours, theirs)
            for p in range(planes):
                wave_ref[b, 0, p] = pltpu.roll(pltpu.roll(probe_ref[p], row, 0), shift, 1)
        loss = loss + field_grads(tables_ref, wave_ref, window_ref, measured, scales)
        for b in range(BATCH):
            row, shift, here, there = place(plan_ref, slots[b], width, columns)
            mine = row_iota < row if pushed else row_iota >= row
            first = lane_iota >= shift
            if pushed:
                start, begin, end = plan_ref[AT_BACK, slots[b]], row // UNIT, units
            else:
                start, begin, end = plan_ref[AT_PULL, slots[b]], 0, (row + UNIT - 1) // UNIT

            @pl.when(scales[b] > 0)
            def _(b=b, mine=mine, first=first, here=here, there=there, start=start, begin=begin, end=end):
                for l in range(slices):
                    for p in range(planes):
                        ours = jnp.where(mine, window_ref[b, l, p], 0.0)
                        grad_ref[l, p, :, here] += jnp.where(first, ours, 0.0)
                        grad_ref[l, p, :, there] += jnp.where(first, 0.0, ours)

                def unit(u, carry):
                    rows = pl.ds(pl.multiple_of(u * UNIT, UNIT), UNIT)
                    for l in range(slices):
                        for p in range(planes):
                            back_ref[start + u - begin, l * planes + p] = window_ref[b, l, p, rows, :]
                    return carry

                lax.fori_loop(begin, end, unit, 0)

        return loss

    before = jnp.float32(0.0) if pushed else loss_in_ref[0]
    loss_ref[0] = lax.fori_loop(0, (count + BATCH - 1) // BATCH, step, before)


def after_kernel(x_ref, *refs):
    pass


def add(plan, slot, grad_ref, layers, came, start, begin, end, below):
    planes, width, columns = grad_ref.shape[1:]
    row, shift, here, there = place(plan, slot, width, columns)
    first = lax.broadcasted_iota(jnp.int32, (UNIT, width), 1) >= shift
    row_iota = lax.broadcasted_iota(jnp.int32, (UNIT, width), 0)

    def unit(u, carry):
        rows = pl.ds(pl.multiple_of(u * UNIT, UNIT), UNIT)
        at = u * UNIT + row_iota
        mine = at < row if below else at >= row
        for l in layers:
            for p in range(planes):
                piece = jnp.where(mine, came[start + u - begin, l * planes + p], 0.0)
                grad_ref[l, p, rows, here] += jnp.where(first, piece, 0.0)
                grad_ref[l, p, rows, there] += jnp.where(first, 0.0, piece)
        return carry

    lax.fori_loop(begin, end, unit, 0)


def add_returned_kernel(plan_ref, returned_ref, grad_in_ref, grad_ref):
    slices, _, width, _ = grad_ref.shape

    def step(i, carry):
        slot = plan_ref[PUSHED, i]
        at, low = plan_ref[AT_BACK, slot], plan_ref[ROW, slot] // UNIT
        add(plan_ref, slot, grad_ref, range(slices), returned_ref, at, low, width // UNIT, False)
        return carry

    lax.fori_loop(0, plan_ref[TOTALS, 0], step, 0)


def add_given_kernel(before_ref, given_ref, grad_ref, grad_hbm, sems):
    slices = grad_ref.shape[0]
    stores = [pltpu.make_async_copy(grad_ref.at[l], grad_hbm.at[l], sems.at[l]) for l in range(slices)]
    for l in range(slices):

        def step(i, carry, l=l):
            slot = before_ref[KEPT, i]
            end = (before_ref[ROW, slot] + UNIT - 1) // UNIT
            add(before_ref, slot, grad_ref, [l], given_ref, before_ref[AT_PULL, slot], 0, end, True)
            return carry

        lax.fori_loop(0, before_ref[TOTALS, 1], step, 0)
        stores[l].start()
    for store in stores:
        store.wait()


def shifted(x, axis, by):
    peers = lax.axis_size(axis)
    return lax.ppermute(x, axis, [(i, (i + by) % peers) for i in range(peers)])


def total_stages(peers):
    stages, step = [], 1
    while step < peers:
        radix = 4 if step * 4 <= peers else 2
        stages.append((step, radix))
        step *= radix
    return stages


def partial_total(x, axis, stage):
    peers = lax.axis_size(axis)
    step, radix = stage

    def other(by):
        return lax.ppermute(x, axis, [(i, i ^ by) for i in range(peers)])

    if radix == 2:
        return x + other(step)
    return (x + other(step)) + (other(2 * step) + other(3 * step))


def local(probe_wave, object_slices, intensities, row_offset, col_offset, counts):
    width = probe_wave.shape[-1]
    slices, planes = object_slices.shape[:2]
    cap = row_offset.shape[0]
    units = width // UNIT
    seen_units = width // (UNIT * UNIT)
    tables = jnp.asarray(make_tables(width))
    seen = intensities.reshape(cap, seen_units, UNIT, UNIT, width)
    room = sizes(cap, width)
    smem = pl.BlockSpec(memory_space=pltpu.SMEM)
    vmem = pl.BlockSpec(memory_space=pltpu.VMEM)
    hbm = pl.BlockSpec(memory_space=pltpu.HBM)
    anywhere = pl.BlockSpec(memory_space=pl.ANY)
    f32 = jnp.float32

    def packed(n):
        return (n, slices * planes, UNIT, width)

    def shape(dims, dtype=f32):
        return jax.ShapeDtypeStruct(dims, dtype)

    def params(mib):
        return pltpu.CompilerParams(vmem_limit_bytes=int(mib * 2**20))

    def cost(us):
        return pl.CostEstimate(flops=int(us * 1e9), bytes_accessed=int(us * 1e6), transcendentals=0)

    strip = object_slices.shape
    meta = jnp.concatenate([counts, row_offset, col_offset])
    plan_shape = shape((8, cap), jnp.int32)
    plan, push, own = pl.pallas_call(
        functools.partial(push_kernel, room=room),
        out_shape=(plan_shape, shape(packed(room[0] + 1)), shape(strip)),
        in_specs=[smem, hbm, hbm],
        out_specs=(smem, vmem, vmem),
        scratch_shapes=[pltpu.SemaphoreType.DMA, pltpu.SemaphoreType.DMA((cap,))],
        compiler_params=params(48),
        cost_estimate=cost(4),
        name="pack_pushed",
    )(meta, object_slices, seen)
    pushed = shifted(push, "tile", 1)
    before, pull = pl.pallas_call(
        pull_kernel,
        out_shape=(plan_shape, shape(packed(room[2]))),
        in_specs=[vmem, vmem],
        out_specs=(smem, vmem),
        scratch_shapes=[
            pltpu.VMEM((UNIT, width), jnp.int32),
            pltpu.SMEM((UNIT, width), jnp.int32),
            pltpu.SemaphoreType.DMA,
        ],
        compiler_params=params(16),
        cost_estimate=cost(2),
        name="pack_pulled",
    )(pushed, own)
    pulled = shifted(pull, "tile", -1)

    def grads(plan, came, back, *kept):
        return pl.pallas_call(
            functools.partial(grad_kernel, pushed=not kept),
            out_shape=(shape(strip), shape(packed(back)), shape((1,))),
            in_specs=[smem] + [vmem] * 4 + ([smem, vmem, vmem] if kept else []),
            out_specs=(vmem, vmem, smem),
            scratch_shapes=[
                pltpu.VMEM((BATCH, slices, planes, width, width), f32),
                pltpu.VMEM((BATCH, slices, planes, width, width), f32),
            ],
            input_output_aliases={7: 0} if kept else {},
            compiler_params=params(24),
            cost_estimate=cost(10),
            name="grads_kept" if kept else "grads_pushed",
        )(plan, probe_wave, own, came, tables, *kept)

    grad, back, loss = grads(before, pushed, room[1])
    returned = shifted(back, "tile", -1)
    grad, back, loss = grads(plan, pulled, room[2], loss, intensities, grad)
    stages = total_stages(lax.axis_size("tile"))
    loss = partial_total(loss, "tile", stages[0])
    back = pl.pallas_call(
        after_kernel,
        out_shape=shape(back.shape),
        in_specs=[anywhere] * 3,
        out_specs=anywhere,
        input_output_aliases={0: 0},
        compiler_params=params(4),
        name="after_returned",
    )(back, returned, loss)
    given = shifted(back, "tile", 1)
    for stage in stages[1:]:
        loss = partial_total(loss, "tile", stage)
    misfit_total = loss.reshape(1)
    grad = pl.pallas_call(
        add_returned_kernel,
        out_shape=shape(strip),
        in_specs=[smem, vmem, vmem],
        out_specs=vmem,
        input_output_aliases={2: 0},
        compiler_params=params(4),
        cost_estimate=cost(1),
        name="add_returned",
    )(plan, returned, grad)
    grad = pl.pallas_call(
        add_given_kernel,
        out_shape=shape(strip),
        in_specs=[smem, vmem, vmem],
        out_specs=hbm,
        scratch_shapes=[pltpu.SemaphoreType.DMA((slices,))],
        compiler_params=params(4),
        cost_estimate=cost(4),
        name="add_given",
    )(before, given, grad)
    return (grad, misfit_total)


def solution(mesh):
    placed = (
        P(),
        P("parts", None, "tile", None),
        P(("parts", "tile"), None, None),
        P(("parts", "tile")),
        P(("parts", "tile")),
        P(("parts", "tile")),
    )
    return jax.shard_map(
        local,
        mesh=mesh,
        in_specs=placed,
        out_specs=(P("parts", None, "tile", None), P("parts")),
        check_vma=False,
    )
```

```python
import functools

import jax
import jax.numpy as jnp
import ml_dtypes
import numpy as np
from jax import lax
from jax.experimental import pallas as pl
from jax.experimental.pallas import tpu as pltpu
from jax.sharding import PartitionSpec as P

BATCH = 4
UNIT = 8
ROW, COL, AT_PUSH, AT_BACK, AT_PULL, PUSHED, KEPT, TOTALS = range(8)


def make_tables(width):
    indices = np.arange(width)
    dft = np.exp(-2j * np.pi * (np.outer(indices, indices) % width) / width) / np.sqrt(width)
    freqs = np.where(indices < width // 2, indices, indices - width).astype(np.float64)
    along = np.conj(dft) @ (np.exp(-0.0015j * freqs**2)[:, None] * dft)
    out = []
    for matrix in (along, dft):
        left = np.block([[matrix.real, -matrix.imag], [matrix.imag, matrix.real]])
        forms = []
        for form in (left, left.T):
            form = form.astype(np.float32)
            high = form.astype(ml_dtypes.bfloat16)
            low = (form - high.astype(np.float32)).astype(ml_dtypes.bfloat16)
            forms.append(np.stack([high, low]))
        out.append(np.stack(forms))
    return np.stack(out)


def split(x):
    high = x.astype(jnp.bfloat16)
    return high, (x - high.astype(jnp.float32)).astype(jnp.bfloat16)


def dot(a, b):
    return jnp.dot(a, b, preferred_element_type=jnp.float32)


def one_sided(tables, which, form, re, im):
    width = re.shape[0]
    high, low = split(jnp.concatenate([re, im], axis=1))
    m_high, m_low = tables[which, form, 0], tables[which, form, 1]
    out = dot(high, m_high) + (dot(high, m_low) + dot(low, m_high))
    return out[:, :width], out[:, width:]


def two_sided(tables, which, conj, re, im):
    form = 0 if conj else 1
    half = [one_sided(tables, which, form, a, b) for a, b in zip(re, im)]
    full = [one_sided(tables, which, form, a.T, b.T) for a, b in half]
    return [a.T for a, _ in full], [b.T for _, b in full]


def field_grads(tables, wave_ref, window_ref, measured, scales):
    batch, slices = wave_ref.shape[:2]
    for layer in range(slices):
        re, im = [], []
        for b in range(batch):
            w_re, w_im = wave_ref[b, layer, 0], wave_ref[b, layer, 1]
            t_re, t_im = window_ref[b, layer, 0], window_ref[b, layer, 1]
            re.append(w_re * t_re - w_im * t_im)
            im.append(w_re * t_im + w_im * t_re)
        if layer + 1 < slices:
            re, im = two_sided(tables, 0, False, re, im)
            for b in range(batch):
                wave_ref[b, layer + 1, 0] = re[b]
                wave_ref[b, layer + 1, 1] = im[b]
    re, im = two_sided(tables, 1, False, re, im)
    loss = 0.0
    back_re, back_im = [], []
    for b in range(batch):
        misfit = re[b] * re[b] + im[b] * im[b] - measured[b]
        loss = loss + scales[b] * (0.25 * jnp.sum(misfit * misfit))
        back_re.append(misfit * re[b])
        back_im.append(misfit * im[b])
    re, im = two_sided(tables, 1, True, back_re, back_im)
    for layer in reversed(range(slices)):
        upper_re, upper_im = [], []
        for b in range(batch):
            w_re, w_im = wave_ref[b, layer, 0], wave_ref[b, layer, 1]
            t_re, t_im = window_ref[b, layer, 0], window_ref[b, layer, 1]
            window_ref[b, layer, 0] = re[b] * w_re + im[b] * w_im
            window_ref[b, layer, 1] = im[b] * w_re - re[b] * w_im
            upper_re.append(re[b] * t_re + im[b] * t_im)
            upper_im.append(im[b] * t_re - re[b] * t_im)
        if layer > 0:
            re, im = two_sided(tables, 0, True, upper_re, upper_im)
    return loss


def place(plan_ref, slot, width, columns):
    row, col = plan_ref[ROW, slot], plan_ref[COL, slot]
    tile = col // width
    here = pl.ds(pl.multiple_of(tile * width, width), width)
    after = jnp.minimum(tile + 1, columns // width - 1)
    there = pl.ds(pl.multiple_of(after * width, width), width)
    return row, col - tile * width, here, there


def sizes(cap, width):
    whole = cap * width // UNIT
    first = (whole * 9 // 32, whole * 27 // 128, whole * 33 // 128)
    return first, (whole * 5 // 16, whole // 4, whole * 5 // 16)


def make_plan(meta_ref, plan_ref, width, rooms, again):
    cap = plan_ref.shape[1]
    units = width // UNIT
    seen_units = width // (UNIT * UNIT)
    shape = (UNIT, 128)
    choice = lax.broadcasted_iota(jnp.int32, shape, 0) * 128 + lax.broadcasted_iota(jnp.int32, shape, 1)
    zero = jnp.zeros(shape, jnp.int32)
    push, back, pull, n_push, bad = zero, zero, zero, zero, (choice >= (1 << cap)).astype(jnp.int32)
    count = meta_ref[0]
    for s in range(cap):
        row = meta_ref[1 + s]
        crosses = jnp.logical_and(s < count, row > 0).astype(jnp.int32)
        taken = (choice >> s) & 1
        ahead = units - row // UNIT
        push += taken * (ahead + seen_units)
        back += taken * ahead
        pull += (1 - taken) * (crosses * ((row + UNIT - 1) // UNIT))
        n_push += taken
        bad += taken * (1 - crosses)
    n_keep = count - n_push
    groups = (n_push + BATCH - 1) // BATCH + (n_keep + BATCH - 1) // BATCH
    worst = 16 * cap

    def best_of(room):
        over = bad + (push > room[0]).astype(jnp.int32) + (back > room[1]).astype(jnp.int32) + (pull > room[2]).astype(jnp.int32)
        score = (groups * 16 + n_keep + worst * (over > 0).astype(jnp.int32)) * (1 << cap) + choice
        return jnp.min(score.astype(jnp.float32)).astype(jnp.int32)

    best = best_of(rooms[0])
    short = (best >= worst << cap).astype(jnp.int32)
    if again:
        best = best_of(rooms[1])
    at_push = at_back = at_pull = n_pushed = n_kept = jnp.int32(0)
    for s in range(cap):
        plan_ref[PUSHED, s] = 0
        plan_ref[KEPT, s] = 0
        plan_ref[TOTALS, s] = 0
    for s in range(cap):
        row = meta_ref[1 + s]
        crosses = (row > 0).astype(jnp.int32)
        now = short * crosses if again else 1 - short * crosses
        taken = ((best >> s) & 1) * (short if again else 1 - short)
        kept = jnp.where(s < count, (1 - taken) * now, 0)
        plan_ref[ROW, s] = row
        plan_ref[COL, s] = meta_ref[1 + cap + s]
        plan_ref[AT_PUSH, s] = at_push
        plan_ref[AT_BACK, s] = at_back
        plan_ref[AT_PULL, s] = at_pull

        @pl.when(taken > 0)
        def _():
            plan_ref[PUSHED, n_pushed] = s

        @pl.when(kept > 0)
        def _():
            plan_ref[KEPT, n_kept] = s

        ahead = units - row // UNIT
        at_push += taken * (ahead + seen_units)
        at_back += taken * ahead
        at_pull += kept * ((row + UNIT - 1) // UNIT)
        n_pushed += taken
        n_kept += kept
    plan_ref[TOTALS, 0] = n_pushed
    plan_ref[TOTALS, 1] = n_kept
    plan_ref[TOTALS, 2] = short


def pack(plan_ref, slot, own_ref, buffer_ref, start, first_unit, last_unit):
    slices, planes, width, columns = own_ref.shape
    _, shift, here, there = place(plan_ref, slot, width, columns)
    first = lax.broadcasted_iota(jnp.int32, (UNIT, width), 1) >= shift

    def step(u, carry):
        rows = pl.ds(pl.multiple_of(u * UNIT, UNIT), UNIT)
        for l in range(slices):
            for p in range(planes):
                buffer_ref[start + u - first_unit, l * planes + p] = jnp.where(
                    first, own_ref[l, p, rows, here], own_ref[l, p, rows, there]
                )
        return carry

    lax.fori_loop(first_unit, last_unit, step, 0)


def push_kernel(meta_ref, own_in_ref, seen_hbm, plan_ref, push_ref, *refs, rooms, again):
    if again:
        own_ref = own_in_ref
        sems, = refs
    else:
        own_ref, left_ref, sem, sems = refs
        load = pltpu.make_async_copy(own_in_ref, own_ref, sem)
        load.start()
    width = own_ref.shape[2]
    units, seen_units = width // UNIT, seen_hbm.shape[1]
    make_plan(meta_ref, plan_ref, width, rooms, again)

    def seen(i):
        slot = plan_ref[PUSHED, i]
        start = plan_ref[AT_PUSH, slot] + units - plan_ref[ROW, slot] // UNIT
        return pltpu.make_async_copy(seen_hbm.at[slot], push_ref.at[pl.ds(start, seen_units)], sems.at[i])

    def begin(i, carry):
        seen(i).start()
        return carry

    def step(i, carry):
        slot = plan_ref[PUSHED, i]
        pack(plan_ref, slot, own_ref, push_ref, plan_ref[AT_PUSH, slot], plan_ref[ROW, slot] // UNIT, units)
        return carry

    def end(i, carry):
        seen(i).wait()
        return carry

    lax.fori_loop(0, plan_ref[TOTALS, 0], begin, 0)
    shape = (UNIT, width)
    index = lax.broadcasted_iota(jnp.int32, shape, 0) * width + lax.broadcasted_iota(jnp.int32, shape, 1)
    told = jnp.zeros(shape, jnp.float32)
    for r in range(plan_ref.shape[0]):
        for s in range(plan_ref.shape[1]):
            told = jnp.where(index == r * width + s, plan_ref[r, s].astype(jnp.float32), told)
    push_ref[push_ref.shape[0] - 1, 0] = told
    if not again:
        left_ref[...] = jnp.full(left_ref.shape, plan_ref[TOTALS, 2].astype(jnp.float32))
        load.wait()
    lax.fori_loop(0, plan_ref[TOTALS, 0], step, 0)
    lax.fori_loop(0, plan_ref[TOTALS, 0], end, 0)


def start_kernel(lefts_ref, grad_ref, left_ref):
    grad_ref[...] = jnp.zeros_like(grad_ref)
    left_ref[0] = jnp.sum(lefts_ref[...])


def pull_kernel(told_ref, own_ref, plan_ref, pull_ref, whole_ref, numbers_ref, sem):
    whole_ref[...] = told_ref[told_ref.shape[0] - 1, 0].astype(jnp.int32)
    copy = pltpu.make_async_copy(whole_ref, numbers_ref, sem)
    copy.start()
    copy.wait()
    for r in range(plan_ref.shape[0]):
        for s in range(plan_ref.shape[1]):
            plan_ref[r, s] = numbers_ref[r, s]

    def step(i, carry):
        slot = plan_ref[KEPT, i]
        end = (plan_ref[ROW, slot] + UNIT - 1) // UNIT
        pack(plan_ref, slot, own_ref, pull_ref, plan_ref[AT_PULL, slot], 0, end)
        return carry

    lax.fori_loop(0, plan_ref[TOTALS, 1], step, 0)


def grad_kernel(plan_ref, probe_ref, own_ref, came_ref, tables_ref, loss_in_ref, *refs, pushed):
    if pushed:
        grad_in_ref, grad_ref, back_ref, loss_ref, wave_ref, window_ref = refs
    else:
        grad_in_ref, seen_ref, grad_ref, back_ref, loss_ref, wave_ref, window_ref = refs
    grad_ref[...] = grad_in_ref[...]
    slices, planes, width, columns = own_ref.shape
    units = width // UNIT
    seen_units = width // (UNIT * UNIT)
    last = came_ref.shape[0] - 1
    row_iota = lax.broadcasted_iota(jnp.int32, (width, width), 0)
    lane_iota = lax.broadcasted_iota(jnp.int32, (width, width), 1)
    count = plan_ref[TOTALS, 0 if pushed else 1]

    def step(group, loss):
        slots, scales, measured = [], [], []
        for b in range(BATCH):
            live = group * BATCH + b < count
            slot = plan_ref[PUSHED if pushed else KEPT, jnp.where(live, group * BATCH + b, group * BATCH)]
            slots.append(slot)
            scales.append(live.astype(jnp.float32))
            row, shift, here, there = place(plan_ref, slot, width, columns)
            mine = row_iota < row if pushed else row_iota >= row
            first = lane_iota >= shift
            if pushed:
                start = plan_ref[AT_PUSH, slot] - row // UNIT
                seen = came_ref[pl.ds(jnp.minimum(start + units, last + 1 - seen_units), seen_units)]
                measured.append(seen.reshape(width, width))
            else:
                start = plan_ref[AT_PULL, slot]
                measured.append(seen_ref[slot])
            at = [jnp.clip(start + u, 0, last) for u in range(units)]
            for l in range(slices):
                for p in range(planes):
                    theirs = jnp.concatenate([came_ref[i, l * planes + p] for i in at], axis=0)
                    ours = jnp.where(first, own_ref[l, p, :, here], own_ref[l, p, :, there])
                    window_ref[b, l, p] = jnp.where(mine, ours, theirs)
            for p in range(planes):
                wave_ref[b, 0, p] = pltpu.roll(pltpu.roll(probe_ref[p], row, 0), shift, 1)
        loss = loss + field_grads(tables_ref, wave_ref, window_ref, measured, scales)
        for b in range(BATCH):
            row, shift, here, there = place(plan_ref, slots[b], width, columns)
            mine = row_iota < row if pushed else row_iota >= row
            first = lane_iota >= shift
            if pushed:
                start, begin, end = plan_ref[AT_BACK, slots[b]], row // UNIT, units
            else:
                start, begin, end = plan_ref[AT_PULL, slots[b]], 0, (row + UNIT - 1) // UNIT

            @pl.when(scales[b] > 0)
            def _(b=b, mine=mine, first=first, here=here, there=there, start=start, begin=begin, end=end):
                for l in range(slices):
                    for p in range(planes):
                        ours = jnp.where(mine, window_ref[b, l, p], 0.0)
                        grad_ref[l, p, :, here] += jnp.where(first, ours, 0.0)
                        grad_ref[l, p, :, there] += jnp.where(first, 0.0, ours)

                def unit(u, carry):
                    rows = pl.ds(pl.multiple_of(u * UNIT, UNIT), UNIT)
                    for l in range(slices):
                        for p in range(planes):
                            back_ref[start + u - begin, l * planes + p] = window_ref[b, l, p, rows, :]
                    return carry

                lax.fori_loop(begin, end, unit, 0)

        return loss

    loss_ref[0] = lax.fori_loop(0, (count + BATCH - 1) // BATCH, step, loss_in_ref[0])


def after_kernel(loss_ref, x_ref, first_ref, x_out_ref, losses_ref):
    losses_ref[...] = jnp.full(losses_ref.shape, loss_ref[0])


def add(plan, slot, grad_ref, layers, came, start, begin, end, below):
    planes, width, columns = grad_ref.shape[1:]
    row, shift, here, there = place(plan, slot, width, columns)
    first = lax.broadcasted_iota(jnp.int32, (UNIT, width), 1) >= shift
    row_iota = lax.broadcasted_iota(jnp.int32, (UNIT, width), 0)

    def unit(u, carry):
        rows = pl.ds(pl.multiple_of(u * UNIT, UNIT), UNIT)
        at = u * UNIT + row_iota
        mine = at < row if below else at >= row
        for l in layers:
            for p in range(planes):
                piece = jnp.where(mine, came[start + u - begin, l * planes + p], 0.0)
                grad_ref[l, p, rows, here] += jnp.where(first, piece, 0.0)
                grad_ref[l, p, rows, there] += jnp.where(first, 0.0, piece)
        return carry

    lax.fori_loop(begin, end, unit, 0)


def add_returned_kernel(plan_ref, returned_ref, grad_in_ref, grad_ref):
    slices, _, width, _ = grad_ref.shape
    grad_ref[...] = grad_in_ref[...]

    def step(i, carry):
        slot = plan_ref[PUSHED, i]
        at, low = plan_ref[AT_BACK, slot], plan_ref[ROW, slot] // UNIT
        add(plan_ref, slot, grad_ref, range(slices), returned_ref, at, low, width // UNIT, False)
        return carry

    lax.fori_loop(0, plan_ref[TOTALS, 0], step, 0)


def add_given(before_ref, given_ref, grad_ref, layers):
    def step(i, carry):
        slot = before_ref[KEPT, i]
        end = (before_ref[ROW, slot] + UNIT - 1) // UNIT
        add(before_ref, slot, grad_ref, layers, given_ref, before_ref[AT_PULL, slot], 0, end, True)
        return carry

    lax.fori_loop(0, before_ref[TOTALS, 1], step, 0)


def add_given_kernel(before_ref, given_ref, grad_in_ref, grad_ref):
    grad_ref[...] = grad_in_ref[...]
    add_given(before_ref, given_ref, grad_ref, range(grad_ref.shape[0]))


def finish_kernel(before_ref, given_ref, losses_ref, grad_in_ref, grad_hbm, loss_ref, grad_ref, sems):
    slices = grad_ref.shape[0]
    stores = [pltpu.make_async_copy(grad_ref.at[l], grad_hbm.at[l], sems.at[l]) for l in range(slices)]
    for l in range(slices):
        grad_ref[l] = grad_in_ref[l]
        add_given(before_ref, given_ref, grad_ref, [l])
        stores[l].start()
    lanes = lax.broadcasted_iota(jnp.int32, losses_ref.shape, 1)
    loss_ref[0] = jnp.sum(jnp.where(lanes == 0, losses_ref[...], 0.0))
    for store in stores:
        store.wait()


def shifted(x, axis, by):
    peers = lax.axis_size(axis)
    return lax.ppermute(x, axis, [(i, (i + by) % peers) for i in range(peers)])


def local(probe_wave, object_slices, intensities, row_offset, col_offset, counts):
    width = probe_wave.shape[-1]
    slices, planes = object_slices.shape[:2]
    cap = row_offset.shape[0]
    peers = lax.axis_size("tile")
    units, seen_units = width // UNIT, width // (UNIT * UNIT)
    tables = jnp.asarray(make_tables(width))
    meta = jnp.concatenate([counts, row_offset, col_offset])
    seen = intensities.reshape(cap, seen_units, UNIT, UNIT, width)
    rooms = sizes(cap, width)
    smem = pl.BlockSpec(memory_space=pltpu.SMEM)
    vmem = pl.BlockSpec(memory_space=pltpu.VMEM)
    anywhere = pl.BlockSpec(memory_space=pl.ANY)
    f32 = jnp.float32

    def shape(dims, dtype=f32):
        return jax.ShapeDtypeStruct(dims, dtype)

    def packed(n):
        return shape((n, slices * planes, UNIT, width))

    def call(kernel, name, cost, ins, in_specs, outs, out_specs, scratch=(), mib=16, aliases=None):
        return pl.pallas_call(
            kernel,
            out_shape=outs,
            in_specs=in_specs,
            out_specs=out_specs,
            scratch_shapes=scratch,
            input_output_aliases=aliases or {},
            compiler_params=pltpu.CompilerParams(vmem_limit_bytes=mib << 20),
            cost_estimate=pl.CostEstimate(flops=int(cost * 1e9), bytes_accessed=int(cost * 1e6), transcendentals=0),
            name=name,
        )(*ins)

    strip = shape(object_slices.shape)
    plan_shape = shape((8, cap), jnp.int32)
    rows = shape((peers, width))
    one = shape((1,))
    dma = pltpu.SemaphoreType.DMA

    def ahead(source, again):
        kernel = functools.partial(push_kernel, rooms=rooms, again=again)
        ins, outs = (meta, source, seen), (plan_shape, packed(rooms[again][0] + 1))
        if again:
            return call(kernel, "pack_more", 4, ins, [smem, vmem, anywhere], outs, (smem, vmem), [dma((cap,))])
        return call(
            kernel, "pack_pushed", 4, ins, [smem, anywhere, anywhere], outs + (strip, rows), (smem, vmem, vmem, vmem),
            [dma, dma((cap,))], 50,
        )

    def behind(pushed, own, again):
        scratch = [pltpu.VMEM((UNIT, width), jnp.int32), pltpu.SMEM((UNIT, width), jnp.int32), dma]
        outs = (plan_shape, packed(rooms[again][2]))
        return call(pull_kernel, "pack_pulled", 2, (pushed, own), [vmem, vmem], outs, (smem, vmem), scratch)

    def grads(plan, own, came, loss, grad, back, is_pushed):
        name, more = ("grads_pushed", ()) if is_pushed else ("grads_kept", (intensities,))
        buffer = pltpu.VMEM((BATCH, slices, planes, width, width), f32)
        return call(
            functools.partial(grad_kernel, pushed=is_pushed), name, 10,
            (plan, probe_wave, own, came, tables, loss, grad) + more,
            [smem] + [vmem] * 4 + [smem, vmem] + [vmem] * len(more),
            (strip, packed(back), one), (vmem, vmem, smem), [buffer, buffer], 24, {6: 0},
        )

    def add_returned(plan, returned, grad):
        return call(
            add_returned_kernel, "add_returned", 1, (plan, returned, grad), [smem, vmem, vmem], strip, vmem, aliases={2: 0}
        )

    plan, push, own, left = ahead(object_slices, False)
    pushed = shifted(push, "tile", 1)
    lefts = lax.all_to_all(left, "tile", 0, 0, tiled=True)
    before, pull = behind(pushed, own, False)
    pulled = shifted(pull, "tile", -1)
    grad, left = call(start_kernel, "start", 1, (lefts,), [vmem], (strip, one), (vmem, smem))

    def unfinished(carry):
        return carry[2][0] > 0

    def second(carry):
        grad, loss, _ = carry
        plan, push = ahead(own, True)
        pushed = shifted(push, "tile", 1)
        before, pull = behind(pushed, own, True)
        pulled = shifted(pull, "tile", -1)
        grad, back, loss = grads(before, own, pushed, loss, grad, rooms[1][1], True)
        returned = shifted(back, "tile", -1)
        grad, back, loss = grads(plan, own, pulled, loss, grad, rooms[1][2], False)
        given = shifted(back, "tile", 1)
        grad = add_returned(plan, returned, grad)
        grad = call(add_given_kernel, "add_given", 1, (before, given, grad), [smem, vmem, vmem], strip, vmem, aliases={2: 0})
        return grad, loss, jnp.zeros_like(left)

    grad, loss, _ = lax.while_loop(unfinished, second, (grad, jnp.zeros((1,), f32), left))
    grad, back, loss = grads(before, own, pushed, loss, grad, rooms[0][1], True)
    returned = shifted(back, "tile", -1)
    grad, back, loss = grads(plan, own, pulled, loss, grad, rooms[0][2], False)
    back, losses = call(
        after_kernel, "after_returned", 1, (loss, back, returned), [smem, anywhere, anywhere],
        (shape(back.shape), rows), (anywhere, vmem), aliases={1: 0},
    )
    given = shifted(back, "tile", 1)
    losses = lax.all_to_all(losses, "tile", 0, 0, tiled=True)
    grad = add_returned(plan, returned, grad)
    return call(
        finish_kernel, "add_given", 4, (before, given, losses, grad), [smem, vmem, vmem, vmem],
        (strip, one), (anywhere, smem), [pltpu.VMEM(strip.shape, f32), dma((slices,))],
    )


def solution(mesh):
    placed = (
        P(),
        P("parts", None, "tile", None),
        P(("parts", "tile"), None, None),
        P(("parts", "tile")),
        P(("parts", "tile")),
        P(("parts", "tile")),
    )
    return jax.shard_map(
        local,
        mesh=mesh,
        in_specs=placed,
        out_specs=(P("parts", None, "tile", None), P("parts")),
        check_vma=False,
    )
```

```python
import functools

import jax
import jax.numpy as jnp
import ml_dtypes
import numpy as np
from jax import lax
from jax.experimental import pallas as pl
from jax.experimental.pallas import tpu as pltpu
from jax.sharding import PartitionSpec as P

BATCH = 4
UNIT = 8
ROW, COL, AT_PUSH, AT_BACK, AT_PULL, PUSHED, KEPT, TOTALS = range(8)


def make_tables(width):
    indices = np.arange(width)
    dft = np.exp(-2j * np.pi * (np.outer(indices, indices) % width) / width) / np.sqrt(width)
    freqs = np.where(indices < width // 2, indices, indices - width).astype(np.float64)
    along = np.conj(dft) @ (np.exp(-0.0015j * freqs**2)[:, None] * dft)
    out = []
    for matrix in (along, dft):
        left = np.block([[matrix.real, -matrix.imag], [matrix.imag, matrix.real]])
        forms = []
        for form in (left, left.T):
            form = form.astype(np.float32)
            high = form.astype(ml_dtypes.bfloat16)
            low = (form - high.astype(np.float32)).astype(ml_dtypes.bfloat16)
            forms.append(np.stack([high, low]))
        out.append(np.stack(forms))
    return np.stack(out)


def split(x):
    high = x.astype(jnp.bfloat16)
    return high, (x - high.astype(jnp.float32)).astype(jnp.bfloat16)


def dot(a, b):
    return jnp.dot(a, b, preferred_element_type=jnp.float32)


def one_sided(tables, which, form, re, im):
    width = re.shape[0]
    high, low = split(jnp.concatenate([re, im], axis=1))
    m_high, m_low = tables[which, form, 0], tables[which, form, 1]
    out = dot(high, m_high) + (dot(high, m_low) + dot(low, m_high))
    return out[:, :width], out[:, width:]


def two_sided(tables, which, conj, re, im):
    form = 0 if conj else 1
    half = [one_sided(tables, which, form, a, b) for a, b in zip(re, im)]
    full = [one_sided(tables, which, form, a.T, b.T) for a, b in half]
    return [a.T for a, _ in full], [b.T for _, b in full]


def field_grads(tables, wave_ref, window_ref, measured, scales):
    batch, slices = wave_ref.shape[:2]
    for layer in range(slices):
        re, im = [], []
        for b in range(batch):
            w_re, w_im = wave_ref[b, layer, 0], wave_ref[b, layer, 1]
            t_re, t_im = window_ref[b, layer, 0], window_ref[b, layer, 1]
            re.append(w_re * t_re - w_im * t_im)
            im.append(w_re * t_im + w_im * t_re)
        if layer + 1 < slices:
            re, im = two_sided(tables, 0, False, re, im)
            for b in range(batch):
                wave_ref[b, layer + 1, 0] = re[b]
                wave_ref[b, layer + 1, 1] = im[b]
    re, im = two_sided(tables, 1, False, re, im)
    loss = 0.0
    back_re, back_im = [], []
    for b in range(batch):
        misfit = re[b] * re[b] + im[b] * im[b] - measured[b]
        loss = loss + scales[b] * (0.25 * jnp.sum(misfit * misfit))
        back_re.append(misfit * re[b])
        back_im.append(misfit * im[b])
    re, im = two_sided(tables, 1, True, back_re, back_im)
    for layer in reversed(range(slices)):
        upper_re, upper_im = [], []
        for b in range(batch):
            w_re, w_im = wave_ref[b, layer, 0], wave_ref[b, layer, 1]
            t_re, t_im = window_ref[b, layer, 0], window_ref[b, layer, 1]
            window_ref[b, layer, 0] = re[b] * w_re + im[b] * w_im
            window_ref[b, layer, 1] = im[b] * w_re - re[b] * w_im
            upper_re.append(re[b] * t_re + im[b] * t_im)
            upper_im.append(im[b] * t_re - re[b] * t_im)
        if layer > 0:
            re, im = two_sided(tables, 0, True, upper_re, upper_im)
    return loss


def place(plan_ref, slot, width, columns):
    row, col = plan_ref[ROW, slot], plan_ref[COL, slot]
    tile = col // width
    here = pl.ds(pl.multiple_of(tile * width, width), width)
    after = jnp.minimum(tile + 1, columns // width - 1)
    there = pl.ds(pl.multiple_of(after * width, width), width)
    return row, col - tile * width, here, there


def sizes(cap, width):
    whole = cap * width // UNIT
    first = (whole * 9 // 32, whole * 27 // 128, whole * 33 // 128)
    return first, (whole * 5 // 16, whole // 4, whole * 5 // 16)


def make_plan(meta_ref, plan_ref, width, rooms, again):
    cap = plan_ref.shape[1]
    units = width // UNIT
    seen_units = width // (UNIT * UNIT)
    shape = (UNIT, 128)
    choice = lax.broadcasted_iota(jnp.int32, shape, 0) * 128 + lax.broadcasted_iota(jnp.int32, shape, 1)
    zero = jnp.zeros(shape, jnp.int32)
    push, back, pull, n_push, bad = zero, zero, zero, zero, (choice >= (1 << cap)).astype(jnp.int32)
    count = meta_ref[0]
    for s in range(cap):
        row = meta_ref[1 + s]
        crosses = jnp.logical_and(s < count, row > 0).astype(jnp.int32)
        taken = (choice >> s) & 1
        ahead = units - row // UNIT
        push += taken * (ahead + seen_units)
        back += taken * ahead
        pull += (1 - taken) * (crosses * ((row + UNIT - 1) // UNIT))
        n_push += taken
        bad += taken * (1 - crosses)
    n_keep = count - n_push
    groups = (n_push + BATCH - 1) // BATCH + (n_keep + BATCH - 1) // BATCH
    worst = 16 * cap

    def best_of(room):
        over = bad + (push > room[0]).astype(jnp.int32) + (back > room[1]).astype(jnp.int32) + (pull > room[2]).astype(jnp.int32)
        score = (groups * 16 + n_keep + worst * (over > 0).astype(jnp.int32)) * (1 << cap) + choice
        return jnp.min(score.astype(jnp.float32)).astype(jnp.int32)

    best = best_of(rooms[0])
    short = (best >= worst << cap).astype(jnp.int32)
    if again:
        best = best_of(rooms[1])
    at_push = at_back = at_pull = n_pushed = n_kept = jnp.int32(0)
    for s in range(cap):
        plan_ref[PUSHED, s] = 0
        plan_ref[KEPT, s] = 0
        plan_ref[TOTALS, s] = 0
    for s in range(cap):
        row = meta_ref[1 + s]
        crosses = (row > 0).astype(jnp.int32)
        now = short * crosses if again else 1 - short * crosses
        taken = ((best >> s) & 1) * (short if again else 1 - short)
        kept = jnp.where(s < count, (1 - taken) * now, 0)
        plan_ref[ROW, s] = row
        plan_ref[COL, s] = meta_ref[1 + cap + s]
        plan_ref[AT_PUSH, s] = at_push
        plan_ref[AT_BACK, s] = at_back
        plan_ref[AT_PULL, s] = at_pull

        @pl.when(taken > 0)
        def _():
            plan_ref[PUSHED, n_pushed] = s

        @pl.when(kept > 0)
        def _():
            plan_ref[KEPT, n_kept] = s

        ahead = units - row // UNIT
        at_push += taken * (ahead + seen_units)
        at_back += taken * ahead
        at_pull += kept * ((row + UNIT - 1) // UNIT)
        n_pushed += taken
        n_kept += kept
    plan_ref[TOTALS, 0] = n_pushed
    plan_ref[TOTALS, 1] = n_kept
    plan_ref[TOTALS, 2] = short


def pack(plan_ref, slot, own_ref, buffer_ref, start, first_unit, last_unit):
    slices, planes, width, columns = own_ref.shape
    _, shift, here, there = place(plan_ref, slot, width, columns)
    first = lax.broadcasted_iota(jnp.int32, (UNIT, width), 1) >= shift

    def step(u, carry):
        rows = pl.ds(pl.multiple_of(u * UNIT, UNIT), UNIT)
        for l in range(slices):
            for p in range(planes):
                buffer_ref[start + u - first_unit, l * planes + p] = jnp.where(
                    first, own_ref[l, p, rows, here], own_ref[l, p, rows, there]
                )
        return carry

    lax.fori_loop(first_unit, last_unit, step, 0)


def push_kernel(meta_ref, own_in_ref, seen_hbm, plan_ref, push_ref, *refs, rooms, again):
    if again:
        own_ref = own_in_ref
        sems, = refs
    else:
        own_ref, left_ref, sem, sems = refs
        load = pltpu.make_async_copy(own_in_ref, own_ref, sem)
        load.start()
    width = own_ref.shape[2]
    units, seen_units = width // UNIT, seen_hbm.shape[1]
    make_plan(meta_ref, plan_ref, width, rooms, again)

    def seen(i):
        slot = plan_ref[PUSHED, i]
        start = plan_ref[AT_PUSH, slot] + units - plan_ref[ROW, slot] // UNIT
        return pltpu.make_async_copy(seen_hbm.at[slot], push_ref.at[pl.ds(start, seen_units)], sems.at[i])

    def begin(i, carry):
        seen(i).start()
        return carry

    def step(i, carry):
        slot = plan_ref[PUSHED, i]
        pack(plan_ref, slot, own_ref, push_ref, plan_ref[AT_PUSH, slot], plan_ref[ROW, slot] // UNIT, units)
        return carry

    def end(i, carry):
        seen(i).wait()
        return carry

    lax.fori_loop(0, plan_ref[TOTALS, 0], begin, 0)
    shape = (UNIT, width)
    index = lax.broadcasted_iota(jnp.int32, shape, 0) * width + lax.broadcasted_iota(jnp.int32, shape, 1)
    told = jnp.zeros(shape, jnp.float32)
    for r in range(plan_ref.shape[0]):
        for s in range(plan_ref.shape[1]):
            told = jnp.where(index == r * width + s, plan_ref[r, s].astype(jnp.float32), told)
    push_ref[push_ref.shape[0] - 1, 0] = told
    if not again:
        left_ref[...] = jnp.full(left_ref.shape, plan_ref[TOTALS, 2].astype(jnp.float32))
        load.wait()
    lax.fori_loop(0, plan_ref[TOTALS, 0], step, 0)
    lax.fori_loop(0, plan_ref[TOTALS, 0], end, 0)


def start_kernel(lefts_ref, plan_ref, grad_ref, left_ref):
    grad_ref[...] = jnp.zeros_like(grad_ref)
    left_ref[0] = jnp.sum(lefts_ref[...])


def pull_kernel(told_ref, own_ref, plan_ref, pull_ref, whole_ref, numbers_ref, sem):
    whole_ref[...] = told_ref[told_ref.shape[0] - 1, 0].astype(jnp.int32)
    copy = pltpu.make_async_copy(whole_ref, numbers_ref, sem)
    copy.start()
    copy.wait()
    for r in range(plan_ref.shape[0]):
        for s in range(plan_ref.shape[1]):
            plan_ref[r, s] = numbers_ref[r, s]

    def step(i, carry):
        slot = plan_ref[KEPT, i]
        end = (plan_ref[ROW, slot] + UNIT - 1) // UNIT
        pack(plan_ref, slot, own_ref, pull_ref, plan_ref[AT_PULL, slot], 0, end)
        return carry

    lax.fori_loop(0, plan_ref[TOTALS, 1], step, 0)


def grad_kernel(plan_ref, probe_ref, own_ref, came_ref, tables_ref, loss_in_ref, *refs, pushed):
    if pushed:
        grad_in_ref, grad_ref, back_ref, loss_ref, wave_ref, window_ref = refs
    else:
        grad_in_ref, seen_ref, grad_ref, back_ref, loss_ref, wave_ref, window_ref = refs
    grad_ref[...] = grad_in_ref[...]
    slices, planes, width, columns = own_ref.shape
    units = width // UNIT
    seen_units = width // (UNIT * UNIT)
    last = came_ref.shape[0] - 1
    row_iota = lax.broadcasted_iota(jnp.int32, (width, width), 0)
    lane_iota = lax.broadcasted_iota(jnp.int32, (width, width), 1)
    count = plan_ref[TOTALS, 0 if pushed else 1]

    def step(group, loss):
        slots, scales, measured = [], [], []
        for b in range(BATCH):
            live = group * BATCH + b < count
            slot = plan_ref[PUSHED if pushed else KEPT, jnp.where(live, group * BATCH + b, group * BATCH)]
            slots.append(slot)
            scales.append(live.astype(jnp.float32))
            row, shift, here, there = place(plan_ref, slot, width, columns)
            mine = row_iota < row if pushed else row_iota >= row
            first = lane_iota >= shift
            if pushed:
                start = plan_ref[AT_PUSH, slot] - row // UNIT
                seen = came_ref[pl.ds(jnp.minimum(start + units, last + 1 - seen_units), seen_units)]
                measured.append(seen.reshape(width, width))
            else:
                start = plan_ref[AT_PULL, slot]
                measured.append(seen_ref[slot])
            at = [jnp.clip(start + u, 0, last) for u in range(units)]
            for l in range(slices):
                for p in range(planes):
                    theirs = jnp.concatenate([came_ref[i, l * planes + p] for i in at], axis=0)
                    ours = jnp.where(first, own_ref[l, p, :, here], own_ref[l, p, :, there])
                    window_ref[b, l, p] = jnp.where(mine, ours, theirs)
            for p in range(planes):
                wave_ref[b, 0, p] = pltpu.roll(pltpu.roll(probe_ref[p], row, 0), shift, 1)
        loss = loss + field_grads(tables_ref, wave_ref, window_ref, measured, scales)
        for b in range(BATCH):
            row, shift, here, there = place(plan_ref, slots[b], width, columns)
            mine = row_iota < row if pushed else row_iota >= row
            first = lane_iota >= shift
            if pushed:
                start, begin, end = plan_ref[AT_BACK, slots[b]], row // UNIT, units
            else:
                start, begin, end = plan_ref[AT_PULL, slots[b]], 0, (row + UNIT - 1) // UNIT

            @pl.when(scales[b] > 0)
            def _(b=b, mine=mine, first=first, here=here, there=there, start=start, begin=begin, end=end):
                for l in range(slices):
                    for p in range(planes):
                        ours = jnp.where(mine, window_ref[b, l, p], 0.0)
                        grad_ref[l, p, :, here] += jnp.where(first, ours, 0.0)
                        grad_ref[l, p, :, there] += jnp.where(first, 0.0, ours)

                def unit(u, carry):
                    rows = pl.ds(pl.multiple_of(u * UNIT, UNIT), UNIT)
                    for l in range(slices):
                        for p in range(planes):
                            back_ref[start + u - begin, l * planes + p] = window_ref[b, l, p, rows, :]
                    return carry

                lax.fori_loop(begin, end, unit, 0)

        return loss

    loss_ref[0] = lax.fori_loop(0, (count + BATCH - 1) // BATCH, step, loss_in_ref[0])


def after_kernel(loss_ref, x_ref, first_ref, x_out_ref, losses_ref):
    losses_ref[...] = jnp.full(losses_ref.shape, loss_ref[0])


def add(plan, slot, grad_ref, layers, came, start, begin, end, below):
    planes, width, columns = grad_ref.shape[1:]
    row, shift, here, there = place(plan, slot, width, columns)
    first = lax.broadcasted_iota(jnp.int32, (UNIT, width), 1) >= shift
    row_iota = lax.broadcasted_iota(jnp.int32, (UNIT, width), 0)

    def unit(u, carry):
        rows = pl.ds(pl.multiple_of(u * UNIT, UNIT), UNIT)
        at = u * UNIT + row_iota
        mine = at < row if below else at >= row
        for l in layers:
            for p in range(planes):
                piece = jnp.where(mine, came[start + u - begin, l * planes + p], 0.0)
                grad_ref[l, p, rows, here] += jnp.where(first, piece, 0.0)
                grad_ref[l, p, rows, there] += jnp.where(first, 0.0, piece)
        return carry

    lax.fori_loop(begin, end, unit, 0)


def add_returned_kernel(plan_ref, returned_ref, grad_in_ref, grad_ref):
    slices, _, width, _ = grad_ref.shape
    grad_ref[...] = grad_in_ref[...]

    def step(i, carry):
        slot = plan_ref[PUSHED, i]
        at, low = plan_ref[AT_BACK, slot], plan_ref[ROW, slot] // UNIT
        add(plan_ref, slot, grad_ref, range(slices), returned_ref, at, low, width // UNIT, False)
        return carry

    lax.fori_loop(0, plan_ref[TOTALS, 0], step, 0)


def add_given(before_ref, given_ref, grad_ref, layers):
    def step(i, carry):
        slot = before_ref[KEPT, i]
        end = (before_ref[ROW, slot] + UNIT - 1) // UNIT
        add(before_ref, slot, grad_ref, layers, given_ref, before_ref[AT_PULL, slot], 0, end, True)
        return carry

    lax.fori_loop(0, before_ref[TOTALS, 1], step, 0)


def add_given_kernel(before_ref, given_ref, grad_in_ref, grad_ref):
    grad_ref[...] = grad_in_ref[...]
    add_given(before_ref, given_ref, grad_ref, range(grad_ref.shape[0]))


def finish_kernel(before_ref, given_ref, losses_ref, grad_in_ref, grad_hbm, loss_ref, grad_ref, sems):
    slices = grad_ref.shape[0]
    stores = [pltpu.make_async_copy(grad_ref.at[l], grad_hbm.at[l], sems.at[l]) for l in range(slices)]
    for l in range(slices):
        grad_ref[l] = grad_in_ref[l]
        add_given(before_ref, given_ref, grad_ref, [l])
        stores[l].start()
    lanes = lax.broadcasted_iota(jnp.int32, losses_ref.shape, 1)
    loss_ref[0] = jnp.sum(jnp.where(lanes == 0, losses_ref[...], 0.0))
    for store in stores:
        store.wait()


def shifted(x, axis, by):
    peers = lax.axis_size(axis)
    return lax.ppermute(x, axis, [(i, (i + by) % peers) for i in range(peers)])


def local(probe_wave, object_slices, intensities, row_offset, col_offset, counts):
    width = probe_wave.shape[-1]
    slices, planes = object_slices.shape[:2]
    cap = row_offset.shape[0]
    peers = lax.axis_size("tile")
    units, seen_units = width // UNIT, width // (UNIT * UNIT)
    tables = jnp.asarray(make_tables(width))
    meta = jnp.concatenate([counts, row_offset, col_offset])
    seen = intensities.reshape(cap, seen_units, UNIT, UNIT, width)
    rooms = sizes(cap, width)
    smem = pl.BlockSpec(memory_space=pltpu.SMEM)
    vmem = pl.BlockSpec(memory_space=pltpu.VMEM)
    anywhere = pl.BlockSpec(memory_space=pl.ANY)
    f32 = jnp.float32

    def shape(dims, dtype=f32):
        return jax.ShapeDtypeStruct(dims, dtype)

    def packed(n):
        return shape((n, slices * planes, UNIT, width))

    def call(kernel, name, cost, ins, in_specs, outs, out_specs, scratch=(), mib=16, aliases=None):
        return pl.pallas_call(
            kernel,
            out_shape=outs,
            in_specs=in_specs,
            out_specs=out_specs,
            scratch_shapes=scratch,
            input_output_aliases=aliases or {},
            compiler_params=pltpu.CompilerParams(vmem_limit_bytes=mib << 20),
            cost_estimate=pl.CostEstimate(flops=int(cost * 1e9), bytes_accessed=int(cost * 1e6), transcendentals=0),
            name=name,
        )(*ins)

    def held(like):
        return pltpu.VMEM(like.shape, like.dtype)

    strip = shape(object_slices.shape)
    plan_shape = shape((8, cap), jnp.int32)
    rows = shape((peers, width))
    one = shape((1,))
    dma = pltpu.SemaphoreType.DMA

    def ahead(source, again):
        kernel = functools.partial(push_kernel, rooms=rooms, again=again)
        ins, outs = (meta, source, seen), (plan_shape, held(packed(rooms[again][0] + 1)))
        if again:
            return call(kernel, "pack_more", 4, ins, [smem, vmem, anywhere], outs, (smem, vmem), [dma((cap,))])
        return call(
            kernel, "pack_pushed", 4, (meta,) + tuple(pltpu.with_memory_space_constraint(x, pltpu.HBM) for x in (source, seen)),
            [smem, anywhere, anywhere], outs + (held(strip), rows), (smem, vmem, vmem, vmem), [dma, dma((cap,))],
        )

    def behind(pushed, own, again):
        scratch = [pltpu.VMEM((UNIT, width), jnp.int32), pltpu.SMEM((UNIT, width), jnp.int32), dma]
        outs = (plan_shape, held(packed(rooms[again][2])))
        return call(pull_kernel, "pack_pulled", 2, (pushed, own), [vmem, vmem], outs, (smem, vmem), scratch)

    def grads(plan, own, came, loss, grad, back, is_pushed):
        name, more = ("grads_pushed", ()) if is_pushed else ("grads_kept", (intensities,))
        buffer = pltpu.VMEM((BATCH, slices, planes, width, width), f32)
        return call(
            functools.partial(grad_kernel, pushed=is_pushed), name, 10,
            (plan, probe_wave, own, came, tables, loss, grad) + more,
            [smem] + [vmem] * 4 + [smem, vmem] + [vmem] * len(more),
            (held(strip), held(packed(back)), one), (vmem, vmem, smem), [buffer, buffer], 24, {6: 0},
        )

    def add_returned(plan, returned, grad):
        return call(
            add_returned_kernel, "add_returned", 1, (plan, returned, grad), [smem, vmem, vmem], held(strip), vmem, aliases={2: 0}
        )

    plan, push, own, left = ahead(object_slices, False)
    pushed = shifted(push, "tile", 1)
    lefts = lax.all_to_all(left, "tile", 0, 0, tiled=True)
    before, pull = behind(pushed, own, False)
    pulled = shifted(pull, "tile", -1)
    grad, left = call(start_kernel, "start", 1, (lefts, before), [vmem, smem], (held(strip), one), (vmem, smem))

    def unfinished(carry):
        return carry[2][0] > 0

    def second(carry):
        grad, loss, _ = carry
        plan, push = ahead(own, True)
        pushed = shifted(push, "tile", 1)
        before, pull = behind(pushed, own, True)
        pulled = shifted(pull, "tile", -1)
        grad, back, loss = grads(before, own, pushed, loss, grad, rooms[1][1], True)
        returned = shifted(back, "tile", -1)
        grad, back, loss = grads(plan, own, pulled, loss, grad, rooms[1][2], False)
        given = shifted(back, "tile", 1)
        grad = add_returned(plan, returned, grad)
        grad = call(add_given_kernel, "add_given", 1, (before, given, grad), [smem, vmem, vmem], held(strip), vmem, aliases={2: 0})
        return grad, loss, jnp.zeros_like(left)

    grad, loss, _ = lax.while_loop(unfinished, second, (grad, jnp.zeros((1,), f32), left))
    grad, back, loss = grads(before, own, pushed, loss, grad, rooms[0][1], True)
    returned = shifted(back, "tile", -1)
    grad, back, loss = grads(plan, own, pulled, loss, grad, rooms[0][2], False)
    back, losses = call(
        after_kernel, "after_returned", 1, (loss, back, returned), [smem, anywhere, anywhere],
        (held(back), rows), (anywhere, vmem), aliases={1: 0},
    )
    given = shifted(back, "tile", 1)
    losses = lax.all_to_all(losses, "tile", 0, 0, tiled=True)
    grad = add_returned(plan, returned, grad)
    return call(
        finish_kernel, "add_given", 4, (before, given, losses, grad), [smem, vmem, vmem, vmem],
        (strip, one), (anywhere, smem), [pltpu.VMEM(strip.shape, f32), dma((slices,))],
    )


def solution(mesh):
    placed = (
        P(),
        P("parts", None, "tile", None),
        P(("parts", "tile"), None, None),
        P(("parts", "tile")),
        P(("parts", "tile")),
        P(("parts", "tile")),
    )
    return jax.shard_map(
        local,
        mesh=mesh,
        in_specs=placed,
        out_specs=(P("parts", None, "tile", None), P("parts")),
        check_vma=False,
    )
```

```python
import functools

import jax
import jax.numpy as jnp
import ml_dtypes
import numpy as np
from jax import lax
from jax.experimental import pallas as pl
from jax.experimental.pallas import tpu as pltpu
from jax.sharding import PartitionSpec as P

BATCH = 4
UNIT = 8
ROW, COL, AT_PUSH, AT_BACK, AT_PULL, PUSHED, KEPT, TOTALS = range(8)


def make_tables(width):
    indices = np.arange(width)
    dft = np.exp(-2j * np.pi * (np.outer(indices, indices) % width) / width) / np.sqrt(width)
    freqs = np.where(indices < width // 2, indices, indices - width).astype(np.float64)
    along = np.conj(dft) @ (np.exp(-0.0015j * freqs**2)[:, None] * dft)
    out = []
    for matrix in (along, dft):
        left = np.block([[matrix.real, -matrix.imag], [matrix.imag, matrix.real]])
        forms = []
        for form in (left, left.T):
            form = form.astype(np.float32)
            high = form.astype(ml_dtypes.bfloat16)
            low = (form - high.astype(np.float32)).astype(ml_dtypes.bfloat16)
            forms.append(np.stack([high, low]))
        out.append(np.stack(forms))
    return np.stack(out)


def split(x):
    high = x.astype(jnp.bfloat16)
    return high, (x - high.astype(jnp.float32)).astype(jnp.bfloat16)


def dot(a, b):
    return jnp.dot(a, b, preferred_element_type=jnp.float32)


def one_sided(tables, which, form, re, im):
    width = re.shape[0]
    high, low = split(jnp.concatenate([re, im], axis=1))
    m_high, m_low = tables[which, form, 0], tables[which, form, 1]
    out = dot(high, m_high) + (dot(high, m_low) + dot(low, m_high))
    return out[:, :width], out[:, width:]


def two_sided(tables, which, conj, re, im):
    form = 0 if conj else 1
    half = [one_sided(tables, which, form, a, b) for a, b in zip(re, im)]
    full = [one_sided(tables, which, form, a.T, b.T) for a, b in half]
    return [a.T for a, _ in full], [b.T for _, b in full]


def field_grads(tables, wave_ref, window_ref, measured, scales):
    batch, slices = wave_ref.shape[:2]
    for layer in range(slices):
        re, im = [], []
        for b in range(batch):
            w_re, w_im = wave_ref[b, layer, 0], wave_ref[b, layer, 1]
            t_re, t_im = window_ref[b, layer, 0], window_ref[b, layer, 1]
            re.append(w_re * t_re - w_im * t_im)
            im.append(w_re * t_im + w_im * t_re)
        if layer + 1 < slices:
            re, im = two_sided(tables, 0, False, re, im)
            for b in range(batch):
                wave_ref[b, layer + 1, 0] = re[b]
                wave_ref[b, layer + 1, 1] = im[b]
    re, im = two_sided(tables, 1, False, re, im)
    loss = 0.0
    back_re, back_im = [], []
    for b in range(batch):
        misfit = re[b] * re[b] + im[b] * im[b] - measured[b]
        loss = loss + scales[b] * (0.25 * jnp.sum(misfit * misfit))
        back_re.append(misfit * re[b])
        back_im.append(misfit * im[b])
    re, im = two_sided(tables, 1, True, back_re, back_im)
    for layer in reversed(range(slices)):
        upper_re, upper_im = [], []
        for b in range(batch):
            w_re, w_im = wave_ref[b, layer, 0], wave_ref[b, layer, 1]
            t_re, t_im = window_ref[b, layer, 0], window_ref[b, layer, 1]
            window_ref[b, layer, 0] = re[b] * w_re + im[b] * w_im
            window_ref[b, layer, 1] = im[b] * w_re - re[b] * w_im
            upper_re.append(re[b] * t_re + im[b] * t_im)
            upper_im.append(im[b] * t_re - re[b] * t_im)
        if layer > 0:
            re, im = two_sided(tables, 0, True, upper_re, upper_im)
    return loss


def place(plan_ref, slot, width, columns):
    row, col = plan_ref[ROW, slot], plan_ref[COL, slot]
    tile = col // width
    here = pl.ds(pl.multiple_of(tile * width, width), width)
    after = jnp.minimum(tile + 1, columns // width - 1)
    there = pl.ds(pl.multiple_of(after * width, width), width)
    return row, col - tile * width, here, there


def sizes(cap, width):
    whole = cap * width // UNIT
    first = (whole * 9 // 32, whole * 27 // 128, whole * 33 // 128)
    return first, (whole * 5 // 16, whole // 4, whole * 5 // 16)


def make_plan(meta_ref, plan_ref, width, rooms, again):
    cap = plan_ref.shape[1]
    units = width // UNIT
    seen_units = width // (UNIT * UNIT)
    shape = (UNIT, 128)
    choice = lax.broadcasted_iota(jnp.int32, shape, 0) * 128 + lax.broadcasted_iota(jnp.int32, shape, 1)
    zero = jnp.zeros(shape, jnp.int32)
    push, back, pull, n_push, bad = zero, zero, zero, zero, (choice >= (1 << cap)).astype(jnp.int32)
    count = meta_ref[0]
    for s in range(cap):
        row = meta_ref[1 + s]
        crosses = jnp.logical_and(s < count, row > 0).astype(jnp.int32)
        taken = (choice >> s) & 1
        ahead = units - row // UNIT
        push += taken * (ahead + seen_units)
        back += taken * ahead
        pull += (1 - taken) * (crosses * ((row + UNIT - 1) // UNIT))
        n_push += taken
        bad += taken * (1 - crosses)
    n_keep = count - n_push
    groups = (n_push + BATCH - 1) // BATCH + (n_keep + BATCH - 1) // BATCH
    worst = 16 * cap

    def best_of(room):
        over = bad + (push > room[0]).astype(jnp.int32) + (back > room[1]).astype(jnp.int32) + (pull > room[2]).astype(jnp.int32)
        score = (groups * 16 + n_keep + worst * (over > 0).astype(jnp.int32)) * (1 << cap) + choice
        return jnp.min(score.astype(jnp.float32)).astype(jnp.int32)

    best = best_of(rooms[0])
    short = (best >= worst << cap).astype(jnp.int32)
    if again:
        best = best_of(rooms[1])
    at_push = at_back = at_pull = n_pushed = n_kept = jnp.int32(0)
    for s in range(cap):
        plan_ref[PUSHED, s] = 0
        plan_ref[KEPT, s] = 0
        plan_ref[TOTALS, s] = 0
    for s in range(cap):
        row = meta_ref[1 + s]
        crosses = (row > 0).astype(jnp.int32)
        now = short * crosses if again else 1 - short * crosses
        taken = ((best >> s) & 1) * (short if again else 1 - short)
        kept = jnp.where(s < count, (1 - taken) * now, 0)
        plan_ref[ROW, s] = row
        plan_ref[COL, s] = meta_ref[1 + cap + s]
        plan_ref[AT_PUSH, s] = at_push
        plan_ref[AT_BACK, s] = at_back
        plan_ref[AT_PULL, s] = at_pull

        @pl.when(taken > 0)
        def _():
            plan_ref[PUSHED, n_pushed] = s

        @pl.when(kept > 0)
        def _():
            plan_ref[KEPT, n_kept] = s

        ahead = units - row // UNIT
        at_push += taken * (ahead + seen_units)
        at_back += taken * ahead
        at_pull += kept * ((row + UNIT - 1) // UNIT)
        n_pushed += taken
        n_kept += kept
    plan_ref[TOTALS, 0] = n_pushed
    plan_ref[TOTALS, 1] = n_kept
    plan_ref[TOTALS, 2] = short


def pack(plan_ref, slot, own_ref, buffer_ref, start, first_unit, last_unit):
    slices, planes, width, columns = own_ref.shape
    _, shift, here, there = place(plan_ref, slot, width, columns)
    first = lax.broadcasted_iota(jnp.int32, (UNIT, width), 1) >= shift

    def step(u, carry):
        rows = pl.ds(pl.multiple_of(u * UNIT, UNIT), UNIT)
        for l in range(slices):
            for p in range(planes):
                buffer_ref[start + u - first_unit, l * planes + p] = jnp.where(
                    first, own_ref[l, p, rows, here], own_ref[l, p, rows, there]
                )
        return carry

    lax.fori_loop(first_unit, last_unit, step, 0)


def push_kernel(meta_ref, own_in_ref, seen_hbm, plan_ref, push_ref, *refs, rooms, again):
    if again:
        own_ref = own_in_ref
        sems, = refs
    else:
        own_ref, sem, sems = refs
        load = pltpu.make_async_copy(own_in_ref, own_ref, sem)
        load.start()
    width = own_ref.shape[2]
    units, seen_units = width // UNIT, seen_hbm.shape[1]
    make_plan(meta_ref, plan_ref, width, rooms, again)

    def seen(i):
        slot = plan_ref[PUSHED, i]
        start = plan_ref[AT_PUSH, slot] + units - plan_ref[ROW, slot] // UNIT
        return pltpu.make_async_copy(seen_hbm.at[slot], push_ref.at[pl.ds(start, seen_units)], sems.at[i])

    def begin(i, carry):
        seen(i).start()
        return carry

    def step(i, carry):
        slot = plan_ref[PUSHED, i]
        pack(plan_ref, slot, own_ref, push_ref, plan_ref[AT_PUSH, slot], plan_ref[ROW, slot] // UNIT, units)
        return carry

    def end(i, carry):
        seen(i).wait()
        return carry

    lax.fori_loop(0, plan_ref[TOTALS, 0], begin, 0)
    shape = (UNIT, width)
    index = lax.broadcasted_iota(jnp.int32, shape, 0) * width + lax.broadcasted_iota(jnp.int32, shape, 1)
    told = jnp.zeros(shape, jnp.float32)
    for r in range(plan_ref.shape[0]):
        for s in range(plan_ref.shape[1]):
            told = jnp.where(index == r * width + s, plan_ref[r, s].astype(jnp.float32), told)
    push_ref[push_ref.shape[0] - 1, 0] = told
    if not again:
        load.wait()
    lax.fori_loop(0, plan_ref[TOTALS, 0], step, 0)
    lax.fori_loop(0, plan_ref[TOTALS, 0], end, 0)


def pull_kernel(told_ref, own_ref, plan_ref, pull_ref, whole_ref, numbers_ref, sem):
    whole_ref[...] = told_ref[told_ref.shape[0] - 1, 0].astype(jnp.int32)
    copy = pltpu.make_async_copy(whole_ref, numbers_ref, sem)
    copy.start()
    copy.wait()
    for r in range(plan_ref.shape[0]):
        for s in range(plan_ref.shape[1]):
            plan_ref[r, s] = numbers_ref[r, s]

    def step(i, carry):
        slot = plan_ref[KEPT, i]
        end = (plan_ref[ROW, slot] + UNIT - 1) // UNIT
        pack(plan_ref, slot, own_ref, pull_ref, plan_ref[AT_PULL, slot], 0, end)
        return carry

    lax.fori_loop(0, plan_ref[TOTALS, 1], step, 0)


def grad_kernel(plan_ref, probe_ref, own_ref, came_ref, tables_ref, *refs, pushed):
    if pushed:
        grad_ref, back_ref, loss_ref, wave_ref, window_ref = refs
        grad_ref[...] = jnp.zeros_like(grad_ref)
        before = jnp.float32(0.0)
    else:
        loss_in_ref, grad_in_ref, seen_ref, grad_ref, back_ref, loss_ref, wave_ref, window_ref = refs
        grad_ref[...] = grad_in_ref[...]
        before = loss_in_ref[0]
    slices, planes, width, columns = own_ref.shape
    units = width // UNIT
    seen_units = width // (UNIT * UNIT)
    last = came_ref.shape[0] - 1
    row_iota = lax.broadcasted_iota(jnp.int32, (width, width), 0)
    lane_iota = lax.broadcasted_iota(jnp.int32, (width, width), 1)
    count = plan_ref[TOTALS, 0 if pushed else 1]

    def step(group, loss):
        slots, scales, measured = [], [], []
        for b in range(BATCH):
            live = group * BATCH + b < count
            slot = plan_ref[PUSHED if pushed else KEPT, jnp.where(live, group * BATCH + b, group * BATCH)]
            slots.append(slot)
            scales.append(live.astype(jnp.float32))
            row, shift, here, there = place(plan_ref, slot, width, columns)
            mine = row_iota < row if pushed else row_iota >= row
            first = lane_iota >= shift
            if pushed:
                start = plan_ref[AT_PUSH, slot] - row // UNIT
                seen = came_ref[pl.ds(jnp.minimum(start + units, last + 1 - seen_units), seen_units)]
                measured.append(seen.reshape(width, width))
            else:
                start = plan_ref[AT_PULL, slot]
                measured.append(seen_ref[slot])
            at = [jnp.clip(start + u, 0, last) for u in range(units)]
            for l in range(slices):
                for p in range(planes):
                    theirs = jnp.concatenate([came_ref[i, l * planes + p] for i in at], axis=0)
                    ours = jnp.where(first, own_ref[l, p, :, here], own_ref[l, p, :, there])
                    window_ref[b, l, p] = jnp.where(mine, ours, theirs)
            for p in range(planes):
                wave_ref[b, 0, p] = pltpu.roll(pltpu.roll(probe_ref[p], row, 0), shift, 1)
        loss = loss + field_grads(tables_ref, wave_ref, window_ref, measured, scales)
        for b in range(BATCH):
            row, shift, here, there = place(plan_ref, slots[b], width, columns)
            mine = row_iota < row if pushed else row_iota >= row
            first = lane_iota >= shift
            if pushed:
                start, begin, end = plan_ref[AT_BACK, slots[b]], row // UNIT, units
            else:
                start, begin, end = plan_ref[AT_PULL, slots[b]], 0, (row + UNIT - 1) // UNIT

            @pl.when(scales[b] > 0)
            def _(b=b, mine=mine, first=first, here=here, there=there, start=start, begin=begin, end=end):
                for l in range(slices):
                    for p in range(planes):
                        ours = jnp.where(mine, window_ref[b, l, p], 0.0)
                        grad_ref[l, p, :, here] += jnp.where(first, ours, 0.0)
                        grad_ref[l, p, :, there] += jnp.where(first, 0.0, ours)

                def unit(u, carry):
                    rows = pl.ds(pl.multiple_of(u * UNIT, UNIT), UNIT)
                    for l in range(slices):
                        for p in range(planes):
                            back_ref[start + u - begin, l * planes + p] = window_ref[b, l, p, rows, :]
                    return carry

                lax.fori_loop(begin, end, unit, 0)

        return loss

    loss_ref[0] = lax.fori_loop(0, (count + BATCH - 1) // BATCH, step, before)
    loss_ref[1] = plan_ref[TOTALS, 2].astype(jnp.float32)


def after_kernel(x_ref, *refs):
    pass


def after_last_kernel(x_ref, last_ref, out_ref):
    for i in range(out_ref.shape[0]):
        out_ref[i] = x_ref[i]


def add(plan, slot, grad_ref, layers, came, start, begin, end, below):
    planes, width, columns = grad_ref.shape[1:]
    row, shift, here, there = place(plan, slot, width, columns)
    first = lax.broadcasted_iota(jnp.int32, (UNIT, width), 1) >= shift
    row_iota = lax.broadcasted_iota(jnp.int32, (UNIT, width), 0)

    def unit(u, carry):
        rows = pl.ds(pl.multiple_of(u * UNIT, UNIT), UNIT)
        at = u * UNIT + row_iota
        mine = at < row if below else at >= row
        for l in layers:
            for p in range(planes):
                piece = jnp.where(mine, came[start + u - begin, l * planes + p], 0.0)
                grad_ref[l, p, rows, here] += jnp.where(first, piece, 0.0)
                grad_ref[l, p, rows, there] += jnp.where(first, 0.0, piece)
        return carry

    lax.fori_loop(begin, end, unit, 0)


def add_returned_kernel(plan_ref, returned_ref, grad_in_ref, grad_ref):
    slices, _, width, _ = grad_ref.shape
    grad_ref[...] = grad_in_ref[...]

    def step(i, carry):
        slot = plan_ref[PUSHED, i]
        at, low = plan_ref[AT_BACK, slot], plan_ref[ROW, slot] // UNIT
        add(plan_ref, slot, grad_ref, range(slices), returned_ref, at, low, width // UNIT, False)
        return carry

    lax.fori_loop(0, plan_ref[TOTALS, 0], step, 0)


def add_given(before_ref, given_ref, grad_ref, layers):
    def step(i, carry):
        slot = before_ref[KEPT, i]
        end = (before_ref[ROW, slot] + UNIT - 1) // UNIT
        add(before_ref, slot, grad_ref, layers, given_ref, before_ref[AT_PULL, slot], 0, end, True)
        return carry

    lax.fori_loop(0, before_ref[TOTALS, 1], step, 0)


def finish_kernel(before_ref, given_ref, grad_in_ref, grad_hbm, grad_ref, sems):
    slices = grad_ref.shape[0]
    stores = [pltpu.make_async_copy(grad_ref.at[l], grad_hbm.at[l], sems.at[l]) for l in range(slices)]
    for l in range(slices):
        grad_ref[l] = grad_in_ref[l]
        add_given(before_ref, given_ref, grad_ref, [l])
        stores[l].start()
    for store in stores:
        store.wait()


def merge_kernel(more_ref, base_hbm, sum_hbm, work_ref, sem):
    for l in range(work_ref.shape[0]):
        load = pltpu.make_async_copy(base_hbm.at[l], work_ref.at[l], sem)
        load.start()
        load.wait()
        work_ref[l] += more_ref[l]
        store = pltpu.make_async_copy(work_ref.at[l], sum_hbm.at[l], sem)
        store.start()
        store.wait()


def shifted(x, axis, by):
    peers = lax.axis_size(axis)
    return lax.ppermute(x, axis, [(i, (i + by) % peers) for i in range(peers)])


def total_stages(peers):
    stages, step = [], 1
    while step < peers:
        radix = 4 if step * 4 <= peers else 2
        stages.append((step, radix))
        step *= radix
    return stages


def partial_total(x, axis, stage):
    peers = lax.axis_size(axis)
    step, radix = stage

    def other(by):
        return lax.ppermute(x, axis, [(i, i ^ by) for i in range(peers)])

    if radix == 2:
        return x + other(step)
    return (x + other(step)) + (other(2 * step) + other(3 * step))


def local(probe_wave, object_slices, intensities, row_offset, col_offset, counts):
    width = probe_wave.shape[-1]
    slices, planes = object_slices.shape[:2]
    cap = row_offset.shape[0]
    peers = lax.axis_size("tile")
    units, seen_units = width // UNIT, width // (UNIT * UNIT)
    tables = jnp.asarray(make_tables(width))
    meta = jnp.concatenate([counts, row_offset, col_offset])
    seen = intensities.reshape(cap, seen_units, UNIT, UNIT, width)
    rooms = sizes(cap, width)
    smem = pl.BlockSpec(memory_space=pltpu.SMEM)
    vmem = pl.BlockSpec(memory_space=pltpu.VMEM)
    anywhere = pl.BlockSpec(memory_space=pl.ANY)
    f32 = jnp.float32

    def shape(dims, dtype=f32):
        return jax.ShapeDtypeStruct(dims, dtype)

    def packed(n):
        return shape((n, slices * planes, UNIT, width))

    def call(kernel, name, cost, ins, in_specs, outs, out_specs, scratch=(), mib=16, aliases=None):
        return pl.pallas_call(
            kernel,
            out_shape=outs,
            in_specs=in_specs,
            out_specs=out_specs,
            scratch_shapes=scratch,
            input_output_aliases=aliases or {},
            compiler_params=pltpu.CompilerParams(vmem_limit_bytes=mib << 20),
            cost_estimate=pl.CostEstimate(flops=int(cost * 1e9), bytes_accessed=int(cost * 1e6), transcendentals=0),
            name=name,
        )(*ins)

    def held(like):
        return pltpu.VMEM(like.shape, like.dtype)

    strip, sums_shape = shape(object_slices.shape), shape((2,))
    plan_shape = shape((8, cap), jnp.int32)
    dma = pltpu.SemaphoreType.DMA

    def held(like):
        return pltpu.VMEM(like.shape, like.dtype)

    def ahead(meta, source, again):
        kernel = functools.partial(push_kernel, rooms=rooms, again=again)
        outs = (plan_shape, held(packed(rooms[again][0] + 1)))
        if again:
            return call(kernel, "pack_more", 4, (meta, source, seen), [smem, vmem, anywhere], outs, (smem, vmem), [dma((cap,))])
        far = [pltpu.with_memory_space_constraint(x, pltpu.HBM) for x in (source, seen)]
        return call(
            kernel, "pack_pushed", 4, (meta, *far), [smem, anywhere, anywhere], outs + (held(strip),), (smem, vmem, vmem),
            [dma, dma((cap,))],
        )

    def behind(pushed, own, again):
        scratch = [pltpu.VMEM((UNIT, width), jnp.int32), pltpu.SMEM((UNIT, width), jnp.int32), dma]
        outs = (plan_shape, held(packed(rooms[again][2])))
        return call(pull_kernel, "pack_pulled", 2, (pushed, own), [vmem, vmem], outs, (smem, vmem), scratch)

    def grads(plan, own, came, back, *kept):
        buffer = pltpu.VMEM((BATCH, slices, planes, width, width), f32)
        return call(
            functools.partial(grad_kernel, pushed=not kept), "grads_kept" if kept else "grads_pushed", 10,
            (plan, probe_wave, own, came, tables, *kept), [smem] + [vmem] * 4 + ([smem, vmem, vmem] if kept else []),
            (held(strip), held(packed(back)), sums_shape), (vmem, vmem, smem), [buffer, buffer], 24, {6: 0} if kept else {},
        )

    stages = total_stages(peers)

    def one_round(own, plan, push, again):
        pushed = shifted(push, "tile", 1)
        before, pull = behind(pushed, own, again)
        pulled = shifted(pull, "tile", -1)
        grad, back, sums = grads(before, own, pushed, rooms[again][1])
        returned = shifted(back, "tile", -1)
        grad, back, sums = grads(plan, own, pulled, rooms[again][2], sums, grad, intensities)
        sums = partial_total(sums, "tile", stages[0])
        back = call(
            after_kernel, "after_returned", 1, (back, returned, sums), [anywhere] * 3, held(back), anywhere, aliases={0: 0}
        )
        given = shifted(back, "tile", 1)
        grad = call(
            add_returned_kernel, "add_returned", 1, (plan, returned, grad), [smem, vmem, vmem], held(strip), vmem,
            aliases={2: 0},
        )
        sums = call(after_last_kernel, "after_given", 1, (sums, given), [smem, anywhere], sums_shape, smem)
        for stage in stages[1:]:
            sums = partial_total(sums, "tile", stage)
        grad = call(
            finish_kernel, "add_given", 4, (before, given, grad), [smem, vmem, vmem], pltpu.HBM(strip.shape, f32), anywhere,
            [pltpu.VMEM(strip.shape, f32), dma((slices,))],
        )
        return grad, sums

    def unfinished(carry):
        return carry[1][1] > 0

    def second(carry):
        grad, sums, meta = carry
        more, more_sums = one_round(own, *ahead(meta, own, True), True)
        grad = call(
            merge_kernel, "merge", 4, (more, pltpu.with_memory_space_constraint(grad, pltpu.HBM)), [vmem, anywhere],
            pltpu.HBM(strip.shape, f32), anywhere, [pltpu.VMEM(strip.shape, f32), dma], aliases={1: 0},
        )
        return grad, jnp.stack([sums[0] + more_sums[0], jnp.float32(0.0)]), jnp.zeros_like(meta)

    plan, push, own = ahead(meta, object_slices, False)
    grad, sums, _ = lax.while_loop(unfinished, second, (*one_round(own, plan, push, False), meta))
    return grad, sums[:1]


def solution(mesh):
    placed = (
        P(),
        P("parts", None, "tile", None),
        P(("parts", "tile"), None, None),
        P(("parts", "tile")),
        P(("parts", "tile")),
        P(("parts", "tile")),
    )
    return jax.shard_map(
        local,
        mesh=mesh,
        in_specs=placed,
        out_specs=(P("parts", None, "tile", None), P("parts")),
        check_vma=False,
    )
```

```python
import functools

import jax
import jax.numpy as jnp
import ml_dtypes
import numpy as np
from jax import lax
from jax.experimental import pallas as pl
from jax.experimental.pallas import tpu as pltpu
from jax.sharding import PartitionSpec as P

BATCH = 4
UNIT = 8
ROW, COL, AT_PUSH, AT_BACK, AT_PULL, PUSHED, KEPT, TOTALS = range(8)


def make_tables(width):
    indices = np.arange(width)
    dft = np.exp(-2j * np.pi * (np.outer(indices, indices) % width) / width) / np.sqrt(width)
    freqs = np.where(indices < width // 2, indices, indices - width).astype(np.float64)
    along = np.conj(dft) @ (np.exp(-0.0015j * freqs**2)[:, None] * dft)
    out = []
    for matrix in (along, dft):
        left = np.block([[matrix.real, -matrix.imag], [matrix.imag, matrix.real]])
        forms = []
        for form in (left, left.T):
            form = form.astype(np.float32)
            high = form.astype(ml_dtypes.bfloat16)
            low = (form - high.astype(np.float32)).astype(ml_dtypes.bfloat16)
            forms.append(np.stack([high, low]))
        out.append(np.stack(forms))
    return np.stack(out)


def split(x):
    high = x.astype(jnp.bfloat16)
    return high, (x - high.astype(jnp.float32)).astype(jnp.bfloat16)


def dot(a, b):
    return jnp.dot(a, b, preferred_element_type=jnp.float32)


def one_sided(tables, which, form, re, im):
    width = re.shape[0]
    high, low = split(jnp.concatenate([re, im], axis=1))
    m_high, m_low = tables[which, form, 0], tables[which, form, 1]
    out = dot(high, m_high) + (dot(high, m_low) + dot(low, m_high))
    return out[:, :width], out[:, width:]


def two_sided(tables, which, conj, re, im):
    form = 0 if conj else 1
    half = [one_sided(tables, which, form, a, b) for a, b in zip(re, im)]
    full = [one_sided(tables, which, form, a.T, b.T) for a, b in half]
    return [a.T for a, _ in full], [b.T for _, b in full]


def forward(tables, wave_ref, window_ref, field_ref, at, measured, scales):
    slices = wave_ref.shape[1]
    for layer in range(slices):
        re, im = [], []
        for b in at:
            w_re, w_im = wave_ref[b, layer, 0], wave_ref[b, layer, 1]
            t_re, t_im = window_ref[b, layer, 0], window_ref[b, layer, 1]
            re.append(w_re * t_re - w_im * t_im)
            im.append(w_re * t_im + w_im * t_re)
        if layer + 1 < slices:
            re, im = two_sided(tables, 0, False, re, im)
            for i, b in enumerate(at):
                wave_ref[b, layer + 1, 0] = re[i]
                wave_ref[b, layer + 1, 1] = im[i]
    re, im = two_sided(tables, 1, False, re, im)
    loss = 0.0
    for i, b in enumerate(at):
        misfit = re[i] * re[i] + im[i] * im[i] - measured[i]
        loss = loss + scales[i] * (0.25 * jnp.sum(misfit * misfit))
        field_ref[b, 0] = misfit * re[i]
        field_ref[b, 1] = misfit * im[i]
    return loss


def backward(tables, wave_ref, window_ref, field_ref, at, out_ref):
    slices = wave_ref.shape[1]
    re, im = two_sided(tables, 1, True, [field_ref[b, 0] for b in at], [field_ref[b, 1] for b in at])
    for layer in reversed(range(slices)):
        upper_re, upper_im = [], []
        for i, b in enumerate(at):
            w_re, w_im = wave_ref[b, layer, 0], wave_ref[b, layer, 1]
            t_re, t_im = window_ref[b, layer, 0], window_ref[b, layer, 1]
            out_ref[i, layer, 0] = re[i] * w_re + im[i] * w_im
            out_ref[i, layer, 1] = im[i] * w_re - re[i] * w_im
            upper_re.append(re[i] * t_re + im[i] * t_im)
            upper_im.append(im[i] * t_re - re[i] * t_im)
        if layer > 0:
            re, im = two_sided(tables, 0, True, upper_re, upper_im)


def place(plan_ref, slot, width, columns):
    row, col = plan_ref[ROW, slot], plan_ref[COL, slot]
    tile = col // width
    here = pl.ds(pl.multiple_of(tile * width, width), width)
    after = jnp.minimum(tile + 1, columns // width - 1)
    there = pl.ds(pl.multiple_of(after * width, width), width)
    return row, col - tile * width, here, there


def sizes(cap, width):
    whole = cap * width // UNIT
    first = (whole * 9 // 32, whole * 27 // 128, whole * 33 // 128)
    return first, (whole * 5 // 16, whole // 4, whole * 5 // 16)


def make_plan(meta_ref, plan_ref, width, rooms, again):
    cap = plan_ref.shape[1]
    units = width // UNIT
    seen_units = width // (UNIT * UNIT)
    shape = (UNIT, 128)
    choice = lax.broadcasted_iota(jnp.int32, shape, 0) * 128 + lax.broadcasted_iota(jnp.int32, shape, 1)
    zero = jnp.zeros(shape, jnp.int32)
    push, back, pull, n_push, bad = zero, zero, zero, zero, (choice >= (1 << cap)).astype(jnp.int32)
    count = meta_ref[0]
    for s in range(cap):
        row = meta_ref[1 + s]
        crosses = jnp.logical_and(s < count, row > 0).astype(jnp.int32)
        taken = (choice >> s) & 1
        ahead = units - row // UNIT
        push += taken * (ahead + seen_units)
        back += taken * ahead
        pull += (1 - taken) * (crosses * ((row + UNIT - 1) // UNIT))
        n_push += taken
        bad += taken * (1 - crosses)
    n_keep = count - n_push
    groups = (n_push + BATCH - 1) // BATCH + (n_keep + BATCH - 1) // BATCH
    worst = 16 * cap

    def best_of(room):
        over = bad + (push > room[0]).astype(jnp.int32) + (back > room[1]).astype(jnp.int32) + (pull > room[2]).astype(jnp.int32)
        score = (groups * 16 + n_keep + worst * (over > 0).astype(jnp.int32)) * (1 << cap) + choice
        return jnp.min(score.astype(jnp.float32)).astype(jnp.int32)

    best = best_of(rooms[0])
    short = (best >= worst << cap).astype(jnp.int32)
    if again:
        best = best_of(rooms[1])
    at_push = at_back = at_pull = n_pushed = n_kept = jnp.int32(0)
    for s in range(cap):
        plan_ref[PUSHED, s] = 0
        plan_ref[KEPT, s] = 0
        plan_ref[TOTALS, s] = 0
    for s in range(cap):
        row = meta_ref[1 + s]
        crosses = (row > 0).astype(jnp.int32)
        now = short * crosses if again else 1 - short * crosses
        taken = ((best >> s) & 1) * (short if again else 1 - short)
        kept = jnp.where(s < count, (1 - taken) * now, 0)
        plan_ref[ROW, s] = row
        plan_ref[COL, s] = meta_ref[1 + cap + s]
        plan_ref[AT_PUSH, s] = at_push
        plan_ref[AT_BACK, s] = at_back
        plan_ref[AT_PULL, s] = at_pull

        @pl.when(taken > 0)
        def _():
            plan_ref[PUSHED, n_pushed] = s

        @pl.when(kept > 0)
        def _():
            plan_ref[KEPT, n_kept] = s

        ahead = units - row // UNIT
        at_push += taken * (ahead + seen_units)
        at_back += taken * ahead
        at_pull += kept * ((row + UNIT - 1) // UNIT)
        n_pushed += taken
        n_kept += kept
    plan_ref[TOTALS, 0] = n_pushed
    plan_ref[TOTALS, 1] = n_kept
    plan_ref[TOTALS, 2] = short


def pack(plan_ref, slot, own_ref, buffer_ref, start, first_unit, last_unit):
    slices, planes, width, columns = own_ref.shape
    _, shift, here, there = place(plan_ref, slot, width, columns)
    first = lax.broadcasted_iota(jnp.int32, (UNIT, width), 1) >= shift

    def step(u, carry):
        rows = pl.ds(pl.multiple_of(u * UNIT, UNIT), UNIT)
        for l in range(slices):
            for p in range(planes):
                buffer_ref[start + u - first_unit, l * planes + p] = jnp.where(
                    first, own_ref[l, p, rows, here], own_ref[l, p, rows, there]
                )
        return carry

    lax.fori_loop(first_unit, last_unit, step, 0)


def push_kernel(meta_ref, own_in_ref, seen_hbm, plan_ref, push_ref, *refs, rooms, again):
    if again:
        own_ref = own_in_ref
        sems, = refs
    else:
        own_ref, sem, sems = refs
        load = pltpu.make_async_copy(own_in_ref, own_ref, sem)
        load.start()
    width = own_ref.shape[2]
    units, seen_units = width // UNIT, seen_hbm.shape[1]
    make_plan(meta_ref, plan_ref, width, rooms, again)

    def seen(i):
        slot = plan_ref[PUSHED, i]
        start = plan_ref[AT_PUSH, slot] + units - plan_ref[ROW, slot] // UNIT
        return pltpu.make_async_copy(seen_hbm.at[slot], push_ref.at[pl.ds(start, seen_units)], sems.at[i])

    def begin(i, carry):
        seen(i).start()
        return carry

    def step(i, carry):
        slot = plan_ref[PUSHED, i]
        pack(plan_ref, slot, own_ref, push_ref, plan_ref[AT_PUSH, slot], plan_ref[ROW, slot] // UNIT, units)
        return carry

    def end(i, carry):
        seen(i).wait()
        return carry

    lax.fori_loop(0, plan_ref[TOTALS, 0], begin, 0)
    shape = (UNIT, width)
    index = lax.broadcasted_iota(jnp.int32, shape, 0) * width + lax.broadcasted_iota(jnp.int32, shape, 1)
    told = jnp.zeros(shape, jnp.float32)
    for r in range(plan_ref.shape[0]):
        for s in range(plan_ref.shape[1]):
            told = jnp.where(index == r * width + s, plan_ref[r, s].astype(jnp.float32), told)
    push_ref[push_ref.shape[0] - 1, 0] = told
    if not again:
        load.wait()
    lax.fori_loop(0, plan_ref[TOTALS, 0], step, 0)
    lax.fori_loop(0, plan_ref[TOTALS, 0], end, 0)


def pull_kernel(told_ref, own_ref, plan_ref, pull_ref, whole_ref, numbers_ref, sem):
    whole_ref[...] = told_ref[told_ref.shape[0] - 1, 0].astype(jnp.int32)
    copy = pltpu.make_async_copy(whole_ref, numbers_ref, sem)
    copy.start()
    copy.wait()
    for r in range(plan_ref.shape[0]):
        for s in range(plan_ref.shape[1]):
            plan_ref[r, s] = numbers_ref[r, s]

    def step(i, carry):
        slot = plan_ref[KEPT, i]
        end = (plan_ref[ROW, slot] + UNIT - 1) // UNIT
        pack(plan_ref, slot, own_ref, pull_ref, plan_ref[AT_PULL, slot], 0, end)
        return carry

    lax.fori_loop(0, plan_ref[TOTALS, 1], step, 0)


def slot_of(plan_ref, group, b, pushed):
    count = plan_ref[TOTALS, 0 if pushed else 1]
    live = group * BATCH + b < count
    return plan_ref[PUSHED if pushed else KEPT, jnp.where(live, group * BATCH + b, group * BATCH)], live


def iotas(width):
    shape = (width, width)
    return lax.broadcasted_iota(jnp.int32, shape, 0), lax.broadcasted_iota(jnp.int32, shape, 1)


def begin_group(plan_ref, probe_ref, own_ref, came_ref, seen_ref, tables_ref, wave_ref, window_ref, field_ref, group, at, pushed):
    slices, planes, width, columns = own_ref.shape
    units = width // UNIT
    seen_units = width // (UNIT * UNIT)
    last = came_ref.shape[0] - 1
    row_iota, lane_iota = iotas(width)
    scales, measured = [], []
    for b in range(BATCH):
        slot, live = slot_of(plan_ref, group, b, pushed)
        scales.append(live.astype(jnp.float32))
        row, shift, here, there = place(plan_ref, slot, width, columns)
        mine = row_iota < row if pushed else row_iota >= row
        first = lane_iota >= shift
        if pushed:
            start = plan_ref[AT_PUSH, slot] - row // UNIT
            seen = came_ref[pl.ds(jnp.minimum(start + units, last + 1 - seen_units), seen_units)]
            measured.append(seen.reshape(width, width))
        else:
            start = plan_ref[AT_PULL, slot]
            measured.append(seen_ref[slot])
        units_at = [jnp.clip(start + u, 0, last) for u in range(units)]
        for l in range(slices):
            for p in range(planes):
                theirs = jnp.concatenate([came_ref[i, l * planes + p] for i in units_at], axis=0)
                ours = jnp.where(first, own_ref[l, p, :, here], own_ref[l, p, :, there])
                window_ref[at[b], l, p] = jnp.where(mine, ours, theirs)
        for p in range(planes):
            wave_ref[at[b], 0, p] = pltpu.roll(pltpu.roll(probe_ref[p], row, 0), shift, 1)
    return forward(tables_ref, wave_ref, window_ref, field_ref, at, measured, scales)


def end_group(plan_ref, tables_ref, wave_ref, window_ref, field_ref, out_ref, grad_ref, back_ref, group, at, pushed):
    slices, planes, width, columns = grad_ref.shape
    units = width // UNIT
    row_iota, lane_iota = iotas(width)
    backward(tables_ref, wave_ref, window_ref, field_ref, at, out_ref)
    for b in range(BATCH):
        slot, live = slot_of(plan_ref, group, b, pushed)
        row, shift, here, there = place(plan_ref, slot, width, columns)
        mine = row_iota < row if pushed else row_iota >= row
        first = lane_iota >= shift
        if pushed:
            start, begin, end = plan_ref[AT_BACK, slot], row // UNIT, units
        else:
            start, begin, end = plan_ref[AT_PULL, slot], 0, (row + UNIT - 1) // UNIT

        @pl.when(live)
        def _(b=b, mine=mine, first=first, here=here, there=there, start=start, begin=begin, end=end):
            for l in range(slices):
                for p in range(planes):
                    ours = jnp.where(mine, out_ref[b, l, p], 0.0)
                    grad_ref[l, p, :, here] += jnp.where(first, ours, 0.0)
                    grad_ref[l, p, :, there] += jnp.where(first, 0.0, ours)

            def unit(u, carry):
                rows = pl.ds(pl.multiple_of(u * UNIT, UNIT), UNIT)
                for l in range(slices):
                    for p in range(planes):
                        back_ref[start + u - begin, l * planes + p] = out_ref[b, l, p, rows, :]
                return carry

            lax.fori_loop(begin, end, unit, 0)


def pushed_kernel(plan_ref, probe_ref, own_ref, came_ref, tables_ref,
                  grad_ref, back_ref, sums_ref, wave_ref, window_ref, field_ref):
    grad_ref[...] = jnp.zeros_like(grad_ref)
    at = list(range(BATCH))

    def step(group, loss):
        loss = loss + begin_group(
            plan_ref, probe_ref, own_ref, came_ref, None, tables_ref, wave_ref, window_ref, field_ref, group, at, True
        )
        end_group(
            plan_ref, tables_ref, wave_ref, window_ref, field_ref, window_ref, grad_ref, back_ref, group, at, True
        )
        return loss

    groups = (plan_ref[TOTALS, 0] + BATCH - 1) // BATCH
    sums_ref[0] = lax.fori_loop(0, groups, step, jnp.float32(0.0))
    sums_ref[1] = jnp.float32(0.0)


def kept_forward_kernel(plan_ref, probe_ref, own_ref, came_ref, tables_ref, sums_in_ref, seen_ref,
                        wave_ref, window_ref, field_ref, sums_ref):
    def step(group, loss):
        at = [group * BATCH + b for b in range(BATCH)]
        return loss + begin_group(
            plan_ref, probe_ref, own_ref, came_ref, seen_ref, tables_ref, wave_ref, window_ref, field_ref, group, at, False
        )

    groups = (plan_ref[TOTALS, 1] + BATCH - 1) // BATCH
    sums_ref[0] = lax.fori_loop(0, groups, step, sums_in_ref[0])
    sums_ref[1] = plan_ref[TOTALS, 2].astype(jnp.float32)


def kept_backward_kernel(plan_ref, tables_ref, wave_ref, window_ref, field_ref, grad_in_ref, grad_ref, back_ref, out_ref):
    grad_ref[...] = grad_in_ref[...]

    def step(group, carry):
        at = [group * BATCH + b for b in range(BATCH)]
        end_group(plan_ref, tables_ref, wave_ref, window_ref, field_ref, out_ref, grad_ref, back_ref, group, at, False)
        return carry

    lax.fori_loop(0, (plan_ref[TOTALS, 1] + BATCH - 1) // BATCH, step, 0)


def after_kernel(x_ref, *refs):
    pass


def add(plan, slot, grad_ref, layers, came, start, begin, end, below):
    planes, width, columns = grad_ref.shape[1:]
    row, shift, here, there = place(plan, slot, width, columns)
    first = lax.broadcasted_iota(jnp.int32, (UNIT, width), 1) >= shift
    row_iota = lax.broadcasted_iota(jnp.int32, (UNIT, width), 0)

    def unit(u, carry):
        rows = pl.ds(pl.multiple_of(u * UNIT, UNIT), UNIT)
        at = u * UNIT + row_iota
        mine = at < row if below else at >= row
        for l in layers:
            for p in range(planes):
                piece = jnp.where(mine, came[start + u - begin, l * planes + p], 0.0)
                grad_ref[l, p, rows, here] += jnp.where(first, piece, 0.0)
                grad_ref[l, p, rows, there] += jnp.where(first, 0.0, piece)
        return carry

    lax.fori_loop(begin, end, unit, 0)


def add_returned_kernel(plan_ref, returned_ref, grad_in_ref, grad_ref):
    slices, _, width, _ = grad_ref.shape
    grad_ref[...] = grad_in_ref[...]

    def step(i, carry):
        slot = plan_ref[PUSHED, i]
        at, low = plan_ref[AT_BACK, slot], plan_ref[ROW, slot] // UNIT
        add(plan_ref, slot, grad_ref, range(slices), returned_ref, at, low, width // UNIT, False)
        return carry

    lax.fori_loop(0, plan_ref[TOTALS, 0], step, 0)


def add_given(before_ref, given_ref, grad_ref, layers):
    def step(i, carry):
        slot = before_ref[KEPT, i]
        end = (before_ref[ROW, slot] + UNIT - 1) // UNIT
        add(before_ref, slot, grad_ref, layers, given_ref, before_ref[AT_PULL, slot], 0, end, True)
        return carry

    lax.fori_loop(0, before_ref[TOTALS, 1], step, 0)


def finish_kernel(before_ref, given_ref, grad_in_ref, grad_hbm, grad_ref, sems):
    slices = grad_ref.shape[0]
    stores = [pltpu.make_async_copy(grad_ref.at[l], grad_hbm.at[l], sems.at[l]) for l in range(slices)]
    for l in range(slices):
        grad_ref[l] = grad_in_ref[l]
        add_given(before_ref, given_ref, grad_ref, [l])
        stores[l].start()
    for store in stores:
        store.wait()


def merge_kernel(more_ref, base_hbm, sum_hbm, work_ref, sem):
    for l in range(work_ref.shape[0]):
        load = pltpu.make_async_copy(base_hbm.at[l], work_ref.at[l], sem)
        load.start()
        load.wait()
        work_ref[l] += more_ref[l]
        store = pltpu.make_async_copy(work_ref.at[l], sum_hbm.at[l], sem)
        store.start()
        store.wait()


def shifted(x, axis, by):
    peers = lax.axis_size(axis)
    return lax.ppermute(x, axis, [(i, (i + by) % peers) for i in range(peers)])


def total_stages(peers):
    stages, step = [], 1
    while step < peers:
        radix = 4 if step * 4 <= peers else 2
        stages.append((step, radix))
        step *= radix
    return stages


def partial_total(x, axis, stage):
    peers = lax.axis_size(axis)
    step, radix = stage

    def other(by):
        return lax.ppermute(x, axis, [(i, i ^ by) for i in range(peers)])

    if radix == 2:
        return x + other(step)
    return (x + other(step)) + (other(2 * step) + other(3 * step))


def local(probe_wave, object_slices, intensities, row_offset, col_offset, counts):
    width = probe_wave.shape[-1]
    slices, planes = object_slices.shape[:2]
    cap = row_offset.shape[0]
    peers = lax.axis_size("tile")
    units, seen_units = width // UNIT, width // (UNIT * UNIT)
    tables = jnp.asarray(make_tables(width))
    meta = jnp.concatenate([counts, row_offset, col_offset])
    seen = intensities.reshape(cap, seen_units, UNIT, UNIT, width)
    rooms = sizes(cap, width)
    smem = pl.BlockSpec(memory_space=pltpu.SMEM)
    vmem = pl.BlockSpec(memory_space=pltpu.VMEM)
    anywhere = pl.BlockSpec(memory_space=pl.ANY)
    f32 = jnp.float32

    def shape(dims, dtype=f32):
        return jax.ShapeDtypeStruct(dims, dtype)

    def packed(n):
        return shape((n, slices * planes, UNIT, width))

    def call(kernel, name, cost, ins, in_specs, outs, out_specs, scratch=(), mib=16, aliases=None):
        return pl.pallas_call(
            kernel,
            out_shape=outs,
            in_specs=in_specs,
            out_specs=out_specs,
            scratch_shapes=scratch,
            input_output_aliases=aliases or {},
            compiler_params=pltpu.CompilerParams(vmem_limit_bytes=mib << 20),
            cost_estimate=pl.CostEstimate(flops=int(cost * 1e9), bytes_accessed=int(cost * 1e6), transcendentals=0),
            name=name,
        )(*ins)

    def held(like):
        return pltpu.VMEM(like.shape, like.dtype)

    strip, sums_shape = shape(object_slices.shape), shape((2,))
    plan_shape = shape((8, cap), jnp.int32)
    dma = pltpu.SemaphoreType.DMA

    def held(like):
        return pltpu.VMEM(like.shape, like.dtype)

    def ahead(meta, source, again):
        kernel = functools.partial(push_kernel, rooms=rooms, again=again)
        outs = (plan_shape, held(packed(rooms[again][0] + 1)))
        if again:
            return call(kernel, "pack_more", 4, (meta, source, seen), [smem, vmem, anywhere], outs, (smem, vmem), [dma((cap,))])
        far = [pltpu.with_memory_space_constraint(x, pltpu.HBM) for x in (source, seen)]
        return call(
            kernel, "pack_pushed", 4, (meta, *far), [smem, anywhere, anywhere], outs + (held(strip),), (smem, vmem, vmem),
            [dma, dma((cap,))],
        )

    def behind(pushed, own, again):
        scratch = [pltpu.VMEM((UNIT, width), jnp.int32), pltpu.SMEM((UNIT, width), jnp.int32), dma]
        outs = (plan_shape, held(packed(rooms[again][2])))
        return call(pull_kernel, "pack_pulled", 2, (pushed, own), [vmem, vmem], outs, (smem, vmem), scratch)

    def waves(n):
        return shape((n, slices, planes, width, width)), shape((n, planes, width, width))

    def grads_pushed(before, own, pushed, back):
        wave, field = (pltpu.VMEM(x.shape, f32) for x in waves(BATCH))
        return call(
            pushed_kernel, "grads_pushed", 10, (before, probe_wave, own, pushed, tables), [smem] + [vmem] * 4,
            (held(strip), held(packed(back)), sums_shape), (vmem, vmem, smem), [wave, wave, field], 24,
        )

    def waves_kept(plan, own, pulled, sums):
        wave, field = (held(x) for x in waves(-(-cap // BATCH) * BATCH))
        return call(
            kept_forward_kernel, "waves_kept", 5, (plan, probe_wave, own, pulled, tables, sums, intensities),
            [smem] + [vmem] * 4 + [smem, vmem], (wave, wave, field, sums_shape), (vmem, vmem, vmem, smem), mib=20,
        )

    def grads_kept(plan, wave, window, field, grad, back):
        return call(
            kept_backward_kernel, "grads_kept", 5, (plan, tables, wave, window, field, grad), [smem] + [vmem] * 5,
            (held(strip), held(packed(back))), (vmem, vmem), [pltpu.VMEM(waves(BATCH)[0].shape, f32)], 20, {5: 0},
        )

    stages = total_stages(peers)

    def one_round(own, plan, push, again):
        pushed = shifted(push, "tile", 1)
        before, pull = behind(pushed, own, again)
        pulled = shifted(pull, "tile", -1)
        grad, back, sums = grads_pushed(before, own, pushed, rooms[again][1])
        returned = shifted(back, "tile", -1)
        wave, window, field, sums = waves_kept(plan, own, pulled, sums)
        for stage in stages:
            sums = partial_total(sums, "tile", stage)
        grad, back = grads_kept(plan, wave, window, field, grad, rooms[again][2])
        back = call(
            after_kernel, "after_returned", 1, (back, returned, sums), [anywhere] * 3, held(back), anywhere, aliases={0: 0}
        )
        given = shifted(back, "tile", 1)
        grad = call(
            add_returned_kernel, "add_returned", 1, (plan, returned, grad), [smem, vmem, vmem], held(strip), vmem,
            aliases={2: 0},
        )
        grad = call(
            finish_kernel, "add_given", 4, (before, given, grad), [smem, vmem, vmem], pltpu.HBM(strip.shape, f32), anywhere,
            [pltpu.VMEM(strip.shape, f32), dma((slices,))],
        )
        return grad, sums

    def unfinished(carry):
        return carry[1] > 0

    def second(carry):
        grad, _, loss, meta = carry
        more, sums = one_round(own, *ahead(meta, own, True), True)
        grad = call(
            merge_kernel, "merge", 4, (more, pltpu.with_memory_space_constraint(grad, pltpu.HBM)), [vmem, anywhere],
            pltpu.HBM(strip.shape, f32), anywhere, [pltpu.VMEM(strip.shape, f32), dma], aliases={1: 0},
        )
        return grad, jnp.float32(0.0), loss + sums[:1], jnp.zeros_like(meta)

    plan, push, own = ahead(meta, object_slices, False)
    grad, sums = one_round(own, plan, push, False)
    grad, _, loss, _ = lax.while_loop(unfinished, second, (grad, sums[1], sums[:1], meta))
    return grad, loss


def solution(mesh):
    placed = (
        P(),
        P("parts", None, "tile", None),
        P(("parts", "tile"), None, None),
        P(("parts", "tile")),
        P(("parts", "tile")),
        P(("parts", "tile")),
    )
    return jax.shard_map(
        local,
        mesh=mesh,
        in_specs=placed,
        out_specs=(P("parts", None, "tile", None), P("parts")),
        check_vma=False,
    )
```

```python
import functools

import jax
import jax.numpy as jnp
import ml_dtypes
import numpy as np
from jax import lax
from jax.experimental import pallas as pl
from jax.experimental.pallas import tpu as pltpu
from jax.sharding import PartitionSpec as P

BATCH = 4
UNIT = 8
ROW, COL, AT_PUSH, AT_BACK, AT_PULL, PUSHED, KEPT, TOTALS = range(8)


def make_tables(width):
    indices = np.arange(width)
    dft = np.exp(-2j * np.pi * (np.outer(indices, indices) % width) / width) / np.sqrt(width)
    freqs = np.where(indices < width // 2, indices, indices - width).astype(np.float64)
    along = np.conj(dft) @ (np.exp(-0.0015j * freqs**2)[:, None] * dft)
    out = []
    for matrix in (along, dft):
        left = np.block([[matrix.real, -matrix.imag], [matrix.imag, matrix.real]])
        forms = []
        for form in (left, left.T):
            form = form.astype(np.float32)
            high = form.astype(ml_dtypes.bfloat16)
            low = (form - high.astype(np.float32)).astype(ml_dtypes.bfloat16)
            forms.append(np.stack([high, low]))
        out.append(np.stack(forms))
    return np.stack(out)


def split(x):
    high = x.astype(jnp.bfloat16)
    return high, (x - high.astype(jnp.float32)).astype(jnp.bfloat16)


def dot(a, b):
    return jnp.dot(a, b, preferred_element_type=jnp.float32)


def one_sided(tables, which, form, re, im):
    width = re.shape[0]
    high, low = split(jnp.concatenate([re, im], axis=1))
    m_high, m_low = tables[which, form, 0], tables[which, form, 1]
    out = dot(high, m_high) + (dot(high, m_low) + dot(low, m_high))
    return out[:, :width], out[:, width:]


def two_sided(tables, which, conj, re, im):
    form = 0 if conj else 1
    half = [one_sided(tables, which, form, a, b) for a, b in zip(re, im)]
    full = [one_sided(tables, which, form, a.T, b.T) for a, b in half]
    return [a.T for a, _ in full], [b.T for _, b in full]


def forward(tables, wave_ref, window_ref, field_ref, at, measured, scales):
    slices = wave_ref.shape[1]
    for layer in range(slices):
        re, im = [], []
        for b in at:
            w_re, w_im = wave_ref[b, layer, 0], wave_ref[b, layer, 1]
            t_re, t_im = window_ref[b, layer, 0], window_ref[b, layer, 1]
            re.append(w_re * t_re - w_im * t_im)
            im.append(w_re * t_im + w_im * t_re)
        if layer + 1 < slices:
            re, im = two_sided(tables, 0, False, re, im)
            for i, b in enumerate(at):
                wave_ref[b, layer + 1, 0] = re[i]
                wave_ref[b, layer + 1, 1] = im[i]
    re, im = two_sided(tables, 1, False, re, im)
    loss = 0.0
    for i, b in enumerate(at):
        misfit = re[i] * re[i] + im[i] * im[i] - measured[i]
        loss = loss + scales[i] * (0.25 * jnp.sum(misfit * misfit))
        field_ref[b, 0] = misfit * re[i]
        field_ref[b, 1] = misfit * im[i]
    return loss


def backward(tables, wave_ref, window_ref, field_ref, at, out_ref, out_at, layers, next_ref=None):
    top = wave_ref.shape[1] - 1
    re, im = [field_ref[b, 0] for b in at], [field_ref[b, 1] for b in at]
    if layers[0] == top:
        re, im = two_sided(tables, 1, True, re, im)
    for layer in layers:
        upper_re, upper_im = [], []
        for i, b in enumerate(at):
            w_re, w_im = wave_ref[b, layer, 0], wave_ref[b, layer, 1]
            t_re, t_im = window_ref[b, layer, 0], window_ref[b, layer, 1]
            out_ref[out_at[i], layer, 0] = re[i] * w_re + im[i] * w_im
            out_ref[out_at[i], layer, 1] = im[i] * w_re - re[i] * w_im
            upper_re.append(re[i] * t_re + im[i] * t_im)
            upper_im.append(im[i] * t_re - re[i] * t_im)
        if layer > 0:
            re, im = two_sided(tables, 0, True, upper_re, upper_im)
    if next_ref is not None:
        for i, b in enumerate(at):
            next_ref[b, 0] = re[i]
            next_ref[b, 1] = im[i]


def place(plan_ref, slot, width, columns):
    row, col = plan_ref[ROW, slot], plan_ref[COL, slot]
    tile = col // width
    here = pl.ds(pl.multiple_of(tile * width, width), width)
    after = jnp.minimum(tile + 1, columns // width - 1)
    there = pl.ds(pl.multiple_of(after * width, width), width)
    return row, col - tile * width, here, there


def sizes(cap, width):
    whole = cap * width // UNIT
    first = (whole * 9 // 32, whole * 27 // 128, whole * 33 // 128)
    return first, (whole * 5 // 16, whole // 4, whole * 5 // 16)


def make_plan(meta_ref, plan_ref, width, rooms, again):
    cap = plan_ref.shape[1]
    units = width // UNIT
    seen_units = width // (UNIT * UNIT)
    shape = (UNIT, 128)
    choice = lax.broadcasted_iota(jnp.int32, shape, 0) * 128 + lax.broadcasted_iota(jnp.int32, shape, 1)
    zero = jnp.zeros(shape, jnp.int32)
    push, back, pull, n_push, bad = zero, zero, zero, zero, (choice >= (1 << cap)).astype(jnp.int32)
    count = meta_ref[0]
    for s in range(cap):
        row = meta_ref[1 + s]
        crosses = jnp.logical_and(s < count, row > 0).astype(jnp.int32)
        taken = (choice >> s) & 1
        ahead = units - row // UNIT
        push += taken * (ahead + seen_units)
        back += taken * ahead
        pull += (1 - taken) * (crosses * ((row + UNIT - 1) // UNIT))
        n_push += taken
        bad += taken * (1 - crosses)
    n_keep = count - n_push
    groups = (n_push + BATCH - 1) // BATCH + (n_keep + BATCH - 1) // BATCH
    worst = 16 * cap

    def best_of(room):
        over = bad + (push > room[0]).astype(jnp.int32) + (back > room[1]).astype(jnp.int32) + (pull > room[2]).astype(jnp.int32)
        score = (groups * 16 + n_keep + worst * (over > 0).astype(jnp.int32)) * (1 << cap) + choice
        return jnp.min(score.astype(jnp.float32)).astype(jnp.int32)

    best = best_of(rooms[0])
    short = (best >= worst << cap).astype(jnp.int32)
    if again:
        best = best_of(rooms[1])
    at_push = at_back = at_pull = n_pushed = n_kept = jnp.int32(0)
    for s in range(cap):
        plan_ref[PUSHED, s] = 0
        plan_ref[KEPT, s] = 0
        plan_ref[TOTALS, s] = 0
    for s in range(cap):
        row = meta_ref[1 + s]
        crosses = (row > 0).astype(jnp.int32)
        now = short * crosses if again else 1 - short * crosses
        taken = ((best >> s) & 1) * (short if again else 1 - short)
        kept = jnp.where(s < count, (1 - taken) * now, 0)
        plan_ref[ROW, s] = row
        plan_ref[COL, s] = meta_ref[1 + cap + s]
        plan_ref[AT_PUSH, s] = at_push
        plan_ref[AT_BACK, s] = at_back
        plan_ref[AT_PULL, s] = at_pull

        @pl.when(taken > 0)
        def _():
            plan_ref[PUSHED, n_pushed] = s

        @pl.when(kept > 0)
        def _():
            plan_ref[KEPT, n_kept] = s

        ahead = units - row // UNIT
        at_push += taken * (ahead + seen_units)
        at_back += taken * ahead
        at_pull += kept * ((row + UNIT - 1) // UNIT)
        n_pushed += taken
        n_kept += kept
    plan_ref[TOTALS, 0] = n_pushed
    plan_ref[TOTALS, 1] = n_kept
    plan_ref[TOTALS, 2] = short


def pack(plan_ref, slot, own_ref, buffer_ref, start, first_unit, last_unit):
    slices, planes, width, columns = own_ref.shape
    _, shift, here, there = place(plan_ref, slot, width, columns)
    first = lax.broadcasted_iota(jnp.int32, (UNIT, width), 1) >= shift

    def step(u, carry):
        rows = pl.ds(pl.multiple_of(u * UNIT, UNIT), UNIT)
        for l in range(slices):
            for p in range(planes):
                buffer_ref[start + u - first_unit, l * planes + p] = jnp.where(
                    first, own_ref[l, p, rows, here], own_ref[l, p, rows, there]
                )
        return carry

    lax.fori_loop(first_unit, last_unit, step, 0)


def push_kernel(meta_ref, own_in_ref, seen_hbm, plan_ref, push_ref, *refs, rooms, again):
    if again:
        own_ref = own_in_ref
        sems, = refs
    else:
        own_ref, sem, sems = refs
        load = pltpu.make_async_copy(own_in_ref, own_ref, sem)
        load.start()
    width = own_ref.shape[2]
    units, seen_units = width // UNIT, seen_hbm.shape[1]
    make_plan(meta_ref, plan_ref, width, rooms, again)

    def seen(i):
        slot = plan_ref[PUSHED, i]
        start = plan_ref[AT_PUSH, slot] + units - plan_ref[ROW, slot] // UNIT
        return pltpu.make_async_copy(seen_hbm.at[slot], push_ref.at[pl.ds(start, seen_units)], sems.at[i])

    def begin(i, carry):
        seen(i).start()
        return carry

    def step(i, carry):
        slot = plan_ref[PUSHED, i]
        pack(plan_ref, slot, own_ref, push_ref, plan_ref[AT_PUSH, slot], plan_ref[ROW, slot] // UNIT, units)
        return carry

    def end(i, carry):
        seen(i).wait()
        return carry

    lax.fori_loop(0, plan_ref[TOTALS, 0], begin, 0)
    shape = (UNIT, width)
    index = lax.broadcasted_iota(jnp.int32, shape, 0) * width + lax.broadcasted_iota(jnp.int32, shape, 1)
    told = jnp.zeros(shape, jnp.float32)
    for r in range(plan_ref.shape[0]):
        for s in range(plan_ref.shape[1]):
            told = jnp.where(index == r * width + s, plan_ref[r, s].astype(jnp.float32), told)
    push_ref[push_ref.shape[0] - 1, 0] = told
    if not again:
        load.wait()
    lax.fori_loop(0, plan_ref[TOTALS, 0], step, 0)
    lax.fori_loop(0, plan_ref[TOTALS, 0], end, 0)


def pull_kernel(told_ref, own_ref, plan_ref, pull_ref, whole_ref, numbers_ref, sem):
    whole_ref[...] = told_ref[told_ref.shape[0] - 1, 0].astype(jnp.int32)
    copy = pltpu.make_async_copy(whole_ref, numbers_ref, sem)
    copy.start()
    copy.wait()
    for r in range(plan_ref.shape[0]):
        for s in range(plan_ref.shape[1]):
            plan_ref[r, s] = numbers_ref[r, s]

    def step(i, carry):
        slot = plan_ref[KEPT, i]
        end = (plan_ref[ROW, slot] + UNIT - 1) // UNIT
        pack(plan_ref, slot, own_ref, pull_ref, plan_ref[AT_PULL, slot], 0, end)
        return carry

    lax.fori_loop(0, plan_ref[TOTALS, 1], step, 0)


def slot_of(plan_ref, group, b, pushed):
    count = plan_ref[TOTALS, 0 if pushed else 1]
    live = group * BATCH + b < count
    return plan_ref[PUSHED if pushed else KEPT, jnp.where(live, group * BATCH + b, group * BATCH)], live


def iotas(width):
    shape = (width, width)
    return lax.broadcasted_iota(jnp.int32, shape, 0), lax.broadcasted_iota(jnp.int32, shape, 1)


def begin_group(plan_ref, probe_ref, own_ref, came_ref, seen_ref, tables_ref, wave_ref, window_ref, field_ref, group, at, pushed):
    slices, planes, width, columns = own_ref.shape
    units = width // UNIT
    seen_units = width // (UNIT * UNIT)
    last = came_ref.shape[0] - 1
    row_iota, lane_iota = iotas(width)
    scales, measured = [], []
    for b in range(BATCH):
        slot, live = slot_of(plan_ref, group, b, pushed)
        scales.append(live.astype(jnp.float32))
        row, shift, here, there = place(plan_ref, slot, width, columns)
        mine = row_iota < row if pushed else row_iota >= row
        first = lane_iota >= shift
        if pushed:
            start = plan_ref[AT_PUSH, slot] - row // UNIT
            seen = came_ref[pl.ds(jnp.minimum(start + units, last + 1 - seen_units), seen_units)]
            measured.append(seen.reshape(width, width))
        else:
            start = plan_ref[AT_PULL, slot]
            measured.append(seen_ref[slot])
        units_at = [jnp.clip(start + u, 0, last) for u in range(units)]
        for l in range(slices):
            for p in range(planes):
                theirs = jnp.concatenate([came_ref[i, l * planes + p] for i in units_at], axis=0)
                ours = jnp.where(first, own_ref[l, p, :, here], own_ref[l, p, :, there])
                window_ref[at[b], l, p] = jnp.where(mine, ours, theirs)
        for p in range(planes):
            wave_ref[at[b], 0, p] = pltpu.roll(pltpu.roll(probe_ref[p], row, 0), shift, 1)
    return forward(tables_ref, wave_ref, window_ref, field_ref, at, measured, scales)


def end_group(plan_ref, out_ref, out_at, grad_ref, back_ref, group, pushed):
    slices, planes, width, columns = grad_ref.shape
    units = width // UNIT
    row_iota, lane_iota = iotas(width)
    for b in range(BATCH):
        slot, live = slot_of(plan_ref, group, b, pushed)
        row, shift, here, there = place(plan_ref, slot, width, columns)
        mine = row_iota < row if pushed else row_iota >= row
        first = lane_iota >= shift
        if pushed:
            start, begin, end = plan_ref[AT_BACK, slot], row // UNIT, units
        else:
            start, begin, end = plan_ref[AT_PULL, slot], 0, (row + UNIT - 1) // UNIT

        @pl.when(live)
        def _(b=b, mine=mine, first=first, here=here, there=there, start=start, begin=begin, end=end):
            for l in range(slices):
                for p in range(planes):
                    ours = jnp.where(mine, out_ref[out_at[b], l, p], 0.0)
                    grad_ref[l, p, :, here] += jnp.where(first, ours, 0.0)
                    grad_ref[l, p, :, there] += jnp.where(first, 0.0, ours)

            def unit(u, carry):
                rows = pl.ds(pl.multiple_of(u * UNIT, UNIT), UNIT)
                for l in range(slices):
                    for p in range(planes):
                        back_ref[start + u - begin, l * planes + p] = out_ref[out_at[b], l, p, rows, :]
                return carry

            lax.fori_loop(begin, end, unit, 0)


def pushed_kernel(plan_ref, probe_ref, own_ref, came_ref, tables_ref,
                  grad_ref, back_ref, sums_ref, wave_ref, window_ref, field_ref):
    grad_ref[...] = jnp.zeros_like(grad_ref)
    at = list(range(BATCH))

    def step(group, loss):
        loss = loss + begin_group(
            plan_ref, probe_ref, own_ref, came_ref, None, tables_ref, wave_ref, window_ref, field_ref, group, at, True
        )
        backward(tables_ref, wave_ref, window_ref, field_ref, at, window_ref, at, range(wave_ref.shape[1])[::-1])
        end_group(plan_ref, window_ref, at, grad_ref, back_ref, group, True)
        return loss

    groups = (plan_ref[TOTALS, 0] + BATCH - 1) // BATCH
    sums_ref[0] = lax.fori_loop(0, groups, step, jnp.float32(0.0))
    sums_ref[1] = jnp.float32(0.0)


def kept_forward_kernel(plan_ref, probe_ref, own_ref, came_ref, tables_ref, sums_in_ref, seen_ref,
                        wave_ref, window_ref, field_ref, sums_ref):
    def step(group, loss):
        at = [group * BATCH + b for b in range(BATCH)]
        return loss + begin_group(
            plan_ref, probe_ref, own_ref, came_ref, seen_ref, tables_ref, wave_ref, window_ref, field_ref, group, at, False
        )

    groups = (plan_ref[TOTALS, 1] + BATCH - 1) // BATCH
    sums_ref[0] = lax.fori_loop(0, groups, step, sums_in_ref[0])
    sums_ref[1] = plan_ref[TOTALS, 2].astype(jnp.float32)


def kept_top_kernel(plan_ref, tables_ref, wave_ref, window_ref, field_ref, out_ref, next_ref):
    layers = range(wave_ref.shape[1])[::-1]

    def step(group, carry):
        at = [group * BATCH + b for b in range(BATCH)]
        backward(
            tables_ref, wave_ref, window_ref, field_ref, at, out_ref, at, layers[: len(layers) // 2], next_ref
        )
        return carry

    lax.fori_loop(0, (plan_ref[TOTALS, 1] + BATCH - 1) // BATCH, step, 0)


def kept_bottom_kernel(plan_ref, tables_ref, wave_ref, window_ref, field_ref, top_ref, grad_in_ref, first_ref,
                       grad_ref, back_ref, out_ref):
    grad_ref[...] = grad_in_ref[...]
    layers = range(wave_ref.shape[1])[::-1]
    lower = layers[len(layers) // 2 :]
    out_at = list(range(BATCH))

    def step(group, carry):
        at = [group * BATCH + b for b in range(BATCH)]
        for i, b in enumerate(at):
            for layer in layers[: len(layers) // 2]:
                out_ref[i, layer] = top_ref[b, layer]
        backward(tables_ref, wave_ref, window_ref, field_ref, at, out_ref, out_at, lower)
        end_group(plan_ref, out_ref, out_at, grad_ref, back_ref, group, False)
        return carry

    lax.fori_loop(0, (plan_ref[TOTALS, 1] + BATCH - 1) // BATCH, step, 0)


def after_kernel(x_ref, *refs):
    pass


def add(plan, slot, grad_ref, layers, came, start, begin, end, below):
    planes, width, columns = grad_ref.shape[1:]
    row, shift, here, there = place(plan, slot, width, columns)
    first = lax.broadcasted_iota(jnp.int32, (UNIT, width), 1) >= shift
    row_iota = lax.broadcasted_iota(jnp.int32, (UNIT, width), 0)

    def unit(u, carry):
        rows = pl.ds(pl.multiple_of(u * UNIT, UNIT), UNIT)
        at = u * UNIT + row_iota
        mine = at < row if below else at >= row
        for l in layers:
            for p in range(planes):
                piece = jnp.where(mine, came[start + u - begin, l * planes + p], 0.0)
                grad_ref[l, p, rows, here] += jnp.where(first, piece, 0.0)
                grad_ref[l, p, rows, there] += jnp.where(first, 0.0, piece)
        return carry

    lax.fori_loop(begin, end, unit, 0)


def add_returned_kernel(plan_ref, returned_ref, grad_in_ref, grad_ref):
    slices, _, width, _ = grad_ref.shape
    grad_ref[...] = grad_in_ref[...]

    def step(i, carry):
        slot = plan_ref[PUSHED, i]
        at, low = plan_ref[AT_BACK, slot], plan_ref[ROW, slot] // UNIT
        add(plan_ref, slot, grad_ref, range(slices), returned_ref, at, low, width // UNIT, False)
        return carry

    lax.fori_loop(0, plan_ref[TOTALS, 0], step, 0)


def add_given(before_ref, given_ref, grad_ref, layers):
    def step(i, carry):
        slot = before_ref[KEPT, i]
        end = (before_ref[ROW, slot] + UNIT - 1) // UNIT
        add(before_ref, slot, grad_ref, layers, given_ref, before_ref[AT_PULL, slot], 0, end, True)
        return carry

    lax.fori_loop(0, before_ref[TOTALS, 1], step, 0)


def finish_kernel(before_ref, given_ref, grad_in_ref, grad_hbm, grad_ref, sems):
    slices = grad_ref.shape[0]
    stores = [pltpu.make_async_copy(grad_ref.at[l], grad_hbm.at[l], sems.at[l]) for l in range(slices)]
    for l in range(slices):
        grad_ref[l] = grad_in_ref[l]
        add_given(before_ref, given_ref, grad_ref, [l])
        stores[l].start()
    for store in stores:
        store.wait()


def merge_kernel(more_ref, base_hbm, sum_hbm, work_ref, sem):
    for l in range(work_ref.shape[0]):
        load = pltpu.make_async_copy(base_hbm.at[l], work_ref.at[l], sem)
        load.start()
        load.wait()
        work_ref[l] += more_ref[l]
        store = pltpu.make_async_copy(work_ref.at[l], sum_hbm.at[l], sem)
        store.start()
        store.wait()


def shifted(x, axis, by):
    peers = lax.axis_size(axis)
    return lax.ppermute(x, axis, [(i, (i + by) % peers) for i in range(peers)])


def total_stages(peers):
    stages, step = [], 1
    while step < peers:
        radix = 4 if step * 4 <= peers else 2
        stages.append((step, radix))
        step *= radix
    return stages


def partial_total(x, axis, stage):
    peers = lax.axis_size(axis)
    step, radix = stage

    def other(by):
        return lax.ppermute(x, axis, [(i, i ^ by) for i in range(peers)])

    if radix == 2:
        return x + other(step)
    return (x + other(step)) + (other(2 * step) + other(3 * step))


def local(probe_wave, object_slices, intensities, row_offset, col_offset, counts):
    width = probe_wave.shape[-1]
    slices, planes = object_slices.shape[:2]
    cap = row_offset.shape[0]
    peers = lax.axis_size("tile")
    units, seen_units = width // UNIT, width // (UNIT * UNIT)
    tables = jnp.asarray(make_tables(width))
    meta = jnp.concatenate([counts, row_offset, col_offset])
    seen = intensities.reshape(cap, seen_units, UNIT, UNIT, width)
    rooms = sizes(cap, width)
    smem = pl.BlockSpec(memory_space=pltpu.SMEM)
    vmem = pl.BlockSpec(memory_space=pltpu.VMEM)
    anywhere = pl.BlockSpec(memory_space=pl.ANY)
    f32 = jnp.float32

    def shape(dims, dtype=f32):
        return jax.ShapeDtypeStruct(dims, dtype)

    def packed(n):
        return shape((n, slices * planes, UNIT, width))

    def call(kernel, name, cost, ins, in_specs, outs, out_specs, scratch=(), mib=16, aliases=None):
        return pl.pallas_call(
            kernel,
            out_shape=outs,
            in_specs=in_specs,
            out_specs=out_specs,
            scratch_shapes=scratch,
            input_output_aliases=aliases or {},
            compiler_params=pltpu.CompilerParams(vmem_limit_bytes=mib << 20),
            cost_estimate=pl.CostEstimate(flops=int(cost * 1e9), bytes_accessed=int(cost * 1e6), transcendentals=0),
            name=name,
        )(*ins)

    def held(like):
        return pltpu.VMEM(like.shape, like.dtype)

    strip, sums_shape = shape(object_slices.shape), shape((2,))
    plan_shape = shape((8, cap), jnp.int32)
    dma = pltpu.SemaphoreType.DMA

    def held(like):
        return pltpu.VMEM(like.shape, like.dtype)

    def ahead(meta, source, again):
        kernel = functools.partial(push_kernel, rooms=rooms, again=again)
        outs = (plan_shape, held(packed(rooms[again][0] + 1)))
        if again:
            return call(kernel, "pack_more", 4, (meta, source, seen), [smem, vmem, anywhere], outs, (smem, vmem), [dma((cap,))])
        far = [pltpu.with_memory_space_constraint(x, pltpu.HBM) for x in (source, seen)]
        return call(
            kernel, "pack_pushed", 4, (meta, *far), [smem, anywhere, anywhere], outs + (held(strip),), (smem, vmem, vmem),
            [dma, dma((cap,))],
        )

    def behind(pushed, own, again):
        scratch = [pltpu.VMEM((UNIT, width), jnp.int32), pltpu.SMEM((UNIT, width), jnp.int32), dma]
        outs = (plan_shape, held(packed(rooms[again][2])))
        return call(pull_kernel, "pack_pulled", 2, (pushed, own), [vmem, vmem], outs, (smem, vmem), scratch)

    def waves(n):
        return shape((n, slices, planes, width, width)), shape((n, planes, width, width))

    def grads_pushed(before, own, pushed, back):
        wave, field = (pltpu.VMEM(x.shape, f32) for x in waves(BATCH))
        return call(
            pushed_kernel, "grads_pushed", 10, (before, probe_wave, own, pushed, tables), [smem] + [vmem] * 4,
            (held(strip), held(packed(back)), sums_shape), (vmem, vmem, smem), [wave, wave, field], 24,
        )

    def waves_kept(plan, own, pulled, sums):
        wave, field = (held(x) for x in waves(-(-cap // BATCH) * BATCH))
        return call(
            kept_forward_kernel, "waves_kept", 5, (plan, probe_wave, own, pulled, tables, sums, intensities),
            [smem] + [vmem] * 4 + [smem, vmem], (wave, wave, field, sums_shape), (vmem, vmem, vmem, smem), mib=20,
        )

    def grads_kept(plan, wave, window, field, grad, back, first):
        top, field = call(
            kept_top_kernel, "grads_top", 3, (plan, tables, wave, window, field), [smem] + [vmem] * 4,
            (held(wave), held(field)), (vmem, vmem), mib=16,
        )
        return call(
            kept_bottom_kernel, "grads_bottom", 3, (plan, tables, wave, window, field, top, grad, first),
            [smem] + [vmem] * 6 + [anywhere],
            (held(strip), held(packed(back))), (vmem, vmem), [pltpu.VMEM(waves(BATCH)[0].shape, f32)], 16, {6: 0},
        )

    stages = total_stages(peers)

    def one_round(own, plan, push, again):
        pushed = shifted(push, "tile", 1)
        before, pull = behind(pushed, own, again)
        pulled = shifted(pull, "tile", -1)
        grad, back, sums = grads_pushed(before, own, pushed, rooms[again][1])
        returned = shifted(back, "tile", -1)
        wave, window, field, sums = waves_kept(plan, own, pulled, sums)
        sums = partial_total(sums, "tile", stages[0])
        grad, back = grads_kept(plan, wave, window, field, grad, rooms[again][2], sums)
        for stage in stages[1:]:
            sums = partial_total(sums, "tile", stage)
        back = call(
            after_kernel, "after_returned", 1, (back, returned, sums), [anywhere] * 3, held(back), anywhere, aliases={0: 0}
        )
        given = shifted(back, "tile", 1)
        grad = call(
            add_returned_kernel, "add_returned", 1, (plan, returned, grad), [smem, vmem, vmem], held(strip), vmem,
            aliases={2: 0},
        )
        grad = call(
            finish_kernel, "add_given", 4, (before, given, grad), [smem, vmem, vmem], pltpu.HBM(strip.shape, f32), anywhere,
            [pltpu.VMEM(strip.shape, f32), dma((slices,))],
        )
        return grad, sums

    def unfinished(carry):
        return carry[1] > 0

    def second(carry):
        grad, _, loss, meta = carry
        more, sums = one_round(own, *ahead(meta, own, True), True)
        grad = call(
            merge_kernel, "merge", 4, (more, pltpu.with_memory_space_constraint(grad, pltpu.HBM)), [vmem, anywhere],
            pltpu.HBM(strip.shape, f32), anywhere, [pltpu.VMEM(strip.shape, f32), dma], aliases={1: 0},
        )
        return grad, jnp.float32(0.0), loss + sums[:1], jnp.zeros_like(meta)

    plan, push, own = ahead(meta, object_slices, False)
    grad, sums = one_round(own, plan, push, False)
    grad, _, loss, _ = lax.while_loop(unfinished, second, (grad, sums[1], sums[:1], meta))
    return grad, loss


def solution(mesh):
    placed = (
        P(),
        P("parts", None, "tile", None),
        P(("parts", "tile"), None, None),
        P(("parts", "tile")),
        P(("parts", "tile")),
        P(("parts", "tile")),
    )
    return jax.shard_map(
        local,
        mesh=mesh,
        in_specs=placed,
        out_specs=(P("parts", None, "tile", None), P("parts")),
        check_vma=False,
    )
```

```python
import functools

import jax
import jax.numpy as jnp
import ml_dtypes
import numpy as np
from jax import lax
from jax.experimental import pallas as pl
from jax.experimental.pallas import tpu as pltpu
from jax.sharding import PartitionSpec as P

BATCH = 4
UNIT = 8
ROW, COL, AT_PUSH, AT_BACK, AT_PULL, PUSHED, KEPT, TOTALS = range(8)


def make_tables(width):
    indices = np.arange(width)
    dft = np.exp(-2j * np.pi * (np.outer(indices, indices) % width) / width) / np.sqrt(width)
    freqs = np.where(indices < width // 2, indices, indices - width).astype(np.float64)
    along = np.conj(dft) @ (np.exp(-0.0015j * freqs**2)[:, None] * dft)
    out = []
    for matrix in (along, dft):
        left = np.block([[matrix.real, -matrix.imag], [matrix.imag, matrix.real]])
        forms = []
        for form in (left, left.T):
            form = form.astype(np.float32)
            high = form.astype(ml_dtypes.bfloat16)
            low = (form - high.astype(np.float32)).astype(ml_dtypes.bfloat16)
            forms.append(np.stack([high, low]))
        out.append(np.stack(forms))
    return np.stack(out)


def split(x):
    high = x.astype(jnp.bfloat16)
    return high, (x - high.astype(jnp.float32)).astype(jnp.bfloat16)


def dot(a, b):
    return jnp.dot(a, b, preferred_element_type=jnp.float32)


def one_sided(tables, which, form, re, im):
    width = re.shape[0]
    high, low = split(jnp.concatenate([re, im], axis=1))
    m_high, m_low = tables[which, form, 0], tables[which, form, 1]
    out = dot(high, m_high) + (dot(high, m_low) + dot(low, m_high))
    return out[:, :width], out[:, width:]


def two_sided(tables, which, conj, re, im):
    form = 0 if conj else 1
    half = [one_sided(tables, which, form, a, b) for a, b in zip(re, im)]
    full = [one_sided(tables, which, form, a.T, b.T) for a, b in half]
    return [a.T for a, _ in full], [b.T for _, b in full]


def forward(tables, wave_ref, window_ref, field_ref, at, measured, scales):
    slices = wave_ref.shape[1]
    for layer in range(slices):
        re, im = [], []
        for b in at:
            w_re, w_im = wave_ref[b, layer, 0], wave_ref[b, layer, 1]
            t_re, t_im = window_ref[b, layer, 0], window_ref[b, layer, 1]
            re.append(w_re * t_re - w_im * t_im)
            im.append(w_re * t_im + w_im * t_re)
        if layer + 1 < slices:
            re, im = two_sided(tables, 0, False, re, im)
            for i, b in enumerate(at):
                wave_ref[b, layer + 1, 0] = re[i]
                wave_ref[b, layer + 1, 1] = im[i]
    re, im = two_sided(tables, 1, False, re, im)
    loss = 0.0
    for i, b in enumerate(at):
        misfit = re[i] * re[i] + im[i] * im[i] - measured[i]
        loss = loss + scales[i] * (0.25 * jnp.sum(misfit * misfit))
        field_ref[b, 0] = misfit * re[i]
        field_ref[b, 1] = misfit * im[i]
    return loss


def backward(tables, wave_ref, window_ref, field_ref, at, out_ref):
    slices = wave_ref.shape[1]
    re, im = two_sided(tables, 1, True, [field_ref[b, 0] for b in at], [field_ref[b, 1] for b in at])
    for layer in reversed(range(slices)):
        upper_re, upper_im = [], []
        for i, b in enumerate(at):
            w_re, w_im = wave_ref[b, layer, 0], wave_ref[b, layer, 1]
            t_re, t_im = window_ref[b, layer, 0], window_ref[b, layer, 1]
            out_ref[i, layer, 0] = re[i] * w_re + im[i] * w_im
            out_ref[i, layer, 1] = im[i] * w_re - re[i] * w_im
            upper_re.append(re[i] * t_re + im[i] * t_im)
            upper_im.append(im[i] * t_re - re[i] * t_im)
        if layer > 0:
            re, im = two_sided(tables, 0, True, upper_re, upper_im)


def place(plan_ref, slot, width, columns):
    row, col = plan_ref[ROW, slot], plan_ref[COL, slot]
    tile = col // width
    here = pl.ds(pl.multiple_of(tile * width, width), width)
    after = jnp.minimum(tile + 1, columns // width - 1)
    there = pl.ds(pl.multiple_of(after * width, width), width)
    return row, col - tile * width, here, there


def sizes(cap, width):
    whole = cap * width // UNIT
    first = (whole * 9 // 32, whole * 27 // 128, whole * 33 // 128)
    return first, (whole * 5 // 16, whole // 4, whole * 5 // 16)


def make_plan(meta_ref, plan_ref, width, rooms, again):
    cap = plan_ref.shape[1]
    units = width // UNIT
    seen_units = width // (UNIT * UNIT)
    shape = (UNIT, 128)
    choice = lax.broadcasted_iota(jnp.int32, shape, 0) * 128 + lax.broadcasted_iota(jnp.int32, shape, 1)
    zero = jnp.zeros(shape, jnp.int32)
    push, back, pull, n_push, bad = zero, zero, zero, zero, (choice >= (1 << cap)).astype(jnp.int32)
    count = meta_ref[0]
    for s in range(cap):
        row = meta_ref[1 + s]
        crosses = jnp.logical_and(s < count, row > 0).astype(jnp.int32)
        taken = (choice >> s) & 1
        ahead = units - row // UNIT
        push += taken * (ahead + seen_units)
        back += taken * ahead
        pull += (1 - taken) * (crosses * ((row + UNIT - 1) // UNIT))
        n_push += taken
        bad += taken * (1 - crosses)
    n_keep = count - n_push
    groups = (n_push + BATCH - 1) // BATCH + (n_keep + BATCH - 1) // BATCH
    worst = 16 * cap

    def best_of(room):
        over = bad + (push > room[0]).astype(jnp.int32) + (back > room[1]).astype(jnp.int32) + (pull > room[2]).astype(jnp.int32)
        score = (groups * 16 + n_keep + worst * (over > 0).astype(jnp.int32)) * (1 << cap) + choice
        return jnp.min(score.astype(jnp.float32)).astype(jnp.int32)

    best = best_of(rooms[0])
    short = (best >= worst << cap).astype(jnp.int32)
    if again:
        best = best_of(rooms[1])
    at_push = at_back = at_pull = n_pushed = n_kept = jnp.int32(0)
    for s in range(cap):
        plan_ref[PUSHED, s] = 0
        plan_ref[KEPT, s] = 0
        plan_ref[TOTALS, s] = 0
    for s in range(cap):
        row = meta_ref[1 + s]
        crosses = (row > 0).astype(jnp.int32)
        now = short * crosses if again else 1 - short * crosses
        taken = ((best >> s) & 1) * (short if again else 1 - short)
        kept = jnp.where(s < count, (1 - taken) * now, 0)
        plan_ref[ROW, s] = row
        plan_ref[COL, s] = meta_ref[1 + cap + s]
        plan_ref[AT_PUSH, s] = at_push
        plan_ref[AT_BACK, s] = at_back
        plan_ref[AT_PULL, s] = at_pull

        @pl.when(taken > 0)
        def _():
            plan_ref[PUSHED, n_pushed] = s

        @pl.when(kept > 0)
        def _():
            plan_ref[KEPT, n_kept] = s

        ahead = units - row // UNIT
        at_push += taken * (ahead + seen_units)
        at_back += taken * ahead
        at_pull += kept * ((row + UNIT - 1) // UNIT)
        n_pushed += taken
        n_kept += kept
    plan_ref[TOTALS, 0] = n_pushed
    plan_ref[TOTALS, 1] = n_kept
    plan_ref[TOTALS, 2] = short


def pack(plan_ref, slot, own_ref, buffer_ref, start, first_unit, last_unit):
    slices, planes, width, columns = own_ref.shape
    _, shift, here, there = place(plan_ref, slot, width, columns)
    first = lax.broadcasted_iota(jnp.int32, (UNIT, width), 1) >= shift

    def step(u, carry):
        rows = pl.ds(pl.multiple_of(u * UNIT, UNIT), UNIT)
        for l in range(slices):
            for p in range(planes):
                buffer_ref[start + u - first_unit, l * planes + p] = jnp.where(
                    first, own_ref[l, p, rows, here], own_ref[l, p, rows, there]
                )
        return carry

    lax.fori_loop(first_unit, last_unit, step, 0)


def push_kernel(meta_ref, own_in_ref, seen_hbm, plan_ref, push_ref, *refs, rooms, again):
    if again:
        own_ref = own_in_ref
        sems, = refs
    else:
        own_ref, sem, sems = refs
        load = pltpu.make_async_copy(own_in_ref, own_ref, sem)
        load.start()
    width = own_ref.shape[2]
    units, seen_units = width // UNIT, seen_hbm.shape[1]
    make_plan(meta_ref, plan_ref, width, rooms, again)

    def seen(i):
        slot = plan_ref[PUSHED, i]
        start = plan_ref[AT_PUSH, slot] + units - plan_ref[ROW, slot] // UNIT
        return pltpu.make_async_copy(seen_hbm.at[slot], push_ref.at[pl.ds(start, seen_units)], sems.at[i])

    def begin(i, carry):
        seen(i).start()
        return carry

    def step(i, carry):
        slot = plan_ref[PUSHED, i]
        pack(plan_ref, slot, own_ref, push_ref, plan_ref[AT_PUSH, slot], plan_ref[ROW, slot] // UNIT, units)
        return carry

    def end(i, carry):
        seen(i).wait()
        return carry

    lax.fori_loop(0, plan_ref[TOTALS, 0], begin, 0)
    shape = (UNIT, width)
    index = lax.broadcasted_iota(jnp.int32, shape, 0) * width + lax.broadcasted_iota(jnp.int32, shape, 1)
    told = jnp.zeros(shape, jnp.float32)
    for r in range(plan_ref.shape[0]):
        for s in range(plan_ref.shape[1]):
            told = jnp.where(index == r * width + s, plan_ref[r, s].astype(jnp.float32), told)
    push_ref[push_ref.shape[0] - 1, 0] = told
    if not again:
        load.wait()
    lax.fori_loop(0, plan_ref[TOTALS, 0], step, 0)
    lax.fori_loop(0, plan_ref[TOTALS, 0], end, 0)


def pull_kernel(told_ref, own_ref, plan_ref, pull_ref, whole_ref, numbers_ref, sem):
    whole_ref[...] = told_ref[told_ref.shape[0] - 1, 0].astype(jnp.int32)
    copy = pltpu.make_async_copy(whole_ref, numbers_ref, sem)
    copy.start()
    copy.wait()
    for r in range(plan_ref.shape[0]):
        for s in range(plan_ref.shape[1]):
            plan_ref[r, s] = numbers_ref[r, s]

    def step(i, carry):
        slot = plan_ref[KEPT, i]
        end = (plan_ref[ROW, slot] + UNIT - 1) // UNIT
        pack(plan_ref, slot, own_ref, pull_ref, plan_ref[AT_PULL, slot], 0, end)
        return carry

    lax.fori_loop(0, plan_ref[TOTALS, 1], step, 0)


def slot_of(plan_ref, group, b, pushed):
    count = plan_ref[TOTALS, 0 if pushed else 1]
    live = group * BATCH + b < count
    return plan_ref[PUSHED if pushed else KEPT, jnp.where(live, group * BATCH + b, group * BATCH)], live


def iotas(width):
    shape = (width, width)
    return lax.broadcasted_iota(jnp.int32, shape, 0), lax.broadcasted_iota(jnp.int32, shape, 1)


def begin_group(plan_ref, probe_ref, own_ref, came_ref, seen_ref, tables_ref, wave_ref, window_ref, field_ref, group, at, pushed):
    slices, planes, width, columns = own_ref.shape
    units = width // UNIT
    seen_units = width // (UNIT * UNIT)
    last = came_ref.shape[0] - 1
    row_iota, lane_iota = iotas(width)
    scales, measured = [], []
    for b in range(BATCH):
        slot, live = slot_of(plan_ref, group, b, pushed)
        scales.append(live.astype(jnp.float32))
        row, shift, here, there = place(plan_ref, slot, width, columns)
        mine = row_iota < row if pushed else row_iota >= row
        first = lane_iota >= shift
        if pushed:
            start = plan_ref[AT_PUSH, slot] - row // UNIT
            seen = came_ref[pl.ds(jnp.minimum(start + units, last + 1 - seen_units), seen_units)]
            measured.append(seen.reshape(width, width))
        else:
            start = plan_ref[AT_PULL, slot]
            measured.append(seen_ref[slot])
        units_at = [jnp.clip(start + u, 0, last) for u in range(units)]
        for l in range(slices):
            for p in range(planes):
                theirs = jnp.concatenate([came_ref[i, l * planes + p] for i in units_at], axis=0)
                ours = jnp.where(first, own_ref[l, p, :, here], own_ref[l, p, :, there])
                window_ref[at[b], l, p] = jnp.where(mine, ours, theirs)
        for p in range(planes):
            wave_ref[at[b], 0, p] = pltpu.roll(pltpu.roll(probe_ref[p], row, 0), shift, 1)
    return forward(tables_ref, wave_ref, window_ref, field_ref, at, measured, scales)


def end_group(plan_ref, tables_ref, wave_ref, window_ref, field_ref, out_ref, grad_ref, back_ref, group, at, pushed):
    slices, planes, width, columns = grad_ref.shape
    units = width // UNIT
    row_iota, lane_iota = iotas(width)
    backward(tables_ref, wave_ref, window_ref, field_ref, at, out_ref)
    for b in range(BATCH):
        slot, live = slot_of(plan_ref, group, b, pushed)
        row, shift, here, there = place(plan_ref, slot, width, columns)
        mine = row_iota < row if pushed else row_iota >= row
        first = lane_iota >= shift
        if pushed:
            start, begin, end = plan_ref[AT_BACK, slot], row // UNIT, units
        else:
            start, begin, end = plan_ref[AT_PULL, slot], 0, (row + UNIT - 1) // UNIT

        @pl.when(live)
        def _(b=b, mine=mine, first=first, here=here, there=there, start=start, begin=begin, end=end):
            for l in range(slices):
                for p in range(planes):
                    ours = jnp.where(mine, out_ref[b, l, p], 0.0)
                    grad_ref[l, p, :, here] += jnp.where(first, ours, 0.0)
                    grad_ref[l, p, :, there] += jnp.where(first, 0.0, ours)

            def unit(u, carry):
                rows = pl.ds(pl.multiple_of(u * UNIT, UNIT), UNIT)
                for l in range(slices):
                    for p in range(planes):
                        back_ref[start + u - begin, l * planes + p] = out_ref[b, l, p, rows, :]
                return carry

            lax.fori_loop(begin, end, unit, 0)


def pushed_kernel(plan_ref, probe_ref, own_ref, came_ref, tables_ref,
                  grad_ref, back_ref, sums_ref, wave_ref, window_ref, field_ref):
    grad_ref[...] = jnp.zeros_like(grad_ref)
    at = list(range(BATCH))

    def step(group, loss):
        loss = loss + begin_group(
            plan_ref, probe_ref, own_ref, came_ref, None, tables_ref, wave_ref, window_ref, field_ref, group, at, True
        )
        end_group(
            plan_ref, tables_ref, wave_ref, window_ref, field_ref, window_ref, grad_ref, back_ref, group, at, True
        )
        return loss

    groups = (plan_ref[TOTALS, 0] + BATCH - 1) // BATCH
    sums_ref[0] = lax.fori_loop(0, groups, step, jnp.float32(0.0))
    sums_ref[1] = jnp.float32(0.0)


def kept_forward_kernel(plan_ref, probe_ref, own_ref, came_ref, tables_ref, sums_in_ref, seen_ref,
                        wave_ref, window_ref, field_ref, sums_ref):
    def step(group, loss):
        at = [group * BATCH + b for b in range(BATCH)]
        return loss + begin_group(
            plan_ref, probe_ref, own_ref, came_ref, seen_ref, tables_ref, wave_ref, window_ref, field_ref, group, at, False
        )

    groups = (plan_ref[TOTALS, 1] + BATCH - 1) // BATCH
    sums_ref[0] = lax.fori_loop(0, groups, step, sums_in_ref[0])
    sums_ref[1] = plan_ref[TOTALS, 2].astype(jnp.float32)


def kept_backward_kernel(plan_ref, tables_ref, wave_ref, window_ref, field_ref, grad_in_ref, grad_ref, back_ref, out_ref):
    grad_ref[...] = grad_in_ref[...]

    def step(group, carry):
        at = [group * BATCH + b for b in range(BATCH)]
        end_group(plan_ref, tables_ref, wave_ref, window_ref, field_ref, out_ref, grad_ref, back_ref, group, at, False)
        return carry

    lax.fori_loop(0, (plan_ref[TOTALS, 1] + BATCH - 1) // BATCH, step, 0)


def after_kernel(x_ref, *refs):
    pass


def add(plan, slot, grad_ref, layers, came, start, begin, end, below):
    planes, width, columns = grad_ref.shape[1:]
    row, shift, here, there = place(plan, slot, width, columns)
    first = lax.broadcasted_iota(jnp.int32, (UNIT, width), 1) >= shift
    row_iota = lax.broadcasted_iota(jnp.int32, (UNIT, width), 0)

    def unit(u, carry):
        rows = pl.ds(pl.multiple_of(u * UNIT, UNIT), UNIT)
        at = u * UNIT + row_iota
        mine = at < row if below else at >= row
        for l in layers:
            for p in range(planes):
                piece = jnp.where(mine, came[start + u - begin, l * planes + p], 0.0)
                grad_ref[l, p, rows, here] += jnp.where(first, piece, 0.0)
                grad_ref[l, p, rows, there] += jnp.where(first, 0.0, piece)
        return carry

    lax.fori_loop(begin, end, unit, 0)


def add_returned_kernel(plan_ref, returned_ref, grad_in_ref, grad_ref):
    slices, _, width, _ = grad_ref.shape
    grad_ref[...] = grad_in_ref[...]

    def step(i, carry):
        slot = plan_ref[PUSHED, i]
        at, low = plan_ref[AT_BACK, slot], plan_ref[ROW, slot] // UNIT
        add(plan_ref, slot, grad_ref, range(slices), returned_ref, at, low, width // UNIT, False)
        return carry

    lax.fori_loop(0, plan_ref[TOTALS, 0], step, 0)


def add_given(before_ref, given_ref, grad_ref, layers):
    def step(i, carry):
        slot = before_ref[KEPT, i]
        end = (before_ref[ROW, slot] + UNIT - 1) // UNIT
        add(before_ref, slot, grad_ref, layers, given_ref, before_ref[AT_PULL, slot], 0, end, True)
        return carry

    lax.fori_loop(0, before_ref[TOTALS, 1], step, 0)


def finish_kernel(before_ref, given_ref, grad_in_ref, grad_hbm, grad_ref, sems):
    slices = grad_ref.shape[0]
    stores = [pltpu.make_async_copy(grad_ref.at[l], grad_hbm.at[l], sems.at[l]) for l in range(slices)]
    for l in range(slices):
        grad_ref[l] = grad_in_ref[l]
        add_given(before_ref, given_ref, grad_ref, [l])
        stores[l].start()
    for store in stores:
        store.wait()


def merge_kernel(more_ref, base_hbm, sum_hbm, work_ref, sem):
    for l in range(work_ref.shape[0]):
        load = pltpu.make_async_copy(base_hbm.at[l], work_ref.at[l], sem)
        load.start()
        load.wait()
        work_ref[l] += more_ref[l]
        store = pltpu.make_async_copy(work_ref.at[l], sum_hbm.at[l], sem)
        store.start()
        store.wait()


def shifted(x, axis, by):
    peers = lax.axis_size(axis)
    return lax.ppermute(x, axis, [(i, (i + by) % peers) for i in range(peers)])


def total_stages(peers):
    stages, step = [], 1
    while step < peers:
        radix = 4 if step * 4 <= peers else 2
        stages.append((step, radix))
        step *= radix
    return stages


def partial_total(x, axis, stage):
    peers = lax.axis_size(axis)
    step, radix = stage

    def other(by):
        return lax.ppermute(x, axis, [(i, i ^ by) for i in range(peers)])

    if radix == 2:
        return x + other(step)
    return (x + other(step)) + (other(2 * step) + other(3 * step))


def local(probe_wave, object_slices, intensities, row_offset, col_offset, counts):
    width = probe_wave.shape[-1]
    slices, planes = object_slices.shape[:2]
    cap = row_offset.shape[0]
    peers = lax.axis_size("tile")
    units, seen_units = width // UNIT, width // (UNIT * UNIT)
    tables = jnp.asarray(make_tables(width))
    meta = jnp.concatenate([counts, row_offset, col_offset])
    seen = intensities.reshape(cap, seen_units, UNIT, UNIT, width)
    rooms = sizes(cap, width)
    smem = pl.BlockSpec(memory_space=pltpu.SMEM)
    vmem = pl.BlockSpec(memory_space=pltpu.VMEM)
    anywhere = pl.BlockSpec(memory_space=pl.ANY)
    f32 = jnp.float32

    def shape(dims, dtype=f32):
        return jax.ShapeDtypeStruct(dims, dtype)

    def packed(n):
        return shape((n, slices * planes, UNIT, width))

    def call(kernel, name, cost, ins, in_specs, outs, out_specs, scratch=(), mib=16, aliases=None):
        return pl.pallas_call(
            kernel,
            out_shape=outs,
            in_specs=in_specs,
            out_specs=out_specs,
            scratch_shapes=scratch,
            input_output_aliases=aliases or {},
            compiler_params=pltpu.CompilerParams(vmem_limit_bytes=mib << 20),
            cost_estimate=pl.CostEstimate(flops=int(cost * 1e9), bytes_accessed=int(cost * 1e6), transcendentals=0),
            name=name,
        )(*ins)

    def held(like):
        return pltpu.VMEM(like.shape, like.dtype)

    strip, sums_shape = shape(object_slices.shape), shape((2,))
    plan_shape = shape((8, cap), jnp.int32)
    dma = pltpu.SemaphoreType.DMA

    def held(like):
        return pltpu.VMEM(like.shape, like.dtype)

    def ahead(meta, source, again):
        kernel = functools.partial(push_kernel, rooms=rooms, again=again)
        outs = (plan_shape, held(packed(rooms[again][0] + 1)))
        if again:
            return call(kernel, "pack_more", 4, (meta, source, seen), [smem, vmem, anywhere], outs, (smem, vmem), [dma((cap,))])
        far = [pltpu.with_memory_space_constraint(x, pltpu.HBM) for x in (source, seen)]
        return call(
            kernel, "pack_pushed", 4, (meta, *far), [smem, anywhere, anywhere], outs + (held(strip),), (smem, vmem, vmem),
            [dma, dma((cap,))],
        )

    def behind(pushed, own, again):
        scratch = [pltpu.VMEM((UNIT, width), jnp.int32), pltpu.SMEM((UNIT, width), jnp.int32), dma]
        outs = (plan_shape, held(packed(rooms[again][2])))
        return call(pull_kernel, "pack_pulled", 2, (pushed, own), [vmem, vmem], outs, (smem, vmem), scratch)

    def waves(n):
        return shape((n, slices, planes, width, width)), shape((n, planes, width, width))

    def grads_pushed(before, own, pushed, back):
        wave, field = (pltpu.VMEM(x.shape, f32) for x in waves(BATCH))
        return call(
            pushed_kernel, "grads_pushed", 10, (before, probe_wave, own, pushed, tables), [smem] + [vmem] * 4,
            (held(strip), held(packed(back)), sums_shape), (vmem, vmem, smem), [wave, wave, field], 24,
        )

    def waves_kept(plan, own, pulled, sums):
        wave, field = (held(x) for x in waves(-(-cap // BATCH) * BATCH))
        return call(
            kept_forward_kernel, "waves_kept", 5, (plan, probe_wave, own, pulled, tables, sums, intensities),
            [smem] + [vmem] * 4 + [smem, vmem], (wave, wave, field, sums_shape), (vmem, vmem, vmem, smem), mib=20,
        )

    def grads_kept(plan, wave, window, field, grad, back):
        return call(
            kept_backward_kernel, "grads_kept", 5, (plan, tables, wave, window, field, grad), [smem] + [vmem] * 5,
            (held(strip), held(packed(back))), (vmem, vmem), [pltpu.VMEM(waves(BATCH)[0].shape, f32)], 20, {5: 0},
        )

    stages = total_stages(peers)

    def one_round(own, plan, push, again):
        pushed = shifted(push, "tile", 1)
        before, pull = behind(pushed, own, again)
        pulled = shifted(pull, "tile", -1)
        grad, back, sums = grads_pushed(before, own, pushed, rooms[again][1])
        returned = shifted(back, "tile", -1)
        wave, window, field, sums = waves_kept(plan, own, pulled, sums)
        sums = partial_total(sums, "tile", stages[0])
        grad, back = grads_kept(plan, wave, window, field, grad, rooms[again][2])
        back = call(
            after_kernel, "after_returned", 1, (back, returned, sums), [anywhere] * 3, held(back), anywhere, aliases={0: 0}
        )
        given = shifted(back, "tile", 1)
        for stage in stages[1:]:
            sums = partial_total(sums, "tile", stage)
        grad = call(
            add_returned_kernel, "add_returned", 1, (plan, returned, grad), [smem, vmem, vmem], held(strip), vmem,
            aliases={2: 0},
        )
        grad = call(
            finish_kernel, "add_given", 4, (before, given, grad), [smem, vmem, vmem], pltpu.HBM(strip.shape, f32), anywhere,
            [pltpu.VMEM(strip.shape, f32), dma((slices,))],
        )
        return grad, sums

    def unfinished(carry):
        return carry[1] > 0

    def second(carry):
        grad, _, loss, meta = carry
        more, sums = one_round(own, *ahead(meta, own, True), True)
        grad = call(
            merge_kernel, "merge", 4, (more, pltpu.with_memory_space_constraint(grad, pltpu.HBM)), [vmem, anywhere],
            pltpu.HBM(strip.shape, f32), anywhere, [pltpu.VMEM(strip.shape, f32), dma], aliases={1: 0},
        )
        return grad, jnp.float32(0.0), loss + sums[:1], jnp.zeros_like(meta)

    plan, push, own = ahead(meta, object_slices, False)
    grad, sums = one_round(own, plan, push, False)
    grad, _, loss, _ = lax.while_loop(unfinished, second, (grad, sums[1], sums[:1], meta))
    return grad, loss


def solution(mesh):
    placed = (
        P(),
        P("parts", None, "tile", None),
        P(("parts", "tile"), None, None),
        P(("parts", "tile")),
        P(("parts", "tile")),
        P(("parts", "tile")),
    )
    return jax.shard_map(
        local,
        mesh=mesh,
        in_specs=placed,
        out_specs=(P("parts", None, "tile", None), P("parts")),
        check_vma=False,
    )
```

```python
import functools

import jax
import jax.numpy as jnp
import ml_dtypes
import numpy as np
from jax import lax
from jax.experimental import pallas as pl
from jax.experimental.pallas import tpu as pltpu
from jax.sharding import PartitionSpec as P

BATCH = 4
UNIT = 8
ROW, COL, AT_PUSH, AT_BACK, AT_PULL, PUSHED, KEPT, TOTALS = range(8)


def make_tables(width):
    indices = np.arange(width)
    dft = np.exp(-2j * np.pi * (np.outer(indices, indices) % width) / width) / np.sqrt(width)
    freqs = np.where(indices < width // 2, indices, indices - width).astype(np.float64)
    along = np.conj(dft) @ (np.exp(-0.0015j * freqs**2)[:, None] * dft)
    out = []
    for matrix in (along, dft):
        left = np.block([[matrix.real, -matrix.imag], [matrix.imag, matrix.real]])
        forms = []
        for form in (left, left.T):
            form = form.astype(np.float32)
            high = form.astype(ml_dtypes.bfloat16)
            low = (form - high.astype(np.float32)).astype(ml_dtypes.bfloat16)
            forms.append(np.stack([high, low]))
        out.append(np.stack(forms))
    return np.stack(out)


def split(x):
    high = x.astype(jnp.bfloat16)
    return high, (x - high.astype(jnp.float32)).astype(jnp.bfloat16)


def dot(a, b):
    return jnp.dot(a, b, preferred_element_type=jnp.float32)


def one_sided(tables, which, form, re, im):
    width = re.shape[0]
    high, low = split(jnp.concatenate([re, im], axis=1))
    m_high, m_low = tables[which, form, 0], tables[which, form, 1]
    out = dot(high, m_high) + (dot(high, m_low) + dot(low, m_high))
    return out[:, :width], out[:, width:]


def two_sided(tables, which, conj, re, im):
    form = 0 if conj else 1
    half = [one_sided(tables, which, form, a, b) for a, b in zip(re, im)]
    full = [one_sided(tables, which, form, a.T, b.T) for a, b in half]
    return [a.T for a, _ in full], [b.T for _, b in full]


def forward(tables, wave_ref, window_ref, field_ref, at, measured, scales):
    slices = wave_ref.shape[1]
    for layer in range(slices):
        re, im = [], []
        for b in at:
            w_re, w_im = wave_ref[b, layer, 0], wave_ref[b, layer, 1]
            t_re, t_im = window_ref[b, layer, 0], window_ref[b, layer, 1]
            re.append(w_re * t_re - w_im * t_im)
            im.append(w_re * t_im + w_im * t_re)
        if layer + 1 < slices:
            re, im = two_sided(tables, 0, False, re, im)
            for i, b in enumerate(at):
                wave_ref[b, layer + 1, 0] = re[i]
                wave_ref[b, layer + 1, 1] = im[i]
    re, im = two_sided(tables, 1, False, re, im)
    loss = 0.0
    for i, b in enumerate(at):
        misfit = re[i] * re[i] + im[i] * im[i] - measured[i]
        loss = loss + scales[i] * (0.25 * jnp.sum(misfit * misfit))
        field_ref[b, 0] = misfit * re[i]
        field_ref[b, 1] = misfit * im[i]
    return loss


def backward(tables, wave_ref, window_ref, field_ref, at, out_ref, out_at):
    slices = wave_ref.shape[1]
    re, im = two_sided(tables, 1, True, [field_ref[b, 0] for b in at], [field_ref[b, 1] for b in at])
    for layer in reversed(range(slices)):
        upper_re, upper_im = [], []
        for i, b in enumerate(at):
            w_re, w_im = wave_ref[b, layer, 0], wave_ref[b, layer, 1]
            t_re, t_im = window_ref[b, layer, 0], window_ref[b, layer, 1]
            out_ref[out_at[i], layer, 0] = re[i] * w_re + im[i] * w_im
            out_ref[out_at[i], layer, 1] = im[i] * w_re - re[i] * w_im
            upper_re.append(re[i] * t_re + im[i] * t_im)
            upper_im.append(im[i] * t_re - re[i] * t_im)
        if layer > 0:
            re, im = two_sided(tables, 0, True, upper_re, upper_im)


def place(plan_ref, slot, width, columns):
    row, col = plan_ref[ROW, slot], plan_ref[COL, slot]
    tile = col // width
    here = pl.ds(pl.multiple_of(tile * width, width), width)
    after = jnp.minimum(tile + 1, columns // width - 1)
    there = pl.ds(pl.multiple_of(after * width, width), width)
    return row, col - tile * width, here, there


def sizes(cap, width):
    whole = cap * width // UNIT
    first = (whole * 9 // 32, whole * 27 // 128, whole * 33 // 128)
    return first, (whole * 5 // 16, whole // 4, whole * 5 // 16)


def make_plan(meta_ref, plan_ref, width, rooms, again):
    cap = plan_ref.shape[1]
    units = width // UNIT
    seen_units = width // (UNIT * UNIT)
    shape = (UNIT, 128)
    choice = lax.broadcasted_iota(jnp.int32, shape, 0) * 128 + lax.broadcasted_iota(jnp.int32, shape, 1)
    zero = jnp.zeros(shape, jnp.int32)
    push, back, pull, n_push, bad = zero, zero, zero, zero, (choice >= (1 << cap)).astype(jnp.int32)
    count = meta_ref[0]
    for s in range(cap):
        row = meta_ref[1 + s]
        crosses = jnp.logical_and(s < count, row > 0).astype(jnp.int32)
        taken = (choice >> s) & 1
        ahead = units - row // UNIT
        push += taken * (ahead + seen_units)
        back += taken * ahead
        pull += (1 - taken) * (crosses * ((row + UNIT - 1) // UNIT))
        n_push += taken
        bad += taken * (1 - crosses)
    n_keep = count - n_push
    groups = (n_push + BATCH - 1) // BATCH + (n_keep + BATCH - 1) // BATCH
    worst = 16 * cap

    def best_of(room):
        over = bad + (push > room[0]).astype(jnp.int32) + (back > room[1]).astype(jnp.int32) + (pull > room[2]).astype(jnp.int32)
        score = (groups * 16 + n_keep + worst * (over > 0).astype(jnp.int32)) * (1 << cap) + choice
        return jnp.min(score.astype(jnp.float32)).astype(jnp.int32)

    best = best_of(rooms[0])
    short = (best >= worst << cap).astype(jnp.int32)
    if again:
        best = best_of(rooms[1])
    at_push = at_back = at_pull = n_pushed = n_kept = jnp.int32(0)
    for s in range(cap):
        plan_ref[PUSHED, s] = 0
        plan_ref[KEPT, s] = 0
        plan_ref[TOTALS, s] = 0
    for s in range(cap):
        row = meta_ref[1 + s]
        crosses = (row > 0).astype(jnp.int32)
        now = short * crosses if again else 1 - short * crosses
        taken = ((best >> s) & 1) * (short if again else 1 - short)
        kept = jnp.where(s < count, (1 - taken) * now, 0)
        plan_ref[ROW, s] = row
        plan_ref[COL, s] = meta_ref[1 + cap + s]
        plan_ref[AT_PUSH, s] = at_push
        plan_ref[AT_BACK, s] = at_back
        plan_ref[AT_PULL, s] = at_pull

        @pl.when(taken > 0)
        def _():
            plan_ref[PUSHED, n_pushed] = s

        @pl.when(kept > 0)
        def _():
            plan_ref[KEPT, n_kept] = s

        ahead = units - row // UNIT
        at_push += taken * (ahead + seen_units)
        at_back += taken * ahead
        at_pull += kept * ((row + UNIT - 1) // UNIT)
        n_pushed += taken
        n_kept += kept
    plan_ref[TOTALS, 0] = n_pushed
    plan_ref[TOTALS, 1] = n_kept
    plan_ref[TOTALS, 2] = short


def pack(plan_ref, slot, own_ref, buffer_ref, start, first_unit, last_unit):
    slices, planes, width, columns = own_ref.shape
    _, shift, here, there = place(plan_ref, slot, width, columns)
    first = lax.broadcasted_iota(jnp.int32, (UNIT, width), 1) >= shift

    def step(u, carry):
        rows = pl.ds(pl.multiple_of(u * UNIT, UNIT), UNIT)
        for l in range(slices):
            for p in range(planes):
                buffer_ref[start + u - first_unit, l * planes + p] = jnp.where(
                    first, own_ref[l, p, rows, here], own_ref[l, p, rows, there]
                )
        return carry

    lax.fori_loop(first_unit, last_unit, step, 0)


def push_kernel(meta_ref, own_in_ref, seen_hbm, plan_ref, push_ref, *refs, rooms, again):
    if again:
        own_ref = own_in_ref
        sems, = refs
    else:
        own_ref, sem, sems = refs
        load = pltpu.make_async_copy(own_in_ref, own_ref, sem)
        load.start()
    width = own_ref.shape[2]
    units, seen_units = width // UNIT, seen_hbm.shape[1]
    make_plan(meta_ref, plan_ref, width, rooms, again)

    def seen(i):
        slot = plan_ref[PUSHED, i]
        start = plan_ref[AT_PUSH, slot] + units - plan_ref[ROW, slot] // UNIT
        return pltpu.make_async_copy(seen_hbm.at[slot], push_ref.at[pl.ds(start, seen_units)], sems.at[i])

    def begin(i, carry):
        seen(i).start()
        return carry

    def step(i, carry):
        slot = plan_ref[PUSHED, i]
        pack(plan_ref, slot, own_ref, push_ref, plan_ref[AT_PUSH, slot], plan_ref[ROW, slot] // UNIT, units)
        return carry

    def end(i, carry):
        seen(i).wait()
        return carry

    lax.fori_loop(0, plan_ref[TOTALS, 0], begin, 0)
    shape = (UNIT, width)
    index = lax.broadcasted_iota(jnp.int32, shape, 0) * width + lax.broadcasted_iota(jnp.int32, shape, 1)
    told = jnp.zeros(shape, jnp.float32)
    for r in range(plan_ref.shape[0]):
        for s in range(plan_ref.shape[1]):
            told = jnp.where(index == r * width + s, plan_ref[r, s].astype(jnp.float32), told)
    push_ref[push_ref.shape[0] - 1, 0] = told
    if not again:
        load.wait()
    lax.fori_loop(0, plan_ref[TOTALS, 0], step, 0)
    lax.fori_loop(0, plan_ref[TOTALS, 0], end, 0)


def pull_kernel(told_ref, own_ref, plan_ref, pull_ref, whole_ref, numbers_ref, sem):
    whole_ref[...] = told_ref[told_ref.shape[0] - 1, 0].astype(jnp.int32)
    copy = pltpu.make_async_copy(whole_ref, numbers_ref, sem)
    copy.start()
    copy.wait()
    for r in range(plan_ref.shape[0]):
        for s in range(plan_ref.shape[1]):
            plan_ref[r, s] = numbers_ref[r, s]

    def step(i, carry):
        slot = plan_ref[KEPT, i]
        end = (plan_ref[ROW, slot] + UNIT - 1) // UNIT
        pack(plan_ref, slot, own_ref, pull_ref, plan_ref[AT_PULL, slot], 0, end)
        return carry

    lax.fori_loop(0, plan_ref[TOTALS, 1], step, 0)


def slot_of(plan_ref, group, b, pushed):
    count = plan_ref[TOTALS, 0 if pushed else 1]
    live = group * BATCH + b < count
    return plan_ref[PUSHED if pushed else KEPT, jnp.where(live, group * BATCH + b, group * BATCH)], live


def iotas(width):
    shape = (width, width)
    return lax.broadcasted_iota(jnp.int32, shape, 0), lax.broadcasted_iota(jnp.int32, shape, 1)


def begin_group(plan_ref, probe_ref, own_ref, came_ref, seen_ref, tables_ref, wave_ref, window_ref, field_ref, group, at, pushed):
    slices, planes, width, columns = own_ref.shape
    units = width // UNIT
    seen_units = width // (UNIT * UNIT)
    last = came_ref.shape[0] - 1
    row_iota, lane_iota = iotas(width)
    scales, measured = [], []
    for b in range(BATCH):
        slot, live = slot_of(plan_ref, group, b, pushed)
        scales.append(live.astype(jnp.float32))
        row, shift, here, there = place(plan_ref, slot, width, columns)
        mine = row_iota < row if pushed else row_iota >= row
        first = lane_iota >= shift
        if pushed:
            start = plan_ref[AT_PUSH, slot] - row // UNIT
            seen = came_ref[pl.ds(jnp.minimum(start + units, last + 1 - seen_units), seen_units)]
            measured.append(seen.reshape(width, width))
        else:
            start = plan_ref[AT_PULL, slot]
            measured.append(seen_ref[slot])
        units_at = [jnp.clip(start + u, 0, last) for u in range(units)]
        for l in range(slices):
            for p in range(planes):
                theirs = jnp.concatenate([came_ref[i, l * planes + p] for i in units_at], axis=0)
                ours = jnp.where(first, own_ref[l, p, :, here], own_ref[l, p, :, there])
                window_ref[at[b], l, p] = jnp.where(mine, ours, theirs)
        for p in range(planes):
            wave_ref[at[b], 0, p] = pltpu.roll(pltpu.roll(probe_ref[p], row, 0), shift, 1)
    return forward(tables_ref, wave_ref, window_ref, field_ref, at, measured, scales)


def pack_back(plan_ref, out_ref, out_at, back_ref, group, pushed):
    slices, planes, width = out_ref.shape[1:4]
    for b in range(BATCH):
        slot, live = slot_of(plan_ref, group, b, pushed)
        row = plan_ref[ROW, slot]
        if pushed:
            start, begin, end = plan_ref[AT_BACK, slot], row // UNIT, width // UNIT
        else:
            start, begin, end = plan_ref[AT_PULL, slot], 0, (row + UNIT - 1) // UNIT

        @pl.when(live)
        def _(b=b, start=start, begin=begin, end=end):
            def unit(u, carry):
                rows = pl.ds(pl.multiple_of(u * UNIT, UNIT), UNIT)
                for l in range(slices):
                    for p in range(planes):
                        back_ref[start + u - begin, l * planes + p] = out_ref[out_at[b], l, p, rows, :]
                return carry

            lax.fori_loop(begin, end, unit, 0)


def add_window(plan_ref, slot, out_ref, at, grad_ref, pushed):
    slices, planes, width, columns = grad_ref.shape
    row_iota, lane_iota = iotas(width)
    row, shift, here, there = place(plan_ref, slot, width, columns)
    mine = row_iota < row if pushed else row_iota >= row
    first = lane_iota >= shift
    for l in range(slices):
        for p in range(planes):
            ours = jnp.where(mine, out_ref[at, l, p], 0.0)
            grad_ref[l, p, :, here] += jnp.where(first, ours, 0.0)
            grad_ref[l, p, :, there] += jnp.where(first, 0.0, ours)


def pushed_kernel(plan_ref, probe_ref, own_ref, came_ref, tables_ref,
                  grad_ref, back_ref, sums_ref, wave_ref, window_ref, field_ref):
    grad_ref[...] = jnp.zeros_like(grad_ref)
    at = list(range(BATCH))

    def step(group, loss):
        loss = loss + begin_group(
            plan_ref, probe_ref, own_ref, came_ref, None, tables_ref, wave_ref, window_ref, field_ref, group, at, True
        )
        backward(tables_ref, wave_ref, window_ref, field_ref, at, window_ref, at)
        pack_back(plan_ref, window_ref, at, back_ref, group, True)
        for b in range(BATCH):
            slot, live = slot_of(plan_ref, group, b, True)

            @pl.when(live)
            def _(b=b, slot=slot):
                add_window(plan_ref, slot, window_ref, b, grad_ref, True)

        return loss

    groups = (plan_ref[TOTALS, 0] + BATCH - 1) // BATCH
    sums_ref[0] = lax.fori_loop(0, groups, step, jnp.float32(0.0))
    sums_ref[1] = jnp.float32(0.0)


def kept_forward_kernel(plan_ref, probe_ref, own_ref, came_ref, tables_ref, sums_in_ref, seen_ref,
                        wave_ref, window_ref, field_ref, sums_ref):
    def step(group, loss):
        at = [group * BATCH + b for b in range(BATCH)]
        return loss + begin_group(
            plan_ref, probe_ref, own_ref, came_ref, seen_ref, tables_ref, wave_ref, window_ref, field_ref, group, at, False
        )

    groups = (plan_ref[TOTALS, 1] + BATCH - 1) // BATCH
    sums_ref[0] = lax.fori_loop(0, groups, step, sums_in_ref[0])
    sums_ref[1] = plan_ref[TOTALS, 2].astype(jnp.float32)


def kept_backward_kernel(plan_ref, tables_ref, wave_ref, window_ref, field_ref, back_ref, out_ref):
    def step(group, carry):
        at = [group * BATCH + b for b in range(BATCH)]
        backward(tables_ref, wave_ref, window_ref, field_ref, at, out_ref, at)
        pack_back(plan_ref, out_ref, at, back_ref, group, False)
        return carry

    lax.fori_loop(0, (plan_ref[TOTALS, 1] + BATCH - 1) // BATCH, step, 0)


def after_kernel(x_ref, *refs):
    pass


def add(plan, slot, grad_ref, layers, came, start, begin, end, below):
    planes, width, columns = grad_ref.shape[1:]
    row, shift, here, there = place(plan, slot, width, columns)
    first = lax.broadcasted_iota(jnp.int32, (UNIT, width), 1) >= shift
    row_iota = lax.broadcasted_iota(jnp.int32, (UNIT, width), 0)

    def unit(u, carry):
        rows = pl.ds(pl.multiple_of(u * UNIT, UNIT), UNIT)
        at = u * UNIT + row_iota
        mine = at < row if below else at >= row
        for l in layers:
            for p in range(planes):
                piece = jnp.where(mine, came[start + u - begin, l * planes + p], 0.0)
                grad_ref[l, p, rows, here] += jnp.where(first, piece, 0.0)
                grad_ref[l, p, rows, there] += jnp.where(first, 0.0, piece)
        return carry

    lax.fori_loop(begin, end, unit, 0)


def add_returned_kernel(plan_ref, returned_ref, out_ref, grad_in_ref, grad_ref):
    slices, _, width, _ = grad_ref.shape
    grad_ref[...] = grad_in_ref[...]

    def kept(i, carry):
        add_window(plan_ref, plan_ref[KEPT, i], out_ref, i, grad_ref, False)
        return carry

    lax.fori_loop(0, plan_ref[TOTALS, 1], kept, 0)

    def step(i, carry):
        slot = plan_ref[PUSHED, i]
        at, low = plan_ref[AT_BACK, slot], plan_ref[ROW, slot] // UNIT
        add(plan_ref, slot, grad_ref, range(slices), returned_ref, at, low, width // UNIT, False)
        return carry

    lax.fori_loop(0, plan_ref[TOTALS, 0], step, 0)


def add_given(before_ref, given_ref, grad_ref, layers):
    def step(i, carry):
        slot = before_ref[KEPT, i]
        end = (before_ref[ROW, slot] + UNIT - 1) // UNIT
        add(before_ref, slot, grad_ref, layers, given_ref, before_ref[AT_PULL, slot], 0, end, True)
        return carry

    lax.fori_loop(0, before_ref[TOTALS, 1], step, 0)


def finish_kernel(before_ref, given_ref, grad_in_ref, grad_hbm, grad_ref, sems):
    slices = grad_ref.shape[0]
    stores = [pltpu.make_async_copy(grad_ref.at[l], grad_hbm.at[l], sems.at[l]) for l in range(slices)]
    for l in range(slices):
        grad_ref[l] = grad_in_ref[l]
        add_given(before_ref, given_ref, grad_ref, [l])
        stores[l].start()
    for store in stores:
        store.wait()


def merge_kernel(more_ref, base_hbm, sum_hbm, work_ref, sem):
    for l in range(work_ref.shape[0]):
        load = pltpu.make_async_copy(base_hbm.at[l], work_ref.at[l], sem)
        load.start()
        load.wait()
        work_ref[l] += more_ref[l]
        store = pltpu.make_async_copy(work_ref.at[l], sum_hbm.at[l], sem)
        store.start()
        store.wait()


def shifted(x, axis, by):
    peers = lax.axis_size(axis)
    return lax.ppermute(x, axis, [(i, (i + by) % peers) for i in range(peers)])


def total_stages(peers):
    stages, step = [], 1
    while step < peers:
        radix = 4 if step * 4 <= peers else 2
        stages.append((step, radix))
        step *= radix
    return stages


def partial_total(x, axis, stage):
    peers = lax.axis_size(axis)
    step, radix = stage

    def other(by):
        return lax.ppermute(x, axis, [(i, i ^ by) for i in range(peers)])

    if radix == 2:
        return x + other(step)
    return (x + other(step)) + (other(2 * step) + other(3 * step))


def local(probe_wave, object_slices, intensities, row_offset, col_offset, counts):
    width = probe_wave.shape[-1]
    slices, planes = object_slices.shape[:2]
    cap = row_offset.shape[0]
    peers = lax.axis_size("tile")
    units, seen_units = width // UNIT, width // (UNIT * UNIT)
    tables = jnp.asarray(make_tables(width))
    meta = jnp.concatenate([counts, row_offset, col_offset])
    seen = intensities.reshape(cap, seen_units, UNIT, UNIT, width)
    rooms = sizes(cap, width)
    smem = pl.BlockSpec(memory_space=pltpu.SMEM)
    vmem = pl.BlockSpec(memory_space=pltpu.VMEM)
    anywhere = pl.BlockSpec(memory_space=pl.ANY)
    f32 = jnp.float32

    def shape(dims, dtype=f32):
        return jax.ShapeDtypeStruct(dims, dtype)

    def packed(n):
        return shape((n, slices * planes, UNIT, width))

    def call(kernel, name, cost, ins, in_specs, outs, out_specs, scratch=(), mib=16, aliases=None):
        return pl.pallas_call(
            kernel,
            out_shape=outs,
            in_specs=in_specs,
            out_specs=out_specs,
            scratch_shapes=scratch,
            input_output_aliases=aliases or {},
            compiler_params=pltpu.CompilerParams(vmem_limit_bytes=mib << 20),
            cost_estimate=pl.CostEstimate(flops=int(cost * 1e9), bytes_accessed=int(cost * 1e6), transcendentals=0),
            name=name,
        )(*ins)

    def held(like):
        return pltpu.VMEM(like.shape, like.dtype)

    strip, sums_shape = shape(object_slices.shape), shape((2,))
    plan_shape = shape((8, cap), jnp.int32)
    dma = pltpu.SemaphoreType.DMA

    def held(like):
        return pltpu.VMEM(like.shape, like.dtype)

    def ahead(meta, source, again):
        kernel = functools.partial(push_kernel, rooms=rooms, again=again)
        outs = (plan_shape, held(packed(rooms[again][0] + 1)))
        if again:
            return call(kernel, "pack_more", 4, (meta, source, seen), [smem, vmem, anywhere], outs, (smem, vmem), [dma((cap,))])
        far = [pltpu.with_memory_space_constraint(x, pltpu.HBM) for x in (source, seen)]
        return call(
            kernel, "pack_pushed", 4, (meta, *far), [smem, anywhere, anywhere], outs + (held(strip),), (smem, vmem, vmem),
            [dma, dma((cap,))],
        )

    def behind(pushed, own, again):
        scratch = [pltpu.VMEM((UNIT, width), jnp.int32), pltpu.SMEM((UNIT, width), jnp.int32), dma]
        outs = (plan_shape, held(packed(rooms[again][2])))
        return call(pull_kernel, "pack_pulled", 2, (pushed, own), [vmem, vmem], outs, (smem, vmem), scratch)

    def waves(n):
        return shape((n, slices, planes, width, width)), shape((n, planes, width, width))

    def grads_pushed(before, own, pushed, back):
        wave, field = (pltpu.VMEM(x.shape, f32) for x in waves(BATCH))
        return call(
            pushed_kernel, "grads_pushed", 10, (before, probe_wave, own, pushed, tables), [smem] + [vmem] * 4,
            (held(strip), held(packed(back)), sums_shape), (vmem, vmem, smem), [wave, wave, field], 24,
        )

    def waves_kept(plan, own, pulled, sums):
        wave, field = (held(x) for x in waves(-(-cap // BATCH) * BATCH))
        return call(
            kept_forward_kernel, "waves_kept", 5, (plan, probe_wave, own, pulled, tables, sums, intensities),
            [smem] + [vmem] * 4 + [smem, vmem], (wave, wave, field, sums_shape), (vmem, vmem, vmem, smem), mib=20,
        )

    def grads_kept(plan, wave, window, field, back):
        return call(
            kept_backward_kernel, "grads_kept", 5, (plan, tables, wave, window, field), [smem] + [vmem] * 4,
            (held(packed(back)), held(wave)), (vmem, vmem), mib=20,
        )

    stages = total_stages(peers)

    def one_round(own, plan, push, again):
        pushed = shifted(push, "tile", 1)
        before, pull = behind(pushed, own, again)
        pulled = shifted(pull, "tile", -1)
        grad, back, sums = grads_pushed(before, own, pushed, rooms[again][1])
        returned = shifted(back, "tile", -1)
        wave, window, field, sums = waves_kept(plan, own, pulled, sums)
        sums = partial_total(sums, "tile", stages[0])
        back, out = grads_kept(plan, wave, window, field, rooms[again][2])
        back = call(
            after_kernel, "after_returned", 1, (back, returned, sums), [anywhere] * 3, held(back), anywhere, aliases={0: 0}
        )
        given = shifted(back, "tile", 1)
        for stage in stages[1:]:
            sums = partial_total(sums, "tile", stage)
        grad = call(
            add_returned_kernel, "add_returned", 3, (plan, returned, out, grad), [smem, vmem, vmem, vmem], held(strip), vmem,
            aliases={3: 0},
        )
        grad = call(
            finish_kernel, "add_given", 4, (before, given, grad), [smem, vmem, vmem], pltpu.HBM(strip.shape, f32), anywhere,
            [pltpu.VMEM(strip.shape, f32), dma((slices,))],
        )
        return grad, sums

    def unfinished(carry):
        return carry[1] > 0

    def second(carry):
        grad, _, loss, meta = carry
        more, sums = one_round(own, *ahead(meta, own, True), True)
        grad = call(
            merge_kernel, "merge", 4, (more, pltpu.with_memory_space_constraint(grad, pltpu.HBM)), [vmem, anywhere],
            pltpu.HBM(strip.shape, f32), anywhere, [pltpu.VMEM(strip.shape, f32), dma], aliases={1: 0},
        )
        return grad, jnp.float32(0.0), loss + sums[:1], jnp.zeros_like(meta)

    plan, push, own = ahead(meta, object_slices, False)
    grad, sums = one_round(own, plan, push, False)
    grad, _, loss, _ = lax.while_loop(unfinished, second, (grad, sums[1], sums[:1], meta))
    return grad, loss


def solution(mesh):
    placed = (
        P(),
        P("parts", None, "tile", None),
        P(("parts", "tile"), None, None),
        P(("parts", "tile")),
        P(("parts", "tile")),
        P(("parts", "tile")),
    )
    return jax.shard_map(
        local,
        mesh=mesh,
        in_specs=placed,
        out_specs=(P("parts", None, "tile", None), P("parts")),
        check_vma=False,
    )
```

```python
import functools

import jax
import jax.numpy as jnp
import ml_dtypes
import numpy as np
from jax import lax
from jax.experimental import pallas as pl
from jax.experimental.pallas import tpu as pltpu
from jax.sharding import PartitionSpec as P

BATCH = 4
UNIT = 8
ROW, COL, AT_PUSH, AT_BACK, AT_PULL, PUSHED, KEPT, TOTALS = range(8)


def make_tables(width):
    indices = np.arange(width)
    dft = np.exp(-2j * np.pi * (np.outer(indices, indices) % width) / width) / np.sqrt(width)
    freqs = np.where(indices < width // 2, indices, indices - width).astype(np.float64)
    along = np.conj(dft) @ (np.exp(-0.0015j * freqs**2)[:, None] * dft)
    out = []
    for matrix in (along, dft):
        left = np.block([[matrix.real, -matrix.imag], [matrix.imag, matrix.real]])
        forms = []
        for form in (left, left.T):
            form = form.astype(np.float32)
            high = form.astype(ml_dtypes.bfloat16)
            low = (form - high.astype(np.float32)).astype(ml_dtypes.bfloat16)
            forms.append(np.stack([high, low]))
        out.append(np.stack(forms))
    return np.stack(out)


def split(x):
    high = x.astype(jnp.bfloat16)
    return high, (x - high.astype(jnp.float32)).astype(jnp.bfloat16)


def dot(a, b):
    return jnp.dot(a, b, preferred_element_type=jnp.float32)


def one_sided(tables, which, form, re, im):
    width = re.shape[0]
    high, low = split(jnp.concatenate([re, im], axis=1))
    m_high, m_low = tables[which, form, 0], tables[which, form, 1]
    out = dot(high, m_high) + (dot(high, m_low) + dot(low, m_high))
    return out[:, :width], out[:, width:]


def two_sided(tables, which, conj, re, im):
    form = 0 if conj else 1
    half = [one_sided(tables, which, form, a, b) for a, b in zip(re, im)]
    full = [one_sided(tables, which, form, a.T, b.T) for a, b in half]
    return [a.T for a, _ in full], [b.T for _, b in full]


def forward(tables, wave_ref, window_ref, field_ref, at, measured, scales):
    slices = wave_ref.shape[1]
    for layer in range(slices):
        re, im = [], []
        for b in at:
            w_re, w_im = wave_ref[b, layer, 0], wave_ref[b, layer, 1]
            t_re, t_im = window_ref[b, layer, 0], window_ref[b, layer, 1]
            re.append(w_re * t_re - w_im * t_im)
            im.append(w_re * t_im + w_im * t_re)
        if layer + 1 < slices:
            re, im = two_sided(tables, 0, False, re, im)
            for i, b in enumerate(at):
                wave_ref[b, layer + 1, 0] = re[i]
                wave_ref[b, layer + 1, 1] = im[i]
    re, im = two_sided(tables, 1, False, re, im)
    loss = 0.0
    for i, b in enumerate(at):
        misfit = re[i] * re[i] + im[i] * im[i] - measured[i]
        loss = loss + scales[i] * (0.25 * jnp.sum(misfit * misfit))
        field_ref[b, 0] = misfit * re[i]
        field_ref[b, 1] = misfit * im[i]
    return loss


def backward(tables, wave_ref, window_ref, field_ref, at, out_ref, out_at):
    slices = wave_ref.shape[1]
    re, im = two_sided(tables, 1, True, [field_ref[b, 0] for b in at], [field_ref[b, 1] for b in at])
    for layer in reversed(range(slices)):
        upper_re, upper_im = [], []
        for i, b in enumerate(at):
            w_re, w_im = wave_ref[b, layer, 0], wave_ref[b, layer, 1]
            t_re, t_im = window_ref[b, layer, 0], window_ref[b, layer, 1]
            out_ref[out_at[i], layer, 0] = re[i] * w_re + im[i] * w_im
            out_ref[out_at[i], layer, 1] = im[i] * w_re - re[i] * w_im
            upper_re.append(re[i] * t_re + im[i] * t_im)
            upper_im.append(im[i] * t_re - re[i] * t_im)
        if layer > 0:
            re, im = two_sided(tables, 0, True, upper_re, upper_im)


def place(plan_ref, slot, width, columns):
    row, col = plan_ref[ROW, slot], plan_ref[COL, slot]
    tile = col // width
    here = pl.ds(pl.multiple_of(tile * width, width), width)
    after = jnp.minimum(tile + 1, columns // width - 1)
    there = pl.ds(pl.multiple_of(after * width, width), width)
    return row, col - tile * width, here, there


def sizes(cap, width):
    whole = cap * width // UNIT
    first = (whole * 9 // 32, whole * 27 // 128, whole * 33 // 128)
    return first, (whole * 5 // 16, whole // 4, whole * 5 // 16)


def make_plan(meta_ref, plan_ref, width, rooms, again):
    cap = plan_ref.shape[1]
    units = width // UNIT
    seen_units = width // (UNIT * UNIT)
    shape = (UNIT, 128)
    choice = lax.broadcasted_iota(jnp.int32, shape, 0) * 128 + lax.broadcasted_iota(jnp.int32, shape, 1)
    zero = jnp.zeros(shape, jnp.int32)
    push, back, pull, n_push, bad = zero, zero, zero, zero, (choice >= (1 << cap)).astype(jnp.int32)
    count = meta_ref[0]
    for s in range(cap):
        row = meta_ref[1 + s]
        crosses = jnp.logical_and(s < count, row > 0).astype(jnp.int32)
        taken = (choice >> s) & 1
        ahead = units - row // UNIT
        push += taken * (ahead + seen_units)
        back += taken * ahead
        pull += (1 - taken) * (crosses * ((row + UNIT - 1) // UNIT))
        n_push += taken
        bad += taken * (1 - crosses)
    n_keep = count - n_push
    groups = (n_push + BATCH - 1) // BATCH + (n_keep + BATCH - 1) // BATCH
    worst = 16 * cap

    def best_of(room):
        over = bad + (push > room[0]).astype(jnp.int32) + (back > room[1]).astype(jnp.int32) + (pull > room[2]).astype(jnp.int32)
        score = (groups * 16 + n_keep + worst * (over > 0).astype(jnp.int32)) * (1 << cap) + choice
        return jnp.min(score.astype(jnp.float32)).astype(jnp.int32)

    best = best_of(rooms[0])
    short = (best >= worst << cap).astype(jnp.int32)
    if again:
        best = best_of(rooms[1])
    at_push = at_back = at_pull = n_pushed = n_kept = jnp.int32(0)
    for s in range(cap):
        plan_ref[PUSHED, s] = 0
        plan_ref[KEPT, s] = 0
        plan_ref[TOTALS, s] = 0
    for s in range(cap):
        row = meta_ref[1 + s]
        crosses = (row > 0).astype(jnp.int32)
        now = short * crosses if again else 1 - short * crosses
        taken = ((best >> s) & 1) * (short if again else 1 - short)
        kept = jnp.where(s < count, (1 - taken) * now, 0)
        plan_ref[ROW, s] = row
        plan_ref[COL, s] = meta_ref[1 + cap + s]
        plan_ref[AT_PUSH, s] = at_push
        plan_ref[AT_BACK, s] = at_back
        plan_ref[AT_PULL, s] = at_pull

        @pl.when(taken > 0)
        def _():
            plan_ref[PUSHED, n_pushed] = s

        @pl.when(kept > 0)
        def _():
            plan_ref[KEPT, n_kept] = s

        ahead = units - row // UNIT
        at_push += taken * (ahead + seen_units)
        at_back += taken * ahead
        at_pull += kept * ((row + UNIT - 1) // UNIT)
        n_pushed += taken
        n_kept += kept
    plan_ref[TOTALS, 0] = n_pushed
    plan_ref[TOTALS, 1] = n_kept
    plan_ref[TOTALS, 2] = short


def pack(plan_ref, slot, own_ref, buffer_ref, start, first_unit, last_unit):
    slices, planes, width, columns = own_ref.shape
    _, shift, here, there = place(plan_ref, slot, width, columns)
    first = lax.broadcasted_iota(jnp.int32, (UNIT, width), 1) >= shift

    def step(u, carry):
        rows = pl.ds(pl.multiple_of(u * UNIT, UNIT), UNIT)
        for l in range(slices):
            for p in range(planes):
                buffer_ref[start + u - first_unit, l * planes + p] = jnp.where(
                    first, own_ref[l, p, rows, here], own_ref[l, p, rows, there]
                )
        return carry

    lax.fori_loop(first_unit, last_unit, step, 0)


def push_kernel(meta_ref, own_in_ref, seen_hbm, plan_ref, push_ref, *refs, rooms, again):
    if again:
        own_ref = own_in_ref
        sems, = refs
    else:
        own_ref, sem, sems = refs
        load = pltpu.make_async_copy(own_in_ref, own_ref, sem)
        load.start()
    width = own_ref.shape[2]
    units, seen_units = width // UNIT, seen_hbm.shape[1]
    make_plan(meta_ref, plan_ref, width, rooms, again)

    def seen(i):
        slot = plan_ref[PUSHED, i]
        start = plan_ref[AT_PUSH, slot] + units - plan_ref[ROW, slot] // UNIT
        return pltpu.make_async_copy(seen_hbm.at[slot], push_ref.at[pl.ds(start, seen_units)], sems.at[i])

    def begin(i, carry):
        seen(i).start()
        return carry

    def step(i, carry):
        slot = plan_ref[PUSHED, i]
        pack(plan_ref, slot, own_ref, push_ref, plan_ref[AT_PUSH, slot], plan_ref[ROW, slot] // UNIT, units)
        return carry

    def end(i, carry):
        seen(i).wait()
        return carry

    lax.fori_loop(0, plan_ref[TOTALS, 0], begin, 0)
    shape = (UNIT, width)
    index = lax.broadcasted_iota(jnp.int32, shape, 0) * width + lax.broadcasted_iota(jnp.int32, shape, 1)
    told = jnp.zeros(shape, jnp.float32)
    for r in range(plan_ref.shape[0]):
        for s in range(plan_ref.shape[1]):
            told = jnp.where(index == r * width + s, plan_ref[r, s].astype(jnp.float32), told)
    push_ref[push_ref.shape[0] - 1, 0] = told
    if not again:
        load.wait()
    lax.fori_loop(0, plan_ref[TOTALS, 0], step, 0)
    lax.fori_loop(0, plan_ref[TOTALS, 0], end, 0)


def pull_kernel(told_ref, own_ref, plan_ref, pull_ref, whole_ref, numbers_ref, sem):
    whole_ref[...] = told_ref[told_ref.shape[0] - 1, 0].astype(jnp.int32)
    copy = pltpu.make_async_copy(whole_ref, numbers_ref, sem)
    copy.start()
    copy.wait()
    for r in range(plan_ref.shape[0]):
        for s in range(plan_ref.shape[1]):
            plan_ref[r, s] = numbers_ref[r, s]

    def step(i, carry):
        slot = plan_ref[KEPT, i]
        end = (plan_ref[ROW, slot] + UNIT - 1) // UNIT
        pack(plan_ref, slot, own_ref, pull_ref, plan_ref[AT_PULL, slot], 0, end)
        return carry

    lax.fori_loop(0, plan_ref[TOTALS, 1], step, 0)


def slot_of(plan_ref, group, b, pushed):
    count = plan_ref[TOTALS, 0 if pushed else 1]
    live = group * BATCH + b < count
    return plan_ref[PUSHED if pushed else KEPT, jnp.where(live, group * BATCH + b, group * BATCH)], live


def iotas(width):
    shape = (width, width)
    return lax.broadcasted_iota(jnp.int32, shape, 0), lax.broadcasted_iota(jnp.int32, shape, 1)


def begin_group(plan_ref, probe_ref, own_ref, came_ref, seen_ref, tables_ref, wave_ref, window_ref, field_ref, group, at, pushed):
    slices, planes, width, columns = own_ref.shape
    units = width // UNIT
    seen_units = width // (UNIT * UNIT)
    last = came_ref.shape[0] - 1
    row_iota, lane_iota = iotas(width)
    scales, measured = [], []
    for b in range(BATCH):
        slot, live = slot_of(plan_ref, group, b, pushed)
        scales.append(live.astype(jnp.float32))
        row, shift, here, there = place(plan_ref, slot, width, columns)
        mine = row_iota < row if pushed else row_iota >= row
        first = lane_iota >= shift
        if pushed:
            start = plan_ref[AT_PUSH, slot] - row // UNIT
            seen = came_ref[pl.ds(jnp.minimum(start + units, last + 1 - seen_units), seen_units)]
            measured.append(seen.reshape(width, width))
        else:
            start = plan_ref[AT_PULL, slot]
            measured.append(seen_ref[slot])
        units_at = [jnp.clip(start + u, 0, last) for u in range(units)]
        for l in range(slices):
            for p in range(planes):
                theirs = jnp.concatenate([came_ref[i, l * planes + p] for i in units_at], axis=0)
                ours = jnp.where(first, own_ref[l, p, :, here], own_ref[l, p, :, there])
                window_ref[at[b], l, p] = jnp.where(mine, ours, theirs)
        for p in range(planes):
            wave_ref[at[b], 0, p] = pltpu.roll(pltpu.roll(probe_ref[p], row, 0), shift, 1)
    return forward(tables_ref, wave_ref, window_ref, field_ref, at, measured, scales)


def pack_back(plan_ref, out_ref, out_at, back_ref, group, pushed):
    slices, planes, width = out_ref.shape[1:4]
    for b in range(BATCH):
        slot, live = slot_of(plan_ref, group, b, pushed)
        row = plan_ref[ROW, slot]
        if pushed:
            start, begin, end = plan_ref[AT_BACK, slot], row // UNIT, width // UNIT
        else:
            start, begin, end = plan_ref[AT_PULL, slot], 0, (row + UNIT - 1) // UNIT

        @pl.when(live)
        def _(b=b, start=start, begin=begin, end=end):
            def unit(u, carry):
                rows = pl.ds(pl.multiple_of(u * UNIT, UNIT), UNIT)
                for l in range(slices):
                    for p in range(planes):
                        back_ref[start + u - begin, l * planes + p] = out_ref[out_at[b], l, p, rows, :]
                return carry

            lax.fori_loop(begin, end, unit, 0)


def add_window(plan_ref, slot, out_ref, at, grad_ref, pushed):
    slices, planes, width, columns = grad_ref.shape
    row_iota, lane_iota = iotas(width)
    row, shift, here, there = place(plan_ref, slot, width, columns)
    mine = row_iota < row if pushed else row_iota >= row
    first = lane_iota >= shift
    for l in range(slices):
        for p in range(planes):
            ours = jnp.where(mine, out_ref[at, l, p], 0.0)
            grad_ref[l, p, :, here] += jnp.where(first, ours, 0.0)
            grad_ref[l, p, :, there] += jnp.where(first, 0.0, ours)


def pushed_kernel(plan_ref, probe_ref, own_ref, came_ref, tables_ref,
                  grad_ref, back_ref, sums_ref, wave_ref, window_ref, field_ref):
    grad_ref[...] = jnp.zeros_like(grad_ref)
    at = list(range(BATCH))

    def step(group, loss):
        loss = loss + begin_group(
            plan_ref, probe_ref, own_ref, came_ref, None, tables_ref, wave_ref, window_ref, field_ref, group, at, True
        )
        backward(tables_ref, wave_ref, window_ref, field_ref, at, window_ref, at)
        pack_back(plan_ref, window_ref, at, back_ref, group, True)
        for b in range(BATCH):
            slot, live = slot_of(plan_ref, group, b, True)

            @pl.when(live)
            def _(b=b, slot=slot):
                add_window(plan_ref, slot, window_ref, b, grad_ref, True)

        return loss

    groups = (plan_ref[TOTALS, 0] + BATCH - 1) // BATCH
    sums_ref[0] = lax.fori_loop(0, groups, step, jnp.float32(0.0))
    sums_ref[1] = jnp.float32(0.0)


def kept_forward_kernel(plan_ref, probe_ref, own_ref, came_ref, tables_ref, sums_in_ref, seen_ref,
                        wave_ref, window_ref, field_ref, sums_ref):
    def step(group, loss):
        at = [group * BATCH + b for b in range(BATCH)]
        return loss + begin_group(
            plan_ref, probe_ref, own_ref, came_ref, seen_ref, tables_ref, wave_ref, window_ref, field_ref, group, at, False
        )

    groups = (plan_ref[TOTALS, 1] + BATCH - 1) // BATCH
    sums_ref[0] = lax.fori_loop(0, groups, step, sums_in_ref[0])
    sums_ref[1] = plan_ref[TOTALS, 2].astype(jnp.float32)


def kept_backward_kernel(plan_ref, tables_ref, wave_ref, window_ref, field_ref, back_ref, out_ref):
    def step(group, carry):
        at = [group * BATCH + b for b in range(BATCH)]
        backward(tables_ref, wave_ref, window_ref, field_ref, at, out_ref, at)
        pack_back(plan_ref, out_ref, at, back_ref, group, False)
        return carry

    lax.fori_loop(0, (plan_ref[TOTALS, 1] + BATCH - 1) // BATCH, step, 0)


def after_kernel(x_ref, *refs):
    pass


def add(plan, slot, grad_ref, layers, came, start, begin, end, below):
    planes, width, columns = grad_ref.shape[1:]
    row, shift, here, there = place(plan, slot, width, columns)
    first = lax.broadcasted_iota(jnp.int32, (UNIT, width), 1) >= shift
    row_iota = lax.broadcasted_iota(jnp.int32, (UNIT, width), 0)

    def unit(u, carry):
        rows = pl.ds(pl.multiple_of(u * UNIT, UNIT), UNIT)
        at = u * UNIT + row_iota
        mine = at < row if below else at >= row
        for l in layers:
            for p in range(planes):
                piece = jnp.where(mine, came[start + u - begin, l * planes + p], 0.0)
                grad_ref[l, p, rows, here] += jnp.where(first, piece, 0.0)
                grad_ref[l, p, rows, there] += jnp.where(first, 0.0, piece)
        return carry

    lax.fori_loop(begin, end, unit, 0)


def add_returned_kernel(plan_ref, returned_ref, out_ref, grad_in_ref, grad_ref):
    slices, _, width, _ = grad_ref.shape
    grad_ref[...] = grad_in_ref[...]

    def kept(i, carry):
        add_window(plan_ref, plan_ref[KEPT, i], out_ref, i, grad_ref, False)
        return carry

    lax.fori_loop(0, plan_ref[TOTALS, 1], kept, 0)

    def step(i, carry):
        slot = plan_ref[PUSHED, i]
        at, low = plan_ref[AT_BACK, slot], plan_ref[ROW, slot] // UNIT
        add(plan_ref, slot, grad_ref, range(slices), returned_ref, at, low, width // UNIT, False)
        return carry

    lax.fori_loop(0, plan_ref[TOTALS, 0], step, 0)


def add_given(before_ref, given_ref, grad_ref, layers):
    def step(i, carry):
        slot = before_ref[KEPT, i]
        end = (before_ref[ROW, slot] + UNIT - 1) // UNIT
        add(before_ref, slot, grad_ref, layers, given_ref, before_ref[AT_PULL, slot], 0, end, True)
        return carry

    lax.fori_loop(0, before_ref[TOTALS, 1], step, 0)


def finish_kernel(before_ref, sums_in_ref, given_ref, grad_in_ref, grad_hbm, sums_ref, grad_ref, sems):
    slices = grad_ref.shape[0]
    for i in range(sums_ref.shape[0]):
        sums_ref[i] = sums_in_ref[i]
    stores = [pltpu.make_async_copy(grad_ref.at[l], grad_hbm.at[l], sems.at[l]) for l in range(slices)]
    for l in range(slices):
        grad_ref[l] = grad_in_ref[l]
        add_given(before_ref, given_ref, grad_ref, [l])
        stores[l].start()
    for store in stores:
        store.wait()


def merge_kernel(more_ref, base_hbm, sum_hbm, work_ref, sem):
    for l in range(work_ref.shape[0]):
        load = pltpu.make_async_copy(base_hbm.at[l], work_ref.at[l], sem)
        load.start()
        load.wait()
        work_ref[l] += more_ref[l]
        store = pltpu.make_async_copy(work_ref.at[l], sum_hbm.at[l], sem)
        store.start()
        store.wait()


def shifted(x, axis, by):
    peers = lax.axis_size(axis)
    return lax.ppermute(x, axis, [(i, (i + by) % peers) for i in range(peers)])


def total_stages(peers):
    stages, step = [], 1
    while step < peers:
        radix = 4 if step * 4 <= peers else 2
        stages.append((step, radix))
        step *= radix
    return stages


def partial_total(x, axis, stage, own=None):
    own = x if own is None else own
    peers = lax.axis_size(axis)
    step, radix = stage

    def other(by):
        return lax.ppermute(x, axis, [(i, i ^ by) for i in range(peers)])

    if radix == 2:
        return own + other(step)
    return (own + other(step)) + (other(2 * step) + other(3 * step))


def local(probe_wave, object_slices, intensities, row_offset, col_offset, counts):
    width = probe_wave.shape[-1]
    slices, planes = object_slices.shape[:2]
    cap = row_offset.shape[0]
    peers = lax.axis_size("tile")
    units, seen_units = width // UNIT, width // (UNIT * UNIT)
    tables = jnp.asarray(make_tables(width))
    meta = jnp.concatenate([counts, row_offset, col_offset])
    seen = intensities.reshape(cap, seen_units, UNIT, UNIT, width)
    rooms = sizes(cap, width)
    smem = pl.BlockSpec(memory_space=pltpu.SMEM)
    vmem = pl.BlockSpec(memory_space=pltpu.VMEM)
    anywhere = pl.BlockSpec(memory_space=pl.ANY)
    f32 = jnp.float32

    def shape(dims, dtype=f32):
        return jax.ShapeDtypeStruct(dims, dtype)

    def packed(n):
        return shape((n, slices * planes, UNIT, width))

    def call(kernel, name, cost, ins, in_specs, outs, out_specs, scratch=(), mib=16, aliases=None):
        return pl.pallas_call(
            kernel,
            out_shape=outs,
            in_specs=in_specs,
            out_specs=out_specs,
            scratch_shapes=scratch,
            input_output_aliases=aliases or {},
            compiler_params=pltpu.CompilerParams(vmem_limit_bytes=mib << 20),
            cost_estimate=pl.CostEstimate(flops=int(cost * 1e9), bytes_accessed=int(cost * 1e6), transcendentals=0),
            name=name,
        )(*ins)

    def held(like):
        return pltpu.VMEM(like.shape, like.dtype)

    strip, sums_shape = shape(object_slices.shape), shape((2,))
    plan_shape = shape((8, cap), jnp.int32)
    dma = pltpu.SemaphoreType.DMA

    def held(like):
        return pltpu.VMEM(like.shape, like.dtype)

    def ahead(meta, source, again):
        kernel = functools.partial(push_kernel, rooms=rooms, again=again)
        outs = (plan_shape, held(packed(rooms[again][0] + 1)))
        if again:
            return call(kernel, "pack_more", 4, (meta, source, seen), [smem, vmem, anywhere], outs, (smem, vmem), [dma((cap,))])
        far = [pltpu.with_memory_space_constraint(x, pltpu.HBM) for x in (source, seen)]
        return call(
            kernel, "pack_pushed", 4, (meta, *far), [smem, anywhere, anywhere], outs + (held(strip),), (smem, vmem, vmem),
            [dma, dma((cap,))],
        )

    def behind(pushed, own, again):
        scratch = [pltpu.VMEM((UNIT, width), jnp.int32), pltpu.SMEM((UNIT, width), jnp.int32), dma]
        outs = (plan_shape, held(packed(rooms[again][2])))
        return call(pull_kernel, "pack_pulled", 2, (pushed, own), [vmem, vmem], outs, (smem, vmem), scratch)

    def waves(n):
        return shape((n, slices, planes, width, width)), shape((n, planes, width, width))

    def grads_pushed(before, own, pushed, back):
        wave, field = (pltpu.VMEM(x.shape, f32) for x in waves(BATCH))
        return call(
            pushed_kernel, "grads_pushed", 10, (before, probe_wave, own, pushed, tables), [smem] + [vmem] * 4,
            (held(strip), held(packed(back)), sums_shape), (vmem, vmem, smem), [wave, wave, field], 24,
        )

    def waves_kept(plan, own, pulled, sums):
        wave, field = (held(x) for x in waves(-(-cap // BATCH) * BATCH))
        return call(
            kept_forward_kernel, "waves_kept", 5, (plan, probe_wave, own, pulled, tables, sums, intensities),
            [smem] + [vmem] * 4 + [smem, vmem], (wave, wave, field, sums_shape), (vmem, vmem, vmem, smem), mib=20,
        )

    def grads_kept(plan, wave, window, field, back):
        return call(
            kept_backward_kernel, "grads_kept", 5, (plan, tables, wave, window, field), [smem] + [vmem] * 4,
            (held(packed(back)), held(wave)), (vmem, vmem), mib=20,
        )

    stages = total_stages(peers)

    def one_round(own, plan, push, again):
        pushed = shifted(push, "tile", 1)
        before, pull = behind(pushed, own, again)
        pulled = shifted(pull, "tile", -1)
        grad, back, sums = grads_pushed(before, own, pushed, rooms[again][1])
        returned = shifted(back, "tile", -1)
        wave, window, field, sums = waves_kept(plan, own, pulled, sums)
        sums = partial_total(sums, "tile", stages[0])
        back, out = grads_kept(plan, wave, window, field, rooms[again][2])
        back = call(
            after_kernel, "after_returned", 1, (back, returned, sums), [anywhere] * 3, held(back), anywhere, aliases={0: 0}
        )
        given = shifted(back, "tile", 1)
        for stage in stages[1:-1]:
            sums = partial_total(sums, "tile", stage)
        grad = call(
            add_returned_kernel, "add_returned", 3, (plan, returned, out, grad), [smem, vmem, vmem, vmem], held(strip), vmem,
            aliases={3: 0},
        )
        grad, same = call(
            finish_kernel, "add_given", 4, (before, sums, given, grad), [smem, smem, vmem, vmem],
            (pltpu.HBM(strip.shape, f32), sums_shape), (anywhere, smem), [pltpu.VMEM(strip.shape, f32), dma((slices,))],
        )
        if len(stages) > 1:
            sums = partial_total(sums, "tile", stages[-1], same)
        return grad, sums

    def unfinished(carry):
        return carry[1] > 0

    def second(carry):
        grad, _, loss, meta = carry
        more, sums = one_round(own, *ahead(meta, own, True), True)
        grad = call(
            merge_kernel, "merge", 4, (more, pltpu.with_memory_space_constraint(grad, pltpu.HBM)), [vmem, anywhere],
            pltpu.HBM(strip.shape, f32), anywhere, [pltpu.VMEM(strip.shape, f32), dma], aliases={1: 0},
        )
        return grad, jnp.float32(0.0), loss + sums[:1], jnp.zeros_like(meta)

    plan, push, own = ahead(meta, object_slices, False)
    grad, sums = one_round(own, plan, push, False)
    grad, _, loss, _ = lax.while_loop(unfinished, second, (grad, sums[1], sums[:1], meta))
    return grad, loss


def solution(mesh):
    placed = (
        P(),
        P("parts", None, "tile", None),
        P(("parts", "tile"), None, None),
        P(("parts", "tile")),
        P(("parts", "tile")),
        P(("parts", "tile")),
    )
    return jax.shard_map(
        local,
        mesh=mesh,
        in_specs=placed,
        out_specs=(P("parts", None, "tile", None), P("parts")),
        check_vma=False,
    )
```
